32 devices in a mesh: seq: 4 (over x, core), head: 2 (over y), dp: 4 (over z).
Axes of the slice: x: 2, y: 2, z: 4, core: 2. Of those that a mesh axis runs over, the one named last changes fastest.
Arguments:
- tokens: bfloat16 [8, 1024, 1024], P('dp', 'seq'), may hold values from -6 to 6
- segment_ids: int32 [8, 1024], P('dp', 'seq'), may hold values from 0 to 6, as said below
- ln1_gain: float32 [1024], replicated, may hold values from 0.5 to 1.5
- ln1_bias: float32 [1024], replicated, may hold values from -2 to 2
- qkv_weight: bfloat16 [1024, 3, 1024], P(None, None, 'head'), may hold values from -0.1875 to 0.1875
- qv_bias: float32 [2, 1024], P(None, 'head'), may hold values from -3 to 3
- out_weight: bfloat16 [1024, 1024], P('head'), may hold values from -0.75 to 0.75
- out_bias: float32 [1024], replicated, may hold values from -3 to 3
- ln2_gain: float32 [1024], replicated, may hold values from 0.5 to 1.5
- ln2_bias: float32 [1024], replicated, may hold values from -2 to 2
- up_weight: bfloat16 [1024, 4096], P(None, 'head'), may hold values from -0.1875 to 0.1875
- up_bias: float32 [4096], P('head'), may hold values from -3 to 3
- down_weight: bfloat16 [4096, 1024], P('head'), may hold values from -0.09375 to 0.09375
- down_bias: float32 [1024], replicated, may hold values from -3 to 3
- out_cotangent: bfloat16 [8, 1024, 1024], P('dp', 'seq'), may hold values from -6 to 6
Outputs:
- output: bfloat16 [8, 1024, 1024], P('dp', 'seq')
- tokens_grad: bfloat16 [8, 1024, 1024], P('dp', 'seq')
- ln1_gain_grad: float32 [1024], P(('seq', 'dp'))
- ln1_bias_grad: float32 [1024], P(('seq', 'dp'))
- qkv_weight_grad: float32 [1024, 3, 1024], P(('seq', 'dp'), None, 'head')
- qv_bias_grad: float32 [2, 1024], P(None, ('head', 'seq', 'dp'))
- out_weight_grad: float32 [1024, 1024], P('head', ('seq', 'dp'))
- out_bias_grad: float32 [1024], P(('seq', 'dp'))
- ln2_gain_grad: float32 [1024], P(('seq', 'dp'))
- ln2_bias_grad: float32 [1024], P(('seq', 'dp'))
- up_weight_grad: float32 [1024, 4096], P(('seq', 'dp'), 'head')
- up_bias_grad: float32 [4096], P(('head', 'seq', 'dp'))
- down_weight_grad: float32 [4096, 1024], P('head', ('seq', 'dp'))
- down_bias_grad: float32 [1024], P(('seq', 'dp'))
The draws below stay inside these ranges and needn't reach their ends.
Inputs may be any that keep to these rules, and one draw needn't show every extreme that they name: `segment_ids`: scene numbers never fall along a sequence.
All inputs are finite; a program needn't handle non-finite values.
Results may differ from the reference program's by a relative error of at most 0.015.
Values may be sent and summed in bfloat16 or wider, within the bound.
A program may use at most 320 MiB of HBM per device.

```python
import jax
import jax.numpy as jnp
from jax import lax

D = 1024
HEADS = 16
HEAD_DIM = 64
FF = 4096
SEQS = 2
BLK = 256
SCENES = 7
LEN = 1024
NSEQ = 8


def draw_segment_ids(key, part):
    key = jax.random.fold_in(key, 11)
    pick_key, long_key, cut_key = jax.random.split(key, 3)
    positions = jnp.arange(LEN, dtype=jnp.int32)
    members = jnp.arange(NSEQ, dtype=jnp.int32)
    chosen = jax.random.randint(pick_key, (NSEQ // SEQS,), 0, SEQS)
    is_long = members % SEQS == chosen[members // SEQS]
    edges = jax.random.randint(long_key, (NSEQ, 2), 1, BLK)
    long_ids = (positions[None, :] >= edges[:, 0:1]).astype(jnp.int32) + (positions[None, :] >= LEN - edges[:, 1:2]).astype(jnp.int32)
    cuts = jax.random.randint(cut_key, (NSEQ, SCENES - 1), 1, LEN)
    short_ids = jnp.sum((positions[None, :, None] >= cuts[:, None, :]).astype(jnp.int32), axis=-1)
    return jnp.where(is_long[:, None], long_ids, short_ids).astype(jnp.int32)


def with_spikes(entries, key, source, target, blocks, factor):
    def block_of(axis_at):
        return (jnp.arange(entries.shape[axis_at]) // (entries.shape[axis_at] // blocks)).reshape((-1,) + (1,) * (entries.ndim - 1 - axis_at))

    first = jax.random.permutation(key, blocks)[block_of(target)]
    other_side = (block_of(target) + blocks // 2) % blocks
    return jnp.where((block_of(source) == first) | (block_of(source) == other_side), factor * entries, entries)


def level_of(key, shape, cuts, least, top_value):
    level, own = 1.0, jax.random.fold_in(key, 6)
    for axis_at, shards_of in cuts:
        steps = jnp.exp(jax.random.uniform(jax.random.fold_in(own, axis_at), (shards_of,), jnp.float32, least / len(cuts), top_value / len(cuts)))
        level = level * jnp.repeat(steps, shape[axis_at] // shards_of).reshape([-1 if axis == axis_at else 1 for axis in range(len(shape))])
    return level


def scatter_about(key, dims, scale, bound, cuts=(), held_as=jnp.bfloat16):
    values = jax.random.normal(key, dims, jnp.float32) * scale
    if len(cuts) > 0:
        values = level_of(key, dims, cuts, -0.22, 0.18) * values
    return jnp.clip(values, min=-bound, max=bound).astype(held_as)


def bell_draw_with(stream_key, extent, deviation, bound, cuts, heavy, kind=jnp.bfloat16):
    entries = deviation * jax.random.normal(stream_key, extent, jnp.float32)
    if cuts:
        entries = entries * level_of(stream_key, extent, cuts, -0.22, 0.18)
    return jnp.clip(with_spikes(entries, jax.random.fold_in(stream_key, 3), *heavy), -bound, bound).astype(kind)


def setup_inputs(seed: int = 0) -> dict:
    splits = jax.random.split(jax.random.key(seed), 16)
    return {
        "tokens": scatter_about(splits[0], (NSEQ, LEN, D), 1.0, 6.0, ((0, 4), (1, 4))),
        "segment_ids": draw_segment_ids(jax.random.fold_in(splits[15], 71), 0),
        "ln1_gain": jnp.clip(1.0 + 0.1 * jax.random.normal(splits[2], (D,), jnp.float32), 0.5, 1.5),
        "ln1_bias": scatter_about(splits[3], (D,), 0.3, 2.0, (), jnp.float32),
        "qkv_weight": scatter_about(splits[4], (D, 3, D), D ** -0.5, 0.1875, ((2, 2),)),
        "qv_bias": scatter_about(splits[5], (2, D), 0.5, 3.0, ((1, 2),), jnp.float32),
        "out_weight": scatter_about(splits[6], (D, D), (D // 16) ** -0.5, 0.75, ((0, 2),)),
        "out_bias": scatter_about(splits[7], (D,), 0.5, 3.0, (), jnp.float32),
        "ln2_gain": jnp.clip(1.0 + 0.1 * jax.random.normal(splits[8], (D,), jnp.float32), 0.5, 1.5),
        "ln2_bias": scatter_about(splits[9], (D,), 0.3, 2.0, (), jnp.float32),
        "up_weight": scatter_about(splits[10], (D, FF), D ** -0.5, 0.1875, ((1, 2),)),
        "up_bias": scatter_about(splits[11], (FF,), 0.5, 3.0, ((0, 2),), jnp.float32),
        "down_weight": scatter_about(splits[12], (FF, D), FF ** -0.5, 0.09375, ((0, 2),)),
        "down_bias": scatter_about(splits[13], (D,), 0.5, 3.0, (), jnp.float32),
        "out_cotangent": bell_draw_with(splits[14], (NSEQ, LEN, D), 1.0, 6.0, ((0, 4), (1, 4)), (1, 2, 4, 2.0)),
    }


EPSILON = 1e-05
HIGHEST = lax.Precision.HIGHEST

@jax.custom_vjp
def low(v):
    return lax.optimization_barrier(v.astype(jnp.bfloat16)).astype(jnp.float32)

@jax.custom_vjp
def low_back(v):
    return v

def low_keep(v):
    return (low(v), None)

def low_pass(kept, grad):
    return (grad,)

def back_keep(v):
    return (v, None)

def back_low(kept, grad):
    return (low(grad),)
low.defvjp(low_keep, low_pass)
low_back.defvjp(back_keep, back_low)

def layer_norm(inputs, gain, shift):
    center = lax.optimization_barrier(jnp.mean(inputs, axis=-1, keepdims=True))
    centred = inputs - center
    spread = lax.optimization_barrier(jnp.mean(centred * centred, axis=-1, keepdims=True))
    return centred * lax.rsqrt(spread + EPSILON) * gain + shift

def head_attention(queries, key_rows, values, allowed):
    scores = low_back(jnp.dot(queries, key_rows.T, precision=HIGHEST) * 0.125)
    masked = jnp.where(allowed, scores, -1e+30)
    running = lax.optimization_barrier(jnp.max(masked, axis=-1, keepdims=True))
    weights = jnp.where(allowed, jnp.exp(masked - running), 0.0)
    denominator = lax.optimization_barrier(jnp.sum(weights, axis=-1, keepdims=True))
    return jnp.dot(low(weights), values, precision=HIGHEST) / denominator

def attention(queries, key_rows, values, segments):
    allowed = segments[:, None] == segments[None, :]

    def one_head(operands):
        return head_attention(operands[0], operands[1], operands[2], allowed)
    stacked = (jnp.moveaxis(queries, 1, 0), jnp.moveaxis(key_rows, 1, 0), jnp.moveaxis(values, 1, 0))
    mixed = lax.map(jax.checkpoint(one_head), stacked)
    return jnp.moveaxis(mixed, 0, 1)

def residual_block(sequence_rows, segments, ln1_gain, ln1_bias, qkv_weight, qv_bias, out_weight, out_bias, ln2_gain, ln2_bias, up_weight, up_bias, down_weight, down_bias):
    length = sequence_rows.shape[0]
    first = low(layer_norm(sequence_rows, ln1_gain, ln1_bias))
    projected = jnp.einsum('ld,dcf->lcf', first, qkv_weight, precision=HIGHEST)
    queries = low_back(low(projected[:, 0] + qv_bias[0]))
    key_rows = low_back(low(projected[:, 1]))
    values = low_back(low(projected[:, 2] + qv_bias[1]))
    shape = (length, HEADS, HEAD_DIM)
    mixed = attention(queries.reshape(shape), key_rows.reshape(shape), values.reshape(shape), segments)
    mixed = low_back(low(mixed.reshape(length, D)))
    branch = low_back(jnp.dot(mixed, out_weight, precision=HIGHEST) + out_bias)
    middle = sequence_rows + branch
    second = low(layer_norm(middle, ln2_gain, ln2_bias))
    hidden = low_back(jnp.dot(second, up_weight, precision=HIGHEST) + up_bias)
    activated = low(jax.nn.gelu(hidden, approximate=True))
    return middle + low_back(jnp.dot(activated, down_weight, precision=HIGHEST) + down_bias)

def reference(tokens, segment_ids, ln1_gain, ln1_bias, qkv_weight, qv_bias, out_weight, out_bias, ln2_gain, ln2_bias, up_weight, up_bias, down_weight, down_bias, out_cotangent):
    params = tuple((parameter.astype(jnp.float32) for parameter in (ln1_gain, ln1_bias, qkv_weight, qv_bias, out_weight, out_bias, ln2_gain, ln2_bias, up_weight, up_bias, down_weight, down_bias)))

    def accumulate(sums, item):
        sequence_rows, segments, cotangent = item

        def run_block(inputs, *weights):
            return residual_block(inputs, segments, *weights)
        result, pullback = jax.vjp(run_block, sequence_rows.astype(jnp.float32), *params)
        grads = pullback(cotangent.astype(jnp.float32))
        sums = tuple((total + grad for total, grad in zip(sums, grads[1:])))
        return (sums, (result.astype(jnp.bfloat16), grads[0].astype(jnp.bfloat16)))
    start = tuple((jnp.zeros_like(parameter) for parameter in params))
    sums, (output, tokens_grad) = lax.scan(accumulate, start, (tokens, segment_ids, out_cotangent))
    return (output, tokens_grad, sums[0], sums[1], sums[2], sums[3], sums[4], sums[5], sums[6], sums[7], sums[8], sums[9], sums[10], sums[11])
```

```python
import functools

import jax
import jax.numpy as jnp
from jax import lax
from jax.experimental import pallas as pl
from jax.experimental.pallas import tpu as pltpu
from jax.sharding import PartitionSpec as P

HEAD_DIM = 64
LANES = 128
EPSILON = 1e-05
MASKED = -1e30
F32 = jnp.float32
LOW = jnp.bfloat16
NN = (((1,), (0,)), ((), ()))
NT = (((1,), (1,)), ((), ()))
TN = (((0,), (0,)), ((), ()))
VMEM_LIMIT = 60 * 2**20


def dot(a, b, dims=NN):
    return lax.dot_general(a, b, dims, preferred_element_type=F32)


def axis_size(name):
    return lax.axis_size(name)


def swap(value, axis, mask):
    return lax.ppermute(value, axis, [(i, i ^ mask) for i in range(axis_size(axis))])


def bits_of(count):
    return [1 << b for b in range(count.bit_length() - 1)]


def layer_norm(inputs, gain, shift):
    center = jnp.mean(inputs, axis=-1, keepdims=True)
    centred = inputs - center
    spread = jnp.mean(centred * centred, axis=-1, keepdims=True)
    inverse = lax.rsqrt(spread + EPSILON)
    normed = centred * inverse
    return (normed * gain + shift, normed, inverse)


def norm_backward(upstream, normed, inverse, gain):
    scaled = upstream * gain
    centred = scaled - jnp.mean(scaled, axis=-1, keepdims=True)
    return inverse * (centred - normed * jnp.mean(scaled * normed, axis=-1, keepdims=True))


def gelu_pair(v):
    c = 0.7978845608028654
    square = v * v
    t = jnp.tanh(c * v * (1.0 + 0.044715 * square))
    half = 0.5 * (1.0 + t)
    return v * half, half + (0.5 * c) * v * (1.0 - t * t) * (1.0 + 3.0 * 0.044715 * square)


def half_lanes(shape, head):
    lane = lax.broadcasted_iota(jnp.int32, shape, 1)
    return (lane < HEAD_DIM) if head == 0 else (lane >= HEAD_DIM)


def attend_kernel(n, q_ref, seg_ref, segk_ref, *refs):
    kv_refs = refs[:n]
    w_ref, attn_ref, low_ref, inv_ref = refs[n:]
    q = q_ref[...] * jnp.asarray(0.125, LOW)
    seg_q = seg_ref[0:1, :]
    for head in range(2):
        qh = jnp.where(half_lanes(q.shape, head), q, jnp.zeros_like(q))
        parts, top = [], None
        for m in range(n):
            s = dot(kv_refs[m][0], qh, NT)
            s = jnp.where(segk_ref[m] == seg_q, s, MASKED)
            peak = jnp.max(s, axis=0, keepdims=True)
            top = peak if top is None else jnp.maximum(top, peak)
            parts.append(s)
        total, mixed = 0.0, 0.0
        for m in range(n):
            w = jnp.exp(parts[m] - top)
            total = total + jnp.sum(w, axis=0, keepdims=True)
            wl = w.astype(LOW)
            w_ref[head, m] = wl
            vt = kv_refs[m][1].T[head * HEAD_DIM:(head + 1) * HEAD_DIM, :]
            mixed = mixed + dot(vt, wl)
        inverse = 1.0 / total
        inv_ref[0, head:head + 1, :] = inverse
        attn_ref[head * HEAD_DIM:(head + 1) * HEAD_DIM, :] = mixed * inverse
    low_ref[...] = attn_ref[...].T.astype(LOW)


def attend(q, seg_rows, seg_cols, kvs):
    n, (rows, width) = len(kvs), q.shape
    pairs = width // LANES
    step = lambda p: (0, p)
    kv_spec = pl.BlockSpec((2, rows, LANES), lambda p: (0, 0, p))
    return pl.pallas_call(
        functools.partial(attend_kernel, n),
        grid=(pairs,),
        in_specs=[
            pl.BlockSpec((rows, LANES), step),
            pl.BlockSpec((8, rows), lambda p: (0, 0)),
            pl.BlockSpec((n, rows, 1), lambda p: (0, 0, 0)),
        ]
        + [kv_spec] * n,
        out_specs=[
            pl.BlockSpec((2, n, rows, rows), lambda p: (p, 0, 0, 0)),
            pl.BlockSpec((LANES, rows), lambda p: (p, 0)),
            pl.BlockSpec((rows, LANES), step),
            pl.BlockSpec((1, 2, rows), lambda p: (p, 0, 0)),
        ],
        out_shape=[
            jax.ShapeDtypeStruct((2 * pairs, n, rows, rows), LOW),
            jax.ShapeDtypeStruct((width, rows), F32),
            jax.ShapeDtypeStruct((rows, width), LOW),
            jax.ShapeDtypeStruct((pairs, 2, rows), F32),
        ],
        compiler_params=pltpu.CompilerParams(vmem_limit_bytes=VMEM_LIMIT),
        cost_estimate=pl.CostEstimate(
            flops=2 * pairs * n * rows * rows * 256 * 4,
            bytes_accessed=2 * pairs * n * rows * rows * 2,
            transcendentals=2 * pairs * n * rows * rows,
        ),
    )(q, seg_rows, seg_cols, *kvs)


def attend_back_kernel(n, q_ref, g_ref, attn_ref, inv_ref, w_ref, *refs):
    kv_refs = refs[:n]
    dq_ref = refs[n]
    dkv_refs = refs[n + 1:2 * n + 1]
    dqt_ref = refs[2 * n + 1]
    q = q_ref[...]
    gt = g_ref[...].astype(F32).T
    qs, gs, gts, deltas = [], [], [], []
    for head in range(2):
        rows_h = slice(head * HEAD_DIM, (head + 1) * HEAD_DIM)
        part = (gt[rows_h] * inv_ref[0, head:head + 1, :]).astype(LOW)
        deltas.append(jnp.sum(part.astype(F32) * attn_ref[rows_h, :], axis=0, keepdims=True))
        zeros = jnp.zeros_like(part)
        full = jnp.concatenate([part, zeros] if head == 0 else [zeros, part], axis=0)
        gts.append(full)
        gs.append(full.T)
        qs.append(jnp.where(half_lanes(q.shape, head), q, jnp.zeros_like(q)))
    dqt = [0.0, 0.0]
    for m in range(n):
        kt = kv_refs[m][0].T
        v = kv_refs[m][1]
        dk = dv = 0.0
        for head in range(2):
            w = w_ref[head, m]
            ds = (w.astype(F32) * (dot(v, gts[head]) - deltas[head])).astype(LOW)
            dk = dk + dot(ds, qs[head])
            dv = dv + dot(w, gs[head])
            dqt[head] = dqt[head] + dot(kt[head * HEAD_DIM:(head + 1) * HEAD_DIM, :], ds)
        dkv_refs[m][0] = (dk * 0.125).astype(LOW)
        dkv_refs[m][1] = dv.astype(LOW)
    dqt_ref[0:HEAD_DIM, :] = dqt[0]
    dqt_ref[HEAD_DIM:LANES, :] = dqt[1]
    dq_ref[...] = (dqt_ref[...].T * 0.125).astype(LOW)


def attend_back(q, g, attn, inverse, weights, kvs):
    n, (rows, width) = len(kvs), q.shape
    pairs = width // LANES
    step = lambda p: (0, p)
    kv_spec = pl.BlockSpec((2, rows, LANES), lambda p: (0, 0, p))
    out = pl.pallas_call(
        functools.partial(attend_back_kernel, n),
        grid=(pairs,),
        in_specs=[
            pl.BlockSpec((rows, LANES), step),
            pl.BlockSpec((rows, LANES), step),
            pl.BlockSpec((LANES, rows), lambda p: (p, 0)),
            pl.BlockSpec((1, 2, rows), lambda p: (p, 0, 0)),
            pl.BlockSpec((2, n, rows, rows), lambda p: (p, 0, 0, 0)),
        ]
        + [kv_spec] * n,
        out_specs=[pl.BlockSpec((rows, LANES), step)] + [kv_spec] * n,
        out_shape=[jax.ShapeDtypeStruct((rows, width), LOW)]
        + [jax.ShapeDtypeStruct((2, rows, width), LOW)] * n,
        scratch_shapes=[pltpu.VMEM((LANES, rows), F32)],
        compiler_params=pltpu.CompilerParams(vmem_limit_bytes=VMEM_LIMIT),
        cost_estimate=pl.CostEstimate(
            flops=2 * pairs * n * rows * rows * 256 * 8,
            bytes_accessed=2 * pairs * n * rows * rows * 2,
            transcendentals=0,
        ),
    )(q, g, attn, inverse, weights, *kvs)
    return out[0], out[1:]


def gather_seq(block):
    bits = bits_of(axis_size("seq"))
    blocks = {0: block}
    for bit in reversed(bits):
        for m in list(blocks):
            blocks[m | bit] = swap(blocks[m], "seq", bit)
    return [blocks[m] for m in range(len(blocks))]


def scatter_seq(parts):
    parts = dict(enumerate(parts))
    for bit in bits_of(axis_size("seq")):
        for m in [m for m in sorted(parts, reverse=True) if m & bit]:
            got = swap(parts.pop(m).astype(LOW), "seq", bit)
            parts[m ^ bit] = parts[m ^ bit].astype(F32) + got.astype(F32)
    return parts[0].astype(F32)


def scatter_line(term):
    n = axis_size("dp")
    me = lax.axis_index("dp")
    rows = term.shape[0] // n
    block = lambda i: lax.dynamic_slice_in_dim(term, jnp.clip(i, 0, n - 1) * rows, rows, 0)
    up = down = None
    for k in range(n - 1, 0, -1):
        send_up = block(me + k) if up is None else block(me + k) + up
        send_down = block(me - k) if down is None else block(me - k) + down
        up = lax.ppermute(
            send_up.astype(LOW), "dp", [(i, i + 1) for i in range(n) if i + k < n]
        ).astype(F32)
        down = lax.ppermute(
            send_down.astype(LOW), "dp", [(i, i - 1) for i in range(n) if i - k >= 0]
        ).astype(F32)
    out = block(me)
    return out if n == 1 else out + up + down


def relative_columns(rows):
    n = axis_size("seq")
    me = lax.axis_index("seq")
    width = rows.shape[1] // n
    return [lax.dynamic_slice_in_dim(rows, (me ^ m) * width, width, 1) for m in range(n)]


def weight_grad(left, right):
    return scatter_line(scatter_seq([dot(part, right, TN) for part in left]))


def scatter_small(blocks):
    for axis in ("seq", "dp"):
        n = axis_size(axis)
        me = lax.axis_index(axis)
        bits = bits_of(n)
        rest = blocks.shape[1:]
        for bit in reversed(bits):
            low, high = blocks[:bit], blocks[bit:]
            mine = (me & bit) != 0
            send = jnp.where(mine, low, high)
            blocks = jnp.where(mine, high, low) + swap(send, axis, bit)
        blocks = blocks.reshape(rest)
    return blocks


def other_head(value):
    return swap(value, "head", 1)


def head_sum(value):
    value = value.astype(LOW)
    return value.astype(F32) + other_head(value).astype(F32)


def by_head(mine, other, axis):
    first = lax.axis_index("head") == 0
    return jnp.where(
        first,
        jnp.concatenate([mine, other], axis),
        jnp.concatenate([other, mine], axis),
    )


def shards(
    tokens,
    segment_ids,
    ln1_gain,
    ln1_bias,
    qkv_weight,
    qv_bias,
    out_weight,
    out_bias,
    ln2_gain,
    ln2_bias,
    up_weight,
    up_bias,
    down_weight,
    down_bias,
    out_cotangent,
):
    count, rows, features = tokens.shape
    local = qkv_weight.shape[2]
    hidden_local = up_weight.shape[1]
    n_seq, n_dp = axis_size("seq"), axis_size("dp")
    every = range(count)
    wq, wk, wv = (qkv_weight[:, c, :] for c in range(3))

    seg = gather_seq(segment_ids)
    seg_rows = [jnp.broadcast_to(segment_ids[s][None, :], (8, rows)) for s in every]
    seg_cols = [jnp.stack([part[s] for part in seg])[:, :, None] for s in every]

    half = out_weight.shape[0] // 2
    core = lax.axis_index("seq") & 1
    fetched = other_head(lax.dynamic_slice_in_dim(out_weight, core * half, half, 0))
    swapped = swap(fetched, "seq", 1)
    out_other = jnp.where(
        core == 0,
        jnp.concatenate([fetched, swapped], 0),
        jnp.concatenate([swapped, fetched], 0),
    )
    out_full = by_head(out_weight, out_other, 0)

    inputs, first, normed1, inverse1, queries, kvs = [], [], [], [], [], []
    for s in every:
        x = tokens[s].astype(F32)
        pre, normed, inverse = layer_norm(x, ln1_gain, ln1_bias)
        low = pre.astype(LOW)
        k = dot(low, wk).astype(LOW)
        v = (dot(low, wv) + qv_bias[1]).astype(LOW)
        kvs.append(gather_seq(jnp.stack([k, v])))
        queries.append((dot(low, wq) + qv_bias[0]).astype(LOW))
        inputs.append(x)
        first.append(low)
        normed1.append(normed)
        inverse1.append(inverse)

    attended = [attend(queries[s], seg_rows[s], seg_cols[s], kvs[s]) for s in every]

    outputs, second, act, g_hidden, g_middle, heads = [], [], [], [], [], []
    g_queries, g_kv = [], []
    vec = {
        name: 0.0 for name in ("out_b", "ln2_g", "ln2_b", "down_b", "up_b", "q_b", "v_b", "ln1_g", "ln1_b")
    }
    add = lambda name, value: vec.__setitem__(name, vec[name] + jnp.sum(value, axis=0))
    state = []
    for s in every:
        weights, attn_full, attn_low, inv_total = attended[s]
        mixed = by_head(attn_low, other_head(attn_low), 1)
        middle = inputs[s] + dot(mixed, out_full) + out_bias
        pre, normed2, inverse2 = layer_norm(middle, ln2_gain, ln2_bias)
        low = pre.astype(LOW)
        hidden = dot(low, up_weight) + up_bias
        activated, slope = gelu_pair(hidden)
        act_low = activated.astype(LOW)
        cot = out_cotangent[s]
        gh = (dot(cot, down_weight, NT) * slope).astype(LOW)
        g_second = head_sum(dot(gh, up_weight, NT))
        mlp = head_sum(dot(act_low, down_weight))
        outputs.append((middle + mlp + down_bias).astype(LOW))
        second.append(low)
        act.append(act_low)
        g_hidden.append(gh)
        heads.append(attn_low)
        state.append((normed2, inverse2, g_second))
        add("down_b", cot.astype(F32))
        add("up_b", gh.astype(F32))

    g_branch, g_first_parts = [], []
    for s in every:
        normed2, inverse2, g_second = state[s]
        weights, attn_full, attn_low, inv_total = attended[s]
        add("ln2_g", g_second * normed2)
        add("ln2_b", g_second)
        gm = out_cotangent[s].astype(F32) + norm_backward(g_second, normed2, inverse2, ln2_gain)
        gb = gm.astype(LOW)
        add("out_b", gb.astype(F32))
        g_attn = dot(gb, out_weight, NT).astype(LOW)
        dq, dkv = attend_back(queries[s], g_attn, attn_full, inv_total, weights, kvs[s])
        g_queries.append(dq)
        g_kv.append(scatter_seq(dkv).astype(LOW))
        g_middle.append(gm)
        g_branch.append(gb)

    join = lambda items: jnp.concatenate(items, axis=0)
    cot_all = out_cotangent.reshape(count * rows, features)
    cot_rel = relative_columns(cot_all)
    down_grad = weight_grad(cot_rel, join(act))
    up_grad = weight_grad(relative_columns(join(second)), join(g_hidden))
    out_grad = weight_grad(relative_columns(join(g_branch)), join(heads))

    tokens_grads = []
    for s in every:
        gq, gk, gv = g_queries[s], g_kv[s][0], g_kv[s][1]
        part = (dot(gq, wq, NT) + dot(gk, wk, NT) + dot(gv, wv, NT)).astype(LOW)
        add("q_b", gq.astype(F32))
        add("v_b", gv.astype(F32))
        add("ln1_g", part.astype(F32) * normed1[s])
        add("ln1_b", part.astype(F32))
        g_first = part.astype(F32) + other_head(part).astype(F32)
        tokens_grads.append(
            (g_middle[s] + norm_backward(g_first, normed1[s], inverse1[s], ln1_gain)).astype(LOW)
        )
    first_rel = relative_columns(join(first))
    g_proj = [join(g_queries), join([g[0] for g in g_kv]), join([g[1] for g in g_kv])]
    qkv_grad = jnp.stack([weight_grad(first_rel, g) for g in g_proj], axis=1)

    ln1 = jnp.stack([vec["ln1_g"], vec["ln1_b"]])
    ln1 = ln1 + other_head(ln1)
    wide = [ln1[0], ln1[1], vec["out_b"], vec["ln2_g"], vec["ln2_b"], vec["down_b"]]
    blocks = [v.reshape(n_seq, n_dp, -1) for v in wide + [vec["q_b"], vec["v_b"], vec["up_b"]]]
    sizes = [b.shape[2] for b in blocks]
    small = scatter_small(jnp.concatenate(blocks, axis=2))
    pieces, at = [], 0
    for size in sizes:
        pieces.append(small[at:at + size])
        at += size

    return (
        jnp.stack(outputs),
        jnp.stack(tokens_grads),
        pieces[0],
        pieces[1],
        qkv_grad,
        jnp.stack([pieces[6], pieces[7]]),
        out_grad.T,
        pieces[2],
        pieces[3],
        pieces[4],
        up_grad,
        pieces[8],
        down_grad.T,
        pieces[5],
    )


def solution(mesh):
    in_specs = (
        P("dp", "seq", None),
        P("dp", "seq"),
        P(),
        P(),
        P(None, None, "head"),
        P(None, "head"),
        P("head", None),
        P(),
        P(),
        P(),
        P(None, "head"),
        P("head"),
        P("head", None),
        P(),
        P("dp", "seq", None),
    )
    out_specs = (
        P("dp", "seq", None),
        P("dp", "seq", None),
        P(("seq", "dp")),
        P(("seq", "dp")),
        P(("seq", "dp"), None, "head"),
        P(None, ("head", "seq", "dp")),
        P("head", ("seq", "dp")),
        P(("seq", "dp")),
        P(("seq", "dp")),
        P(("seq", "dp")),
        P(("seq", "dp"), "head"),
        P(("head", "seq", "dp")),
        P("head", ("seq", "dp")),
        P(("seq", "dp")),
    )
    return jax.shard_map(shards, mesh=mesh, in_specs=in_specs, out_specs=out_specs, check_vma=False)
```

```python
import functools

import jax
import jax.numpy as jnp
from jax import lax
from jax.experimental import pallas as pl
from jax.experimental.pallas import tpu as pltpu
from jax.sharding import PartitionSpec as P

HEAD_DIM = 64
LANES = 128
EPSILON = 1e-05
MASKED = -1e30
F32 = jnp.float32
LOW = jnp.bfloat16
NN = (((1,), (0,)), ((), ()))
NT = (((1,), (1,)), ((), ()))
TN = (((0,), (0,)), ((), ()))
VMEM_LIMIT = 60 * 2**20


def dot(a, b, dims=NN):
    return lax.dot_general(a, b, dims, preferred_element_type=F32)


def axis_size(name):
    return lax.axis_size(name)


def swap(value, axis, mask):
    return lax.ppermute(value, axis, [(i, i ^ mask) for i in range(axis_size(axis))])


def bits_of(count):
    return [1 << b for b in range(count.bit_length() - 1)]


def layer_norm(inputs, gain, shift):
    center = jnp.mean(inputs, axis=-1, keepdims=True)
    centred = inputs - center
    spread = jnp.mean(centred * centred, axis=-1, keepdims=True)
    inverse = lax.rsqrt(spread + EPSILON)
    normed = centred * inverse
    return (normed * gain + shift, normed, inverse)


def norm_backward(upstream, normed, inverse, gain):
    scaled = upstream * gain
    centred = scaled - jnp.mean(scaled, axis=-1, keepdims=True)
    return inverse * (centred - normed * jnp.mean(scaled * normed, axis=-1, keepdims=True))


def gelu_pair(v):
    c = 0.7978845608028654
    square = v * v
    t = jnp.tanh(c * v * (1.0 + 0.044715 * square))
    half = 0.5 * (1.0 + t)
    return v * half, half + (0.5 * c) * v * (1.0 - t * t) * (1.0 + 3.0 * 0.044715 * square)


def half_lanes(shape, head):
    lane = lax.broadcasted_iota(jnp.int32, shape, 1)
    return (lane < HEAD_DIM) if head == 0 else (lane >= HEAD_DIM)


def attend_kernel(n, q_ref, seg_ref, segk_ref, *refs):
    kv_refs = refs[:n]
    w_ref, attn_ref, low_ref, inv_ref = refs[n:]
    q = q_ref[...] * jnp.asarray(0.125, LOW)
    seg_q = seg_ref[0:1, :]
    for head in range(2):
        qh = jnp.where(half_lanes(q.shape, head), q, jnp.zeros_like(q))
        parts, top = [], None
        for m in range(n):
            s = dot(kv_refs[m][0], qh, NT)
            s = jnp.where(segk_ref[m] == seg_q, s, MASKED)
            peak = jnp.max(s, axis=0, keepdims=True)
            top = peak if top is None else jnp.maximum(top, peak)
            parts.append(s)
        total, mixed = 0.0, 0.0
        for m in range(n):
            w = jnp.exp(parts[m] - top)
            total = total + jnp.sum(w, axis=0, keepdims=True)
            wl = w.astype(LOW)
            w_ref[head, m] = wl
            vt = kv_refs[m][1].T[head * HEAD_DIM:(head + 1) * HEAD_DIM, :]
            mixed = mixed + dot(vt, wl)
        inverse = 1.0 / total
        inv_ref[0, head:head + 1, :] = inverse
        attn_ref[head * HEAD_DIM:(head + 1) * HEAD_DIM, :] = mixed * inverse
    low_ref[...] = attn_ref[...].T.astype(LOW)


def attend(q, seg_rows, seg_cols, kvs):
    n, (rows, width) = len(kvs), q.shape
    pairs = width // LANES
    step = lambda p: (0, p)
    kv_spec = pl.BlockSpec((2, rows, LANES), lambda p: (0, 0, p))
    return pl.pallas_call(
        functools.partial(attend_kernel, n),
        grid=(pairs,),
        in_specs=[
            pl.BlockSpec((rows, LANES), step),
            pl.BlockSpec((8, rows), lambda p: (0, 0)),
            pl.BlockSpec((n, rows, 1), lambda p: (0, 0, 0)),
        ]
        + [kv_spec] * n,
        out_specs=[
            pl.BlockSpec((2, n, rows, rows), lambda p: (p, 0, 0, 0)),
            pl.BlockSpec((LANES, rows), lambda p: (p, 0)),
            pl.BlockSpec((rows, LANES), step),
            pl.BlockSpec((1, 2, rows), lambda p: (p, 0, 0)),
        ],
        out_shape=[
            jax.ShapeDtypeStruct((2 * pairs, n, rows, rows), LOW),
            jax.ShapeDtypeStruct((width, rows), F32),
            jax.ShapeDtypeStruct((rows, width), LOW),
            jax.ShapeDtypeStruct((pairs, 2, rows), F32),
        ],
        compiler_params=pltpu.CompilerParams(vmem_limit_bytes=VMEM_LIMIT),
        cost_estimate=pl.CostEstimate(
            flops=2 * pairs * n * rows * rows * 256 * 4,
            bytes_accessed=2 * pairs * n * rows * rows * 2,
            transcendentals=2 * pairs * n * rows * rows,
        ),
    )(q, seg_rows, seg_cols, *kvs)


def attend_back_kernel(n, q_ref, g_ref, attn_ref, inv_ref, w_ref, *refs):
    kv_refs = refs[:n]
    dq_ref = refs[n]
    dkv_refs = refs[n + 1:2 * n + 1]
    dqt_ref = refs[2 * n + 1]
    q = q_ref[...]
    gt = g_ref[...].astype(F32).T
    qs, gs, gts, deltas = [], [], [], []
    for head in range(2):
        rows_h = slice(head * HEAD_DIM, (head + 1) * HEAD_DIM)
        part = (gt[rows_h] * inv_ref[0, head:head + 1, :]).astype(LOW)
        deltas.append(jnp.sum(part.astype(F32) * attn_ref[rows_h, :], axis=0, keepdims=True))
        zeros = jnp.zeros_like(part)
        full = jnp.concatenate([part, zeros] if head == 0 else [zeros, part], axis=0)
        gts.append(full)
        gs.append(full.T)
        qs.append(jnp.where(half_lanes(q.shape, head), q, jnp.zeros_like(q)))
    dqt = [0.0, 0.0]
    for m in range(n):
        kt = kv_refs[m][0].T
        v = kv_refs[m][1]
        dk = dv = 0.0
        for head in range(2):
            w = w_ref[head, m]
            ds = (w.astype(F32) * (dot(v, gts[head]) - deltas[head])).astype(LOW)
            dk = dk + dot(ds, qs[head])
            dv = dv + dot(w, gs[head])
            dqt[head] = dqt[head] + dot(kt[head * HEAD_DIM:(head + 1) * HEAD_DIM, :], ds)
        dkv_refs[m][0] = (dk * 0.125).astype(LOW)
        dkv_refs[m][1] = dv.astype(LOW)
    dqt_ref[0:HEAD_DIM, :] = dqt[0]
    dqt_ref[HEAD_DIM:LANES, :] = dqt[1]
    dq_ref[...] = (dqt_ref[...].T * 0.125).astype(LOW)


def attend_back(q, g, attn, inverse, weights, kvs):
    n, (rows, width) = len(kvs), q.shape
    pairs = width // LANES
    step = lambda p: (0, p)
    kv_spec = pl.BlockSpec((2, rows, LANES), lambda p: (0, 0, p))
    out = pl.pallas_call(
        functools.partial(attend_back_kernel, n),
        grid=(pairs,),
        in_specs=[
            pl.BlockSpec((rows, LANES), step),
            pl.BlockSpec((rows, LANES), step),
            pl.BlockSpec((LANES, rows), lambda p: (p, 0)),
            pl.BlockSpec((1, 2, rows), lambda p: (p, 0, 0)),
            pl.BlockSpec((2, n, rows, rows), lambda p: (p, 0, 0, 0)),
        ]
        + [kv_spec] * n,
        out_specs=[pl.BlockSpec((rows, LANES), step)] + [kv_spec] * n,
        out_shape=[jax.ShapeDtypeStruct((rows, width), LOW)]
        + [jax.ShapeDtypeStruct((2, rows, width), LOW)] * n,
        scratch_shapes=[pltpu.VMEM((LANES, rows), F32)],
        compiler_params=pltpu.CompilerParams(vmem_limit_bytes=VMEM_LIMIT),
        cost_estimate=pl.CostEstimate(
            flops=2 * pairs * n * rows * rows * 256 * 8,
            bytes_accessed=2 * pairs * n * rows * rows * 2,
            transcendentals=0,
        ),
    )(q, g, attn, inverse, weights, *kvs)
    return out[0], out[1:]


def gather_seq(block):
    bits = bits_of(axis_size("seq"))
    blocks = {0: block}
    for bit in reversed(bits):
        for m in list(blocks):
            blocks[m | bit] = swap(blocks[m], "seq", bit)
    return [blocks[m] for m in range(len(blocks))]


def scatter_seq(parts):
    parts = dict(enumerate(parts))
    for bit in bits_of(axis_size("seq")):
        for m in [m for m in sorted(parts, reverse=True) if m & bit]:
            got = swap(parts.pop(m).astype(LOW), "seq", bit)
            parts[m ^ bit] = parts[m ^ bit].astype(F32) + got.astype(F32)
    return parts[0].astype(F32)


def scatter_line(term):
    n = axis_size("dp")
    me = lax.axis_index("dp")
    rows = term.shape[0] // n
    block = lambda i: lax.dynamic_slice_in_dim(term, jnp.clip(i, 0, n - 1) * rows, rows, 0)
    up = down = None
    for k in range(n - 1, 0, -1):
        send_up = block(me + k) if up is None else block(me + k) + up
        send_down = block(me - k) if down is None else block(me - k) + down
        up = lax.ppermute(
            send_up.astype(LOW), "dp", [(i, i + 1) for i in range(n) if i + k < n]
        ).astype(F32)
        down = lax.ppermute(
            send_down.astype(LOW), "dp", [(i, i - 1) for i in range(n) if i - k >= 0]
        ).astype(F32)
    out = block(me)
    return out if n == 1 else out + up + down


def relative_columns(rows):
    n = axis_size("seq")
    me = lax.axis_index("seq")
    width = rows.shape[1] // n
    return [lax.dynamic_slice_in_dim(rows, (me ^ m) * width, width, 1) for m in range(n)]


def weight_grad(left, right):
    return scatter_line(scatter_seq([dot(part, right, TN) for part in left]))


def scatter_small(blocks):
    for axis in ("seq", "dp"):
        n = axis_size(axis)
        me = lax.axis_index(axis)
        bits = bits_of(n)
        rest = blocks.shape[1:]
        for bit in reversed(bits):
            low, high = blocks[:bit], blocks[bit:]
            mine = (me & bit) != 0
            send = jnp.where(mine, low, high)
            blocks = jnp.where(mine, high, low) + swap(send, axis, bit)
        blocks = blocks.reshape(rest)
    return blocks


def other_head(value):
    return swap(value, "head", 1)


def head_sum(value):
    value = value.astype(LOW)
    return value.astype(F32) + other_head(value).astype(F32)


def by_head(mine, other, axis):
    first = lax.axis_index("head") == 0
    return jnp.where(
        first,
        jnp.concatenate([mine, other], axis),
        jnp.concatenate([other, mine], axis),
    )


MESH = pl.DeviceIdType.MESH
CHUNK = 32
WIDE = 512


def loop(count, body):
    def step(i, carry):
        body(i)
        return carry

    lax.fori_loop(0, count, step, 0)


def span(i, size):
    return pl.ds(pl.multiple_of(i * size, size), size)


def fold(value):
    return jnp.sum(value.reshape(value.shape[0] // 8, 8, value.shape[1]), axis=0)


class Copies:
    def __init__(self, send, recv):
        self.send, self.recv, self.all, self.n = send, recv, [], 0

    def start(self, src, dst, device):
        copy = pltpu.make_async_remote_copy(
            src_ref=src,
            dst_ref=dst,
            send_sem=self.send.at[self.n],
            recv_sem=self.recv.at[self.n],
            device_id=device,
            device_id_type=MESH,
        )
        copy.start()
        self.n += 1
        self.all.append(copy)
        return copy


N_COPIES = 96
N_LOCAL = 24


def layer_kernel(n_dp, *refs):
    (
        tok_h, seg_in, g1, b1, wqkv_h, qvb, outw_h, outb, g2, b2, up_h, upb, down_h, downb, cot_h,
        out_h, tg_h, downg_h, upg_h, outg_h, qkvg_h, vec_o,
        tok, cot, wqkv, outw, up, down, q, kv, attn_t, attn, mid, lnb, act, gh,
        first_t, second_t, cot_t, gb_t, g_attn, t2, gs, ffn, stat, st,
        gs_r, ffn_r, gf_r, dkv_r, act_r, gh_r, first_r, second_r, cot_r, gb_r, heads_r, dqkv_r, xr, zr,
        segs, segk, vec, qvacc, upacc, ln1_r, vs, vr,
        send, recv, local,
    ) = refs
    rows = tok.shape[0] // 2
    width = tok.shape[1]
    heads_w = q.shape[1]
    hidden = act.shape[1]
    pairs = heads_w // LANES
    quarter = width // 4
    block = quarter // n_dp
    s = lax.axis_index("seq")
    h = lax.axis_index("head")
    z = lax.axis_index("dp")
    x, core = s // 2, s % 2
    seq_peer = [None] + [((x ^ (m >> 1)) * 2 + (core ^ (m & 1)), h, z) for m in (1, 2, 3)]
    across = (s, 1 - h, z)
    along = [None] + [(s, h, lax.rem(z + n_dp - d, n_dp)) for d in range(1, n_dp)]
    copies = Copies(send, recv)
    loads = []

    def load(src, dst):
        copy = pltpu.make_async_copy(src, dst, local.at[len(loads)])
        copy.start()
        loads.append(copy)
        return copy

    get_tok = load(tok_h, tok)
    get_qkv = load(wqkv_h, wqkv)
    own_out = pl.ds(pl.multiple_of(h * heads_w, heads_w), heads_w)
    get_out = load(outw_h, outw.at[own_out, :])
    get_cot = load(cot_h, cot)
    get_up = load(up_h, up)
    get_down = load(down_h, down)

    barrier = pltpu.get_barrier_semaphore()
    partners = seq_peer[1:] + [across] + along[1:]
    for device in partners:
        pl.semaphore_signal(barrier, inc=1, device_id=device, device_id_type=MESH)

    vec[...] = jnp.zeros_like(vec)
    qvacc[...] = jnp.zeros_like(qvacc)
    upacc[...] = jnp.zeros_like(upacc)
    segs[0] = seg_in[...]
    pl.semaphore_wait(barrier, len(partners))

    seg_got = [None] + [copies.start(segs.at[0], segs.at[m], seq_peer[m]) for m in (1, 2, 3)]

    def seq_rows(i):
        return slice(i * rows, (i + 1) * rows)

    def flip(src, i, dst):
        def part(c):
            dst[span(c, 256), seq_rows(i)] = src[:, span(c, 256)].T

        loop(width // 256, part)

    def swap_rows(flipped, target):
        return [
            copies.start(
                flipped.at[pl.ds(pl.multiple_of(c * 2 * quarter + (1 - core) * quarter, quarter), quarter), :],
                target.at[c],
                seq_peer[1],
            )
            for c in range(2)
        ]

    kv_got = [[None] * 4, [None] * 4]

    def project(i):
        def norm(c):
            at = pl.ds(pl.multiple_of(i * rows + c * CHUNK, CHUNK), CHUNK)
            v = tok[at, :].astype(F32)
            center = jnp.mean(v, axis=-1, keepdims=True)
            v = v - center
            inverse = lax.rsqrt(jnp.mean(v * v, axis=-1, keepdims=True) + EPSILON)
            stat[0, at, 0:1] = center
            stat[0, at, 1:2] = inverse
            lnb[i, span(c, CHUNK), :] = (v * inverse * g1[...] + b1[...]).astype(LOW)

        loop(rows // CHUNK, norm)
        low = lnb.at[i]

        def tile_kv(j):
            at = span(j, 256)
            kv[i, 0, :, at] = dot(low[...], wqkv[1, :, at]).astype(LOW)
            up_at = pl.ds(pl.multiple_of(heads_w + j * 256, 256), 256)
            kv[i, 0, :, up_at] = (dot(low[...], wqkv[2, :, at]) + qvb[1:2, at]).astype(LOW)

        if i == 0:
            get_qkv.wait()
        loop(heads_w // 256, tile_kv)
        kv_got[i][2] = copies.start(kv.at[i, 0], kv.at[i, 2], seq_peer[2])
        kv_got[i][1] = copies.start(kv.at[i, 0], kv.at[i, 1], seq_peer[1])

        def tile_q(j):
            at = span(j, 256)
            q[seq_rows(i), at] = (dot(low[...], wqkv[0, :, at]) + qvb[0:1, at]).astype(LOW)

        loop(heads_w // 256, tile_q)
        flip(low, i, first_t)

    def attend_blocks(i, blocks, begin, end):
        seg_q = segs[0, i:i + 1, :].astype(F32)

        def pair(p):
            lanes = span(p, LANES)
            v_lanes = pl.ds(pl.multiple_of(heads_w + p * LANES, LANES), LANES)
            qp = q[seq_rows(i), lanes] * jnp.asarray(0.125, LOW)
            vts = [kv[i, m, :, v_lanes].T for m in blocks]
            for head in range(2):
                at = pl.ds(pl.multiple_of(p * LANES + head * HEAD_DIM, HEAD_DIM), HEAD_DIM)
                qh = jnp.where(half_lanes(qp.shape, head), qp, jnp.zeros_like(qp))
                parts = []
                top = None if begin else st[i, p, head:head + 1, :]
                old = top
                for m in blocks:
                    score = dot(kv[i, m, :, lanes], qh, NT)
                    score = jnp.where(segk[m, :, i:i + 1] == seg_q, score, MASKED)
                    peak = jnp.max(score, axis=0, keepdims=True)
                    top = peak if top is None else jnp.maximum(top, peak)
                    parts.append(score)
                total = mixed = 0.0
                for part, vt in zip(parts, vts):
                    w = jnp.exp(part - top)
                    total = total + jnp.sum(w, axis=0, keepdims=True)
                    mixed = mixed + dot(vt[head * HEAD_DIM:(head + 1) * HEAD_DIM, :], w.astype(LOW))
                if not begin:
                    scale = jnp.exp(old - top)
                    total = total + scale * st[i, p, 2 + head:3 + head, :]
                    mixed = mixed + scale * attn_t[i, at, :]
                if end:
                    mixed = mixed / total
                    st[i, p, 4 + head:5 + head, :] = top + jnp.log(total)
                else:
                    st[i, p, head:head + 1, :] = top
                    st[i, p, 2 + head:3 + head, :] = total
                attn_t[i, at, :] = mixed
            if end:
                to = pl.ds(pl.multiple_of(h * heads_w + p * LANES, LANES), LANES)
                attn[seq_rows(i), to] = attn_t[i, lanes, :].T.astype(LOW)

        loop(pairs, pair)

    def seg_columns(m):
        segk[m] = segs[m].astype(F32).T

    own_heads = pl.ds(pl.multiple_of(h * heads_w, heads_w), heads_w)
    attn_got = [None, None]

    def attend_far(i):
        kv_got[i][2].wait_recv()
        kv_got[i][3] = copies.start(kv.at[i, 2], kv.at[i, 3], seq_peer[1])
        attend_blocks(i, (2,), False, False)
        kv_got[i][3].wait_recv()
        attend_blocks(i, (3,), False, True)
        mine = attn.at[seq_rows(i), own_heads]
        attn_got[i] = copies.start(mine, mine, across)
        heads_sent[i] = copies.start(mine, heads_r.at[seq_rows(i), :], seq_peer[1])

    heads_sent = [None, None]

    def middle(i):
        attn_got[i].wait_recv()

        def tile(j):
            at = span(j, 256)
            mid[seq_rows(i), at] = (
                dot(attn[seq_rows(i), :], outw[:, at])
                + tok[seq_rows(i), at].astype(F32)
                + outb[:, at]
            )

        loop(width // 256, tile)

        def norm(c):
            at = pl.ds(pl.multiple_of(i * rows + c * CHUNK, CHUNK), CHUNK)
            v = mid[at, :]
            center = jnp.mean(v, axis=-1, keepdims=True)
            v = v - center
            inverse = lax.rsqrt(jnp.mean(v * v, axis=-1, keepdims=True) + EPSILON)
            stat[1, at, 0:1] = center
            stat[1, at, 1:2] = inverse
            lnb[i, span(c, CHUNK), :] = (v * inverse * g2[...] + b2[...]).astype(LOW)

        loop(rows // CHUNK, norm)

    gs_got, ffn_got, act_got, gh_got = [None] * 2, [None] * 2, [None] * 2, [None] * 2

    def feed(i):
        at_rows = seq_rows(i)

        def tile(j):
            at = span(j, 256)
            value, slope = gelu_pair(dot(lnb[i], up[:, at]) + upb[:, at])
            act[at_rows, at] = value.astype(LOW)
            g = (dot(cot[at_rows, :], down[at, :], NT) * slope).astype(LOW)
            gh[at_rows, at] = g
            upacc[:, at] += fold(g.astype(F32))

        loop(hidden // 256, tile)

        def back(j):
            gs[at_rows, span(j, 256)] = dot(gh[at_rows, :], up[span(j, 256), :], NT).astype(LOW)

        loop(width // 256, back)
        gs_got[i] = copies.start(gs.at[at_rows, :], gs_r.at[at_rows, :], across)
        act_got[i] = copies.start(act.at[at_rows, :], act_r.at[at_rows, :], seq_peer[1])
        gh_got[i] = copies.start(gh.at[at_rows, :], gh_r.at[at_rows, :], seq_peer[1])
        flip(lnb.at[i], i, second_t)

    def feed_out(i):
        at_rows = seq_rows(i)

        def tile(j):
            ffn[at_rows, span(j, 256)] = dot(act[at_rows, :], down[:, span(j, 256)]).astype(LOW)

        loop(width // 256, tile)
        ffn_got[i] = copies.start(ffn.at[at_rows, :], ffn_r.at[at_rows, :], across)

    def finish_output(i):
        ffn_got[i].wait()

        def part(c):
            at = pl.ds(pl.multiple_of(i * rows + c * CHUNK, CHUNK), CHUNK)
            both = ffn[at, :].astype(F32) + ffn_r[at, :].astype(F32)
            ffn[at, :] = (mid[at, :] + both + downb[...]).astype(LOW)

        loop(rows // CHUNK, part)
        load(ffn.at[seq_rows(i), :], out_h.at[seq_rows(i), :])

    gb = down.at[2 * rows:4 * rows, :]
    parts_kv = [down.at[(4 + m) * rows:(5 + m) * rows, :] for m in range(4)]
    dqkv = up.at[2 * rows:4 * rows, :]

    def norm2_back(i):
        gs_got[i].wait_recv()

        def part(c):
            at = pl.ds(pl.multiple_of(i * rows + c * CHUNK, CHUNK), CHUNK)
            g = gs[at, :].astype(F32) + gs_r[at, :].astype(F32)
            inverse = stat[1, at, 1:2]
            normed = (mid[at, :] - stat[1, at, 0:1]) * inverse
            vec[3] += fold(g * normed)
            vec[4] += fold(g)
            e = g * g2[...]
            e = e - jnp.mean(e, axis=-1, keepdims=True) - normed * jnp.mean(e * normed, axis=-1, keepdims=True)
            low = (cot[at, :].astype(F32) + inverse * e).astype(LOW)
            gb[at, :] = low
            vec[2] += fold(low.astype(F32))

        loop(rows // CHUNK, part)

        def tile(j):
            w_rows = pl.ds(pl.multiple_of(h * heads_w + j * 256, 256), 256)
            g_attn[i, :, span(j, 256)] = dot(gb[seq_rows(i), :], outw[w_rows, :], NT).astype(LOW)

        loop(heads_w // 256, tile)

    def attend_back_pairs(i, start, stop):
        seg_q = segs[0, i:i + 1, :].astype(F32)

        def pair(p):
            lanes = span(p, LANES)
            v_lanes = pl.ds(pl.multiple_of(heads_w + p * LANES, LANES), LANES)
            qp = q[seq_rows(i), lanes]
            g = g_attn[i, :, lanes]
            gt = g.astype(F32).T
            qs, qscaled, gs_, gts, deltas, lses = [], [], [], [], [], []
            for head in range(2):
                at = pl.ds(pl.multiple_of(p * LANES + head * HEAD_DIM, HEAD_DIM), HEAD_DIM)
                mask = half_lanes(qp.shape, head)
                part = gt[head * HEAD_DIM:(head + 1) * HEAD_DIM, :]
                deltas.append(jnp.sum(part * attn_t[i, at, :], axis=0, keepdims=True))
                zeros = jnp.zeros_like(part)
                full = jnp.concatenate([part, zeros] if head == 0 else [zeros, part], axis=0)
                gts.append(full.astype(LOW))
                gs_.append(jnp.where(mask, g, jnp.zeros_like(g)))
                qs.append(jnp.where(mask, qp, jnp.zeros_like(qp)))
                qscaled.append(qs[-1] * jnp.asarray(0.125, LOW))
                lses.append(st[i, p, 4 + head:5 + head, :])
            dqt = [0.0, 0.0]
            for m in range(4):
                k = kv[i, m, :, lanes]
                kt = k.T
                v = kv[i, m, :, v_lanes]
                allowed = segk[m, :, i:i + 1] == seg_q
                dk = dv = 0.0
                for head in range(2):
                    score = dot(k, qscaled[head], NT)
                    probs = jnp.exp(jnp.where(allowed, score - lses[head], MASKED))
                    ds = (probs * (dot(v, gts[head]) - deltas[head])).astype(LOW)
                    dk = dk + dot(ds, qs[head])
                    dv = dv + dot(probs.astype(LOW), gs_[head])
                    dqt[head] = dqt[head] + dot(kt[head * HEAD_DIM:(head + 1) * HEAD_DIM, :], ds)
                parts_kv[m][:, lanes] = (dk * 0.125).astype(LOW)
                parts_kv[m][:, v_lanes] = dv.astype(LOW)
            dq = (jnp.concatenate(dqt, axis=0).T * 0.125).astype(LOW)
            dqkv[seq_rows(i), lanes] = dq
            qvacc[:, lanes] += fold(dq.astype(F32))

        lax.fori_loop(start, stop, lambda p, c: (pair(p), c)[1], 0)

    near_got, far_got, dq_got = [None] * 2, [None] * 2, [None] * 2
    kv_cols = pl.ds(heads_w, 2 * heads_w)

    def keys_near(i):
        near_got[i] = [
            copies.start(parts_kv[3], dkv_r.at[i, 2], seq_peer[1]),
            copies.start(parts_kv[1], dkv_r.at[i, 0], seq_peer[1]),
        ]
        at = (seq_rows(i), pl.ds(0, heads_w))
        dq_got[i] = copies.start(dqkv.at[at], dqkv_r.at[at], seq_peer[1])

    def keys_far(i):
        near_got[i][0].wait_recv()

        def part(c):
            at = span(c, 64)
            t2[i, at, :] = (parts_kv[2][at, :].astype(F32) + dkv_r[i, 2, at, :].astype(F32)).astype(LOW)

        loop(rows // 64, part)
        far_got[i] = copies.start(t2.at[i], dkv_r.at[i, 1], seq_peer[2])
        near_got[i][1].wait_recv()

        def rest(c):
            at = span(c, 64)
            to = pl.ds(pl.multiple_of(i * rows + c * 64, 64), 64)
            dqkv[to, kv_cols] = (parts_kv[0][at, :].astype(F32) + dkv_r[i, 0, at, :].astype(F32)).astype(LOW)

        loop(rows // 64, rest)

    dkv_got, gf_got = [None] * 2, [None] * 2

    def keys_done(i):
        far_got[i].wait_recv()

        def part(c):
            at = span(c, 64)
            to = pl.ds(pl.multiple_of(i * rows + c * 64, 64), 64)
            low = (dqkv[to, kv_cols].astype(F32) + dkv_r[i, 1, at, :].astype(F32)).astype(LOW)
            dqkv[to, kv_cols] = low
            qvacc[:, pl.ds(heads_w, heads_w)] += fold(low[:, heads_w:].astype(F32))

        loop(rows // 64, part)
        at = (seq_rows(i), kv_cols)
        dkv_got[i] = copies.start(dqkv.at[at], dqkv_r.at[at], seq_peer[1])

    def first_back(i):
        gs_got[i].wait_send()

        def tile(j):
            at = span(j, 256)
            total = 0.0
            for c in range(3):
                total = total + dot(dqkv[seq_rows(i), c * heads_w:(c + 1) * heads_w], wqkv[c, at, :], NT)
            gs[seq_rows(i), at] = total.astype(LOW)

        loop(width // 256, tile)
        gf_got[i] = copies.start(gs.at[seq_rows(i), :], gf_r.at[seq_rows(i), :], across)

        def sums(c):
            at = pl.ds(pl.multiple_of(i * rows + c * CHUNK, CHUNK), CHUNK)
            g = gs[at, :].astype(F32)
            normed = (tok[at, :].astype(F32) - stat[0, at, 0:1]) * stat[0, at, 1:2]
            vec[0] += fold(g * normed)
            vec[1] += fold(g)

        loop(rows // CHUNK, sums)

    def norm1_back(i):
        gf_got[i].wait()

        def part(c):
            at = pl.ds(pl.multiple_of(i * rows + c * CHUNK, CHUNK), CHUNK)
            g = gs[at, :].astype(F32) + gf_r[at, :].astype(F32)
            inverse = stat[0, at, 1:2]
            normed = (tok[at, :].astype(F32) - stat[0, at, 0:1]) * inverse
            e = g * g1[...]
            e = e - jnp.mean(e, axis=-1, keepdims=True) - normed * jnp.mean(e * normed, axis=-1, keepdims=True)
            gs[at, :] = (gb[at, :].astype(F32) + inverse * e).astype(LOW)

        loop(rows // CHUNK, part)
        load(gs.at[seq_rows(i), :], tg_h.at[seq_rows(i), :])

    def piece_tiles(piece, chip, body):
        left, left_r, right, right_r, cols = piece
        at_rows = pl.ds(pl.multiple_of(chip * 2 * quarter + core * quarter, quarter), quarter)

        def tile(j):
            at = span(j, WIDE)
            body(j, dot(left[at_rows, :], right[:, at]) + dot(left_r[chip], right_r[:, at]))

        loop(cols // WIDE, tile)

    class Group:
        def __init__(self, pieces, hold, offset, arrivals):
            self.pieces, self.hold, self.arrivals = pieces, hold, arrivals
            self.cols = sum(p[4] for p in pieces)
            self.xr = xr.at[:, pl.ds(offset, self.cols)]
            self.zr = [zr.at[d, :, pl.ds(offset, self.cols)] for d in range(n_dp - 1)]

        def tiles(self, chip, body):
            base = 0
            for piece in self.pieces:
                piece_tiles(
                    piece,
                    chip,
                    lambda j, value, base=base: body(
                        pl.ds(pl.multiple_of(base + j * WIDE, WIDE), WIDE), value
                    ),
                )
                base += piece[4]

        def first(self):
            for copy in self.arrivals():
                copy.wait_recv()

            def keep(at, value):
                self.hold[:, at] = value.astype(LOW)

            self.tiles(1 - x, keep)
            self.far = copies.start(self.hold, self.xr, seq_peer[2])

        def second(self):
            self.far.wait()

            def keep(at, value):
                self.hold[:, at] = (value + self.xr[:, at].astype(F32)).astype(LOW)

            self.tiles(x, keep)
            self.got = []
            for d in range(1, n_dp):
                to = lax.rem(z + n_dp - d, n_dp)
                mine = pl.ds(pl.multiple_of(to * block, block), block)
                self.got.append(copies.start(self.hold.at[mine, :], self.zr[d - 1], along[d]))

        def third(self, stage, row, targets):
            for copy in self.got:
                copy.wait_recv()
            mine = pl.ds(pl.multiple_of(z * block, block), block)
            at_col = 0
            for target, size in targets:
                at = pl.ds(at_col, size)
                total = self.hold[mine, at].astype(F32)
                for d in range(n_dp - 1):
                    total = total + self.zr[d][:, at].astype(F32)
                place = stage.at[row:row + block, 0:size]
                stage[row:row + block, 0:size] = total
                load(place, target)
                at_col += size
                row += block
            return row

    attn_own = attn.at[:, own_heads]
    q_cols, k_cols, v_cols = (slice(c * heads_w, (c + 1) * heads_w) for c in range(3))
    flips = {}
    group_a = Group(
        [(cot_t, cot_r, act, act_r, hidden)], up.at[0:rows, :], 0, lambda: flips["cot"] + act_got
    )
    group_b = Group(
        [(second_t, second_r, gh, gh_r, hidden)], up.at[rows:2 * rows, :], hidden, lambda: flips["second"] + gh_got
    )
    group_c = Group(
        [
            (gb_t, gb_r, attn_own, heads_r, heads_w),
            (first_t, first_r, dqkv.at[:, q_cols], dqkv_r.at[:, q_cols], heads_w),
        ],
        down.at[0:rows, :],
        2 * hidden,
        lambda: flips["gb"] + flips["first"] + heads_sent + dq_got,
    )
    group_d = Group(
        [(first_t, first_r, dqkv.at[:, c], dqkv_r.at[:, c], heads_w) for c in (k_cols, v_cols)],
        down.at[rows:2 * rows, :],
        2 * hidden + 2 * heads_w,
        lambda: dkv_got,
    )

    get_tok.wait()
    project(0)
    project(1)
    flips["first"] = swap_rows(first_t, first_r)
    get_out.wait()
    core_rows = pl.ds(pl.multiple_of(h * heads_w + core * (heads_w // 2), heads_w // 2), heads_w // 2)
    out_got = copies.start(outw.at[core_rows, :], outw.at[core_rows, :], across)
    for m in (1, 2, 3):
        seg_got[m].wait_recv()
    for m in range(4):
        seg_columns(m)
    for i in range(2):
        kv_got[i][1].wait_recv()
        attend_blocks(i, (0, 1), True, False)
    get_cot.wait()

    def sum_cot(c):
        vec[5] += fold(cot[span(c, CHUNK), :].astype(F32))

    loop(2 * rows // CHUNK, sum_cot)
    for i in range(2):
        flip(cot.at[seq_rows(i), :], i, cot_t)
    flips["cot"] = swap_rows(cot_t, cot_r)
    attend_far(0)
    attend_far(1)
    out_got.wait_recv()
    got_rows = pl.ds(
        pl.multiple_of((1 - h) * heads_w + core * (heads_w // 2), heads_w // 2), heads_w // 2
    )
    out_near = copies.start(outw.at[got_rows, :], outw.at[got_rows, :], seq_peer[1])
    out_near.wait_recv()
    get_up.wait()
    get_down.wait()
    for i in range(2):
        middle(i)
        feed(i)
    flips["second"] = swap_rows(second_t, second_r)
    feed_out(0)
    feed_out(1)
    group_a.first()
    norm2_back(0)
    attend_back_pairs(0, 0, pairs)
    keys_near(0)
    group_a.second()
    keys_far(0)
    group_b.first()
    norm2_back(1)
    for i in range(2):
        flip(gb.at[seq_rows(i), :], i, gb_t)
    flips["gb"] = swap_rows(gb_t, gb_r)
    near_got[0][0].wait_send()
    near_got[0][1].wait_send()
    attend_back_pairs(1, 0, pairs)
    keys_near(1)
    keys_done(0)
    keys_far(1)
    group_c.first()
    first_back(0)
    group_b.second()
    finish_output(0)
    finish_output(1)
    keys_done(1)
    first_back(1)
    ln1_got = copies.start(vec.at[0:2], ln1_r, across)
    group_d.first()
    group_c.second()
    norm1_back(0)
    group_d.second()
    norm1_back(1)

    ln1_got.wait()
    lines = [jnp.sum(vec[k] + ln1_r[k], axis=0, keepdims=True) for k in range(2)]
    lines += [jnp.sum(vec[k], axis=0, keepdims=True) for k in range(2, 6)]
    lines += [jnp.sum(qvacc[...], axis=0, keepdims=True)]
    ups = jnp.sum(upacc[...], axis=0, keepdims=True)
    lines += [ups[:, c * width:(c + 1) * width] for c in range(hidden // width)]
    lines += [jnp.zeros((16 - len(lines), width), F32)]
    vs[0] = jnp.concatenate(lines, axis=0)
    copies.start(vs.at[0], vr.at[0], seq_peer[1]).wait_recv()
    vs[1] = vs[0] + vr[0]
    copies.start(vs.at[1], vr.at[1], seq_peer[2]).wait_recv()
    vs[2] = vs[1] + vr[1]
    got = [copies.start(vs.at[2], vr.at[1 + d], along[d]) for d in range(1, n_dp)]
    row = group_a.third(mid, 0, [(downg_h.at[:, pl.ds(c * width, width)], width) for c in range(hidden // width)])
    row = group_b.third(mid, row, [(upg_h.at[:, pl.ds(c * width, width)], width) for c in range(hidden // width)])
    row = group_c.third(mid, row, [(outg_h, heads_w), (qkvg_h.at[0], heads_w)])
    row = group_d.third(mid, row, [(qkvg_h.at[1], heads_w), (qkvg_h.at[2], heads_w)])
    total = vs[2]
    for d in range(1, n_dp):
        got[d - 1].wait_recv()
        total = total + vr[1 + d]
    vec_o[...] = total
    waited = {id(c) for c in gs_got + [g.far for g in (group_a, group_b, group_c, group_d)]}
    waited |= {id(c) for c in ffn_got + gf_got + near_got[0] + [ln1_got]}
    for copy in copies.all:
        if id(copy) not in waited:
            copy.wait_send()
    for copy in loads[6:]:
        copy.wait()


def one_kernel(args):
    (
        tokens, segment_ids, ln1_gain, ln1_bias, qkv_weight, qv_bias, out_weight, out_bias,
        ln2_gain, ln2_bias, up_weight, up_bias, down_weight, down_bias, out_cotangent,
    ) = args
    count, rows, width = tokens.shape
    heads_w, hidden = qkv_weight.shape[2], up_weight.shape[1]
    n_dp = axis_size("dp")
    block = width // (4 * n_dp)
    total = count * rows
    grads = 2 * hidden + 4 * heads_w
    line = lambda v: v.reshape(1, -1)
    low = lambda *shape: pltpu.VMEM(shape, LOW)
    full = lambda *shape: pltpu.VMEM(shape, F32)
    shape = jax.ShapeDtypeStruct
    vmem, anywhere = pl.BlockSpec(memory_space=pltpu.VMEM), pl.BlockSpec(memory_space=pl.ANY)
    seg = jnp.concatenate([segment_ids, jnp.zeros((8 - count, rows), jnp.int32)], axis=0)
    return pl.pallas_call(
        functools.partial(layer_kernel, n_dp),
        in_specs=[anywhere, vmem, vmem, vmem, anywhere, vmem, anywhere, vmem, vmem, vmem, anywhere, vmem, anywhere, vmem, anywhere],
        out_specs=[anywhere] * 6 + [vmem],
        out_shape=[
            shape((total, width), LOW),
            shape((total, width), LOW),
            shape((block, hidden), F32),
            shape((block, hidden), F32),
            shape((block, heads_w), F32),
            shape((3, block, heads_w), F32),
            shape((16, width), F32),
        ],
        scratch_shapes=[
            low(total, width), low(total, width), low(3, width, heads_w), low(2 * heads_w, width),
            low(width, hidden), low(hidden, width), low(total, heads_w), low(2, 4, rows, 2 * heads_w),
            full(2, heads_w, rows), low(total, width), full(total, width), low(2, rows, width),
            low(total, hidden), low(total, hidden),
            low(width, total), low(width, total), low(width, total), low(width, total),
            low(2, rows, heads_w), low(2, rows, 2 * heads_w), low(total, width), low(total, width),
            full(2, total, 2), full(2, heads_w // LANES, 8, rows),
            low(total, width), low(total, width), low(total, width), low(2, 3, rows, 2 * heads_w),
            low(total, hidden), low(total, hidden),
            low(2, width // 4, total), low(2, width // 4, total), low(2, width // 4, total), low(2, width // 4, total),
            low(total, heads_w), low(total, 3 * heads_w), low(width // 4, grads), low(n_dp - 1, block, grads),
            pltpu.VMEM((4, 8, rows), jnp.int32), full(4, rows, 8), full(6, 8, width), full(8, 2 * heads_w), full(8, hidden),
            full(2, 8, width), full(3, 16, width), full(n_dp + 1, 16, width),
            pltpu.SemaphoreType.DMA((N_COPIES,)), pltpu.SemaphoreType.DMA((N_COPIES,)), pltpu.SemaphoreType.DMA((N_LOCAL,)),
        ],
        compiler_params=pltpu.CompilerParams(
            collective_id=0, has_side_effects=True, vmem_limit_bytes=FAST_VMEM
        ),
    )(
        tokens.reshape(total, width), seg, line(ln1_gain), line(ln1_bias), jnp.transpose(qkv_weight, (1, 0, 2)),
        qv_bias, out_weight, line(out_bias), line(ln2_gain), line(ln2_bias), up_weight, line(up_bias),
        down_weight, line(down_bias), out_cotangent.reshape(total, width),
    )


FAST_VMEM = 62 * 2**20


def fits(args):
    tokens, qkv_weight, up_weight = args[0], args[4], args[10]
    count, rows, width = tokens.shape
    heads_w, hidden = qkv_weight.shape[2], up_weight.shape[1]
    return (
        (axis_size("seq"), axis_size("head"), axis_size("dp")) == (4, 2, 4)
        and (count, rows) == (2, 256)
        and (width, heads_w, hidden) == (1024, 512, 2048)
    )


def fast(*args):
    tokens = args[0]
    out, tokens_grad, down_grad, up_grad, out_grad, qkv_grad, vec = one_kernel(args)
    n_dp = axis_size("dp")
    at = lax.axis_index("seq") * n_dp + lax.axis_index("dp")
    parts = axis_size("seq") * n_dp

    def mine(values):
        size = values.shape[-1] // parts
        return lax.dynamic_slice_in_dim(values, at * size, size, values.ndim - 1)

    return (
        out.reshape(tokens.shape),
        tokens_grad.reshape(tokens.shape),
        mine(vec[0]),
        mine(vec[1]),
        jnp.transpose(qkv_grad, (1, 0, 2)),
        mine(vec[6].reshape(2, -1)),
        out_grad.T,
        mine(vec[2]),
        mine(vec[3]),
        mine(vec[4]),
        up_grad,
        mine(vec[7:9].reshape(-1)),
        down_grad.T,
        mine(vec[5]),
    )


def shards(*args):
    return fast(*args) if fits(args) else general(*args)


def general(
    tokens,
    segment_ids,
    ln1_gain,
    ln1_bias,
    qkv_weight,
    qv_bias,
    out_weight,
    out_bias,
    ln2_gain,
    ln2_bias,
    up_weight,
    up_bias,
    down_weight,
    down_bias,
    out_cotangent,
):
    count, rows, features = tokens.shape
    local = qkv_weight.shape[2]
    hidden_local = up_weight.shape[1]
    n_seq, n_dp = axis_size("seq"), axis_size("dp")
    every = range(count)
    wq, wk, wv = (qkv_weight[:, c, :] for c in range(3))

    seg = gather_seq(segment_ids)
    seg_rows = [jnp.broadcast_to(segment_ids[s][None, :], (8, rows)) for s in every]
    seg_cols = [jnp.stack([part[s] for part in seg])[:, :, None] for s in every]

    half = out_weight.shape[0] // 2
    core = lax.axis_index("seq") & 1
    fetched = other_head(lax.dynamic_slice_in_dim(out_weight, core * half, half, 0))
    swapped = swap(fetched, "seq", 1)
    out_other = jnp.where(
        core == 0,
        jnp.concatenate([fetched, swapped], 0),
        jnp.concatenate([swapped, fetched], 0),
    )
    out_full = by_head(out_weight, out_other, 0)

    inputs, first, normed1, inverse1, queries, kvs = [], [], [], [], [], []
    for s in every:
        x = tokens[s].astype(F32)
        pre, normed, inverse = layer_norm(x, ln1_gain, ln1_bias)
        low = pre.astype(LOW)
        k = dot(low, wk).astype(LOW)
        v = (dot(low, wv) + qv_bias[1]).astype(LOW)
        kvs.append(gather_seq(jnp.stack([k, v])))
        queries.append((dot(low, wq) + qv_bias[0]).astype(LOW))
        inputs.append(x)
        first.append(low)
        normed1.append(normed)
        inverse1.append(inverse)

    attended = [attend(queries[s], seg_rows[s], seg_cols[s], kvs[s]) for s in every]

    outputs, second, act, g_hidden, g_middle, heads = [], [], [], [], [], []
    g_queries, g_kv = [], []
    vec = {
        name: 0.0 for name in ("out_b", "ln2_g", "ln2_b", "down_b", "up_b", "q_b", "v_b", "ln1_g", "ln1_b")
    }
    add = lambda name, value: vec.__setitem__(name, vec[name] + jnp.sum(value, axis=0))
    state = []
    for s in every:
        weights, attn_full, attn_low, inv_total = attended[s]
        mixed = by_head(attn_low, other_head(attn_low), 1)
        middle = inputs[s] + dot(mixed, out_full) + out_bias
        pre, normed2, inverse2 = layer_norm(middle, ln2_gain, ln2_bias)
        low = pre.astype(LOW)
        hidden = dot(low, up_weight) + up_bias
        activated, slope = gelu_pair(hidden)
        act_low = activated.astype(LOW)
        cot = out_cotangent[s]
        gh = (dot(cot, down_weight, NT) * slope).astype(LOW)
        g_second = head_sum(dot(gh, up_weight, NT))
        mlp = head_sum(dot(act_low, down_weight))
        outputs.append((middle + mlp + down_bias).astype(LOW))
        second.append(low)
        act.append(act_low)
        g_hidden.append(gh)
        heads.append(attn_low)
        state.append((normed2, inverse2, g_second))
        add("down_b", cot.astype(F32))
        add("up_b", gh.astype(F32))

    g_branch, g_first_parts = [], []
    for s in every:
        normed2, inverse2, g_second = state[s]
        weights, attn_full, attn_low, inv_total = attended[s]
        add("ln2_g", g_second * normed2)
        add("ln2_b", g_second)
        gm = out_cotangent[s].astype(F32) + norm_backward(g_second, normed2, inverse2, ln2_gain)
        gb = gm.astype(LOW)
        add("out_b", gb.astype(F32))
        g_attn = dot(gb, out_weight, NT).astype(LOW)
        dq, dkv = attend_back(queries[s], g_attn, attn_full, inv_total, weights, kvs[s])
        g_queries.append(dq)
        g_kv.append(scatter_seq(dkv).astype(LOW))
        g_middle.append(gm)
        g_branch.append(gb)

    join = lambda items: jnp.concatenate(items, axis=0)
    cot_all = out_cotangent.reshape(count * rows, features)
    cot_rel = relative_columns(cot_all)
    down_grad = weight_grad(cot_rel, join(act))
    up_grad = weight_grad(relative_columns(join(second)), join(g_hidden))
    out_grad = weight_grad(relative_columns(join(g_branch)), join(heads))

    tokens_grads = []
    for s in every:
        gq, gk, gv = g_queries[s], g_kv[s][0], g_kv[s][1]
        part = (dot(gq, wq, NT) + dot(gk, wk, NT) + dot(gv, wv, NT)).astype(LOW)
        add("q_b", gq.astype(F32))
        add("v_b", gv.astype(F32))
        add("ln1_g", part.astype(F32) * normed1[s])
        add("ln1_b", part.astype(F32))
        g_first = part.astype(F32) + other_head(part).astype(F32)
        tokens_grads.append(
            (g_middle[s] + norm_backward(g_first, normed1[s], inverse1[s], ln1_gain)).astype(LOW)
        )
    first_rel = relative_columns(join(first))
    g_proj = [join(g_queries), join([g[0] for g in g_kv]), join([g[1] for g in g_kv])]
    qkv_grad = jnp.stack([weight_grad(first_rel, g) for g in g_proj], axis=1)

    ln1 = jnp.stack([vec["ln1_g"], vec["ln1_b"]])
    ln1 = ln1 + other_head(ln1)
    wide = [ln1[0], ln1[1], vec["out_b"], vec["ln2_g"], vec["ln2_b"], vec["down_b"]]
    blocks = [v.reshape(n_seq, n_dp, -1) for v in wide + [vec["q_b"], vec["v_b"], vec["up_b"]]]
    sizes = [b.shape[2] for b in blocks]
    small = scatter_small(jnp.concatenate(blocks, axis=2))
    pieces, at = [], 0
    for size in sizes:
        pieces.append(small[at:at + size])
        at += size

    return (
        jnp.stack(outputs),
        jnp.stack(tokens_grads),
        pieces[0],
        pieces[1],
        qkv_grad,
        jnp.stack([pieces[6], pieces[7]]),
        out_grad.T,
        pieces[2],
        pieces[3],
        pieces[4],
        up_grad,
        pieces[8],
        down_grad.T,
        pieces[5],
    )


def solution(mesh):
    in_specs = (
        P("dp", "seq", None),
        P("dp", "seq"),
        P(),
        P(),
        P(None, None, "head"),
        P(None, "head"),
        P("head", None),
        P(),
        P(),
        P(),
        P(None, "head"),
        P("head"),
        P("head", None),
        P(),
        P("dp", "seq", None),
    )
    out_specs = (
        P("dp", "seq", None),
        P("dp", "seq", None),
        P(("seq", "dp")),
        P(("seq", "dp")),
        P(("seq", "dp"), None, "head"),
        P(None, ("head", "seq", "dp")),
        P("head", ("seq", "dp")),
        P(("seq", "dp")),
        P(("seq", "dp")),
        P(("seq", "dp")),
        P(("seq", "dp"), "head"),
        P(("head", "seq", "dp")),
        P("head", ("seq", "dp")),
        P(("seq", "dp")),
    )
    return jax.shard_map(shards, mesh=mesh, in_specs=in_specs, out_specs=out_specs, check_vma=False)
```

```python
import functools

import jax
import jax.numpy as jnp
from jax import lax
from jax.experimental import pallas as pl
from jax.experimental.pallas import tpu as pltpu
from jax.sharding import PartitionSpec as P

HEAD_DIM = 64
LANES = 128
EPSILON = 1e-05
MASKED = -1e30
F32 = jnp.float32
LOW = jnp.bfloat16
NN = (((1,), (0,)), ((), ()))
NT = (((1,), (1,)), ((), ()))
TN = (((0,), (0,)), ((), ()))
VMEM_LIMIT = 60 * 2**20


def dot(a, b, dims=NN):
    return lax.dot_general(a, b, dims, preferred_element_type=F32)


def axis_size(name):
    return lax.axis_size(name)


def swap(value, axis, mask):
    return lax.ppermute(value, axis, [(i, i ^ mask) for i in range(axis_size(axis))])


def bits_of(count):
    return [1 << b for b in range(count.bit_length() - 1)]


def layer_norm(inputs, gain, shift):
    center = jnp.mean(inputs, axis=-1, keepdims=True)
    centred = inputs - center
    spread = jnp.mean(centred * centred, axis=-1, keepdims=True)
    inverse = lax.rsqrt(spread + EPSILON)
    normed = centred * inverse
    return (normed * gain + shift, normed, inverse)


def norm_backward(upstream, normed, inverse, gain):
    scaled = upstream * gain
    centred = scaled - jnp.mean(scaled, axis=-1, keepdims=True)
    return inverse * (centred - normed * jnp.mean(scaled * normed, axis=-1, keepdims=True))


def gelu_pair(v):
    c = 0.7978845608028654
    square = v * v
    t = jnp.tanh(c * v * (1.0 + 0.044715 * square))
    half = 0.5 * (1.0 + t)
    return v * half, half + (0.5 * c) * v * (1.0 - t * t) * (1.0 + 3.0 * 0.044715 * square)


def half_lanes(shape, head):
    lane = lax.broadcasted_iota(jnp.int32, shape, 1)
    return (lane < HEAD_DIM) if head == 0 else (lane >= HEAD_DIM)


def attend_kernel(n, q_ref, seg_ref, segk_ref, *refs):
    kv_refs = refs[:n]
    w_ref, attn_ref, low_ref, inv_ref = refs[n:]
    q = q_ref[...] * jnp.asarray(0.125, LOW)
    seg_q = seg_ref[0:1, :]
    for head in range(2):
        qh = jnp.where(half_lanes(q.shape, head), q, jnp.zeros_like(q))
        parts, top = [], None
        for m in range(n):
            s = dot(kv_refs[m][0], qh, NT)
            s = jnp.where(segk_ref[m] == seg_q, s, MASKED)
            peak = jnp.max(s, axis=0, keepdims=True)
            top = peak if top is None else jnp.maximum(top, peak)
            parts.append(s)
        total, mixed = 0.0, 0.0
        for m in range(n):
            w = jnp.exp(parts[m] - top)
            total = total + jnp.sum(w, axis=0, keepdims=True)
            wl = w.astype(LOW)
            w_ref[head, m] = wl
            vt = kv_refs[m][1].T[head * HEAD_DIM:(head + 1) * HEAD_DIM, :]
            mixed = mixed + dot(vt, wl)
        inverse = 1.0 / total
        inv_ref[0, head:head + 1, :] = inverse
        attn_ref[head * HEAD_DIM:(head + 1) * HEAD_DIM, :] = mixed * inverse
    low_ref[...] = attn_ref[...].T.astype(LOW)


def attend(q, seg_rows, seg_cols, kvs):
    n, (rows, width) = len(kvs), q.shape
    pairs = width // LANES
    step = lambda p: (0, p)
    kv_spec = pl.BlockSpec((2, rows, LANES), lambda p: (0, 0, p))
    return pl.pallas_call(
        functools.partial(attend_kernel, n),
        grid=(pairs,),
        in_specs=[
            pl.BlockSpec((rows, LANES), step),
            pl.BlockSpec((8, rows), lambda p: (0, 0)),
            pl.BlockSpec((n, rows, 1), lambda p: (0, 0, 0)),
        ]
        + [kv_spec] * n,
        out_specs=[
            pl.BlockSpec((2, n, rows, rows), lambda p: (p, 0, 0, 0)),
            pl.BlockSpec((LANES, rows), lambda p: (p, 0)),
            pl.BlockSpec((rows, LANES), step),
            pl.BlockSpec((1, 2, rows), lambda p: (p, 0, 0)),
        ],
        out_shape=[
            jax.ShapeDtypeStruct((2 * pairs, n, rows, rows), LOW),
            jax.ShapeDtypeStruct((width, rows), F32),
            jax.ShapeDtypeStruct((rows, width), LOW),
            jax.ShapeDtypeStruct((pairs, 2, rows), F32),
        ],
        compiler_params=pltpu.CompilerParams(vmem_limit_bytes=VMEM_LIMIT),
        cost_estimate=pl.CostEstimate(
            flops=2 * pairs * n * rows * rows * 256 * 4,
            bytes_accessed=2 * pairs * n * rows * rows * 2,
            transcendentals=2 * pairs * n * rows * rows,
        ),
    )(q, seg_rows, seg_cols, *kvs)


def attend_back_kernel(n, q_ref, g_ref, attn_ref, inv_ref, w_ref, *refs):
    kv_refs = refs[:n]
    dq_ref = refs[n]
    dkv_refs = refs[n + 1:2 * n + 1]
    dqt_ref = refs[2 * n + 1]
    q = q_ref[...]
    gt = g_ref[...].astype(F32).T
    qs, gs, gts, deltas = [], [], [], []
    for head in range(2):
        rows_h = slice(head * HEAD_DIM, (head + 1) * HEAD_DIM)
        part = (gt[rows_h] * inv_ref[0, head:head + 1, :]).astype(LOW)
        deltas.append(jnp.sum(part.astype(F32) * attn_ref[rows_h, :], axis=0, keepdims=True))
        zeros = jnp.zeros_like(part)
        full = jnp.concatenate([part, zeros] if head == 0 else [zeros, part], axis=0)
        gts.append(full)
        gs.append(full.T)
        qs.append(jnp.where(half_lanes(q.shape, head), q, jnp.zeros_like(q)))
    dqt = [0.0, 0.0]
    for m in range(n):
        kt = kv_refs[m][0].T
        v = kv_refs[m][1]
        dk = dv = 0.0
        for head in range(2):
            w = w_ref[head, m]
            ds = (w.astype(F32) * (dot(v, gts[head]) - deltas[head])).astype(LOW)
            dk = dk + dot(ds, qs[head])
            dv = dv + dot(w, gs[head])
            dqt[head] = dqt[head] + dot(kt[head * HEAD_DIM:(head + 1) * HEAD_DIM, :], ds)
        dkv_refs[m][0] = (dk * 0.125).astype(LOW)
        dkv_refs[m][1] = dv.astype(LOW)
    dqt_ref[0:HEAD_DIM, :] = dqt[0]
    dqt_ref[HEAD_DIM:LANES, :] = dqt[1]
    dq_ref[...] = (dqt_ref[...].T * 0.125).astype(LOW)


def attend_back(q, g, attn, inverse, weights, kvs):
    n, (rows, width) = len(kvs), q.shape
    pairs = width // LANES
    step = lambda p: (0, p)
    kv_spec = pl.BlockSpec((2, rows, LANES), lambda p: (0, 0, p))
    out = pl.pallas_call(
        functools.partial(attend_back_kernel, n),
        grid=(pairs,),
        in_specs=[
            pl.BlockSpec((rows, LANES), step),
            pl.BlockSpec((rows, LANES), step),
            pl.BlockSpec((LANES, rows), lambda p: (p, 0)),
            pl.BlockSpec((1, 2, rows), lambda p: (p, 0, 0)),
            pl.BlockSpec((2, n, rows, rows), lambda p: (p, 0, 0, 0)),
        ]
        + [kv_spec] * n,
        out_specs=[pl.BlockSpec((rows, LANES), step)] + [kv_spec] * n,
        out_shape=[jax.ShapeDtypeStruct((rows, width), LOW)]
        + [jax.ShapeDtypeStruct((2, rows, width), LOW)] * n,
        scratch_shapes=[pltpu.VMEM((LANES, rows), F32)],
        compiler_params=pltpu.CompilerParams(vmem_limit_bytes=VMEM_LIMIT),
        cost_estimate=pl.CostEstimate(
            flops=2 * pairs * n * rows * rows * 256 * 8,
            bytes_accessed=2 * pairs * n * rows * rows * 2,
            transcendentals=0,
        ),
    )(q, g, attn, inverse, weights, *kvs)
    return out[0], out[1:]


def gather_seq(block):
    bits = bits_of(axis_size("seq"))
    blocks = {0: block}
    for bit in reversed(bits):
        for m in list(blocks):
            blocks[m | bit] = swap(blocks[m], "seq", bit)
    return [blocks[m] for m in range(len(blocks))]


def scatter_seq(parts):
    parts = dict(enumerate(parts))
    for bit in bits_of(axis_size("seq")):
        for m in [m for m in sorted(parts, reverse=True) if m & bit]:
            got = swap(parts.pop(m).astype(LOW), "seq", bit)
            parts[m ^ bit] = parts[m ^ bit].astype(F32) + got.astype(F32)
    return parts[0].astype(F32)


def scatter_line(term):
    n = axis_size("dp")
    me = lax.axis_index("dp")
    rows = term.shape[0] // n
    block = lambda i: lax.dynamic_slice_in_dim(term, jnp.clip(i, 0, n - 1) * rows, rows, 0)
    up = down = None
    for k in range(n - 1, 0, -1):
        send_up = block(me + k) if up is None else block(me + k) + up
        send_down = block(me - k) if down is None else block(me - k) + down
        up = lax.ppermute(
            send_up.astype(LOW), "dp", [(i, i + 1) for i in range(n) if i + k < n]
        ).astype(F32)
        down = lax.ppermute(
            send_down.astype(LOW), "dp", [(i, i - 1) for i in range(n) if i - k >= 0]
        ).astype(F32)
    out = block(me)
    return out if n == 1 else out + up + down


def relative_columns(rows):
    n = axis_size("seq")
    me = lax.axis_index("seq")
    width = rows.shape[1] // n
    return [lax.dynamic_slice_in_dim(rows, (me ^ m) * width, width, 1) for m in range(n)]


def weight_grad(left, right):
    return scatter_line(scatter_seq([dot(part, right, TN) for part in left]))


def scatter_small(blocks):
    for axis in ("seq", "dp"):
        n = axis_size(axis)
        me = lax.axis_index(axis)
        bits = bits_of(n)
        rest = blocks.shape[1:]
        for bit in reversed(bits):
            low, high = blocks[:bit], blocks[bit:]
            mine = (me & bit) != 0
            send = jnp.where(mine, low, high)
            blocks = jnp.where(mine, high, low) + swap(send, axis, bit)
        blocks = blocks.reshape(rest)
    return blocks


def other_head(value):
    return swap(value, "head", 1)


def head_sum(value):
    value = value.astype(LOW)
    return value.astype(F32) + other_head(value).astype(F32)


def by_head(mine, other, axis):
    first = lax.axis_index("head") == 0
    return jnp.where(
        first,
        jnp.concatenate([mine, other], axis),
        jnp.concatenate([other, mine], axis),
    )


MESH = pl.DeviceIdType.MESH
CHUNK = 32
WIDE = 512


def loop(count, body):
    def step(i, carry):
        body(i)
        return carry

    lax.fori_loop(0, count, step, 0)


def span(i, size):
    return pl.ds(pl.multiple_of(i * size, size), size)


def fold(value):
    return jnp.sum(value.reshape(value.shape[0] // 8, 8, value.shape[1]), axis=0)


class Copy:
    def __init__(self, copy, remote):
        self.copy, self.remote = copy, remote
        self.sent = self.got = False

    def wait_recv(self):
        if not self.got:
            self.got = True
            if self.remote:
                self.copy.wait_recv()
            else:
                self.copy.wait()

    def wait_send(self):
        if self.remote and not self.sent:
            self.copy.wait_send()
        self.sent = True

    def wait(self):
        self.wait_send()
        self.wait_recv()


class Copies:
    def __init__(self, send, recv, local):
        self.sems, self.all = (send, recv, local), []
        self.n_remote = self.n_local = 0

    def start(self, src, dst, device):
        copy = pltpu.make_async_remote_copy(
            src_ref=src,
            dst_ref=dst,
            send_sem=self.sems[0].at[self.n_remote],
            recv_sem=self.sems[1].at[self.n_remote],
            device_id=device,
            device_id_type=MESH,
        )
        self.n_remote += 1
        return self.begin(copy, True)

    def load(self, src, dst):
        copy = pltpu.make_async_copy(src, dst, self.sems[2].at[self.n_local])
        self.n_local += 1
        return self.begin(copy, False)

    def begin(self, copy, remote):
        copy.start()
        self.all.append(Copy(copy, remote))
        return self.all[-1]

    def finish(self):
        for copy in self.all:
            copy.wait()


N_COPIES = 128
N_LOCAL = 24


def layer_kernel(n_dp, *refs):
    (
        tok_h, seg_in, g1, b1, wqkv_h, qvb, outw_h, outb, g2, b2, up_h, upb, down_h, downb, cot_h,
        out_h, tg_h, downg_h, upg_h, outg_h, qkvg_h, vec_o,
        tok, cot, wqkv, outw, up, down, q, kv, attn_t, attn, mid, lnb, act, gh,
        first_t, second_t, cot_t, gb_t, g_attn, gs, ffn, stat, st,
        gs_r, ffn_r, gf_r, dkv_r, q_far, g_far, st_far, act_r, gh_r, first_r, second_r, cot_r, gb_r, heads_r, dqkv_r,
        xr, zr, xz, zz,
        segs, segk, vec, qvacc, upacc, ln1_r, vs, vr,
        send, recv, local,
    ) = refs
    rows = tok.shape[0] // 2
    width = tok.shape[1]
    heads_w = q.shape[1]
    hidden = act.shape[1]
    pairs = heads_w // LANES
    quarter = width // 4
    block = quarter // n_dp
    s = lax.axis_index("seq")
    h = lax.axis_index("head")
    z = lax.axis_index("dp")
    x, core = s // 2, s % 2
    seq_peer = [None] + [((x ^ (m >> 1)) * 2 + (core ^ (m & 1)), h, z) for m in (1, 2, 3)]
    across = (s, 1 - h, z)
    next_z, far_z = z + 1 - 2 * lax.rem(z, 2), lax.rem(z + 2, 4)
    beside, beyond = (s, h, next_z), (s, h, far_z)
    half_w = heads_w // 2
    copies = Copies(send, recv, local)
    load = copies.load

    own_out = pl.ds(pl.multiple_of(h * heads_w, heads_w), heads_w)
    get_tok = load(tok_h, tok)
    get_qkv = load(wqkv_h, wqkv)

    barrier = pltpu.get_barrier_semaphore()
    partners = seq_peer[1:] + [across, beside, beyond]
    for device in partners:
        pl.semaphore_signal(barrier, inc=1, device_id=device, device_id_type=MESH)

    vec[...] = jnp.zeros_like(vec)
    qvacc[...] = jnp.zeros_like(qvacc)
    upacc[...] = jnp.zeros_like(upacc)
    segs[0] = jnp.zeros_like(segs[0])
    segs[0, 0:2, :] = seg_in[...]
    def seq_rows(i):
        return slice(i * rows, (i + 1) * rows)

    def flip(src, i, dst):
        def part(c):
            dst[span(c, 256), seq_rows(i)] = src[:, span(c, 256)].T

        loop(width // 256, part)

    def swap_rows(flipped, target):
        return [
            copies.start(
                flipped.at[pl.ds(pl.multiple_of(c * 2 * quarter + (1 - core) * quarter, quarter), quarter), :],
                target.at[c],
                seq_peer[1],
            )
            for c in range(2)
        ]

    kv_got = [[[None] * 2 for _ in range(4)] for _ in range(2)]
    q_got, q_next = [None] * 2, [None] * 2

    def first_norm(i):
        def norm(c):
            at = pl.ds(pl.multiple_of(i * rows + c * CHUNK, CHUNK), CHUNK)
            v = tok[at, :].astype(F32)
            center = jnp.mean(v, axis=-1, keepdims=True)
            v = v - center
            inverse = lax.rsqrt(jnp.mean(v * v, axis=-1, keepdims=True) + EPSILON)
            stat[0, at, 0:1] = center
            stat[0, at, 1:2] = inverse
            lnb[i, span(c, CHUNK), :] = (v * inverse * g1[...] + b1[...]).astype(LOW)

        loop(rows // CHUNK, norm)

    def keys_values(i):
        k = dot(lnb[i], wqkv[1]).astype(LOW)
        v = (dot(lnb[i], wqkv[2]) + qvb[1:2, :]).astype(LOW)
        for part in range(2):
            cols = slice(part * half_w, (part + 1) * half_w)
            kv[i, 0, part, :, 0:half_w] = k[:, cols]
            kv[i, 0, part, :, half_w:heads_w] = v[:, cols]

    def send_keys(i):
        for part in range(2):
            kv_got[i][2][part] = copies.start(kv.at[i, 0, part], kv.at[i, 2, part], seq_peer[2])
        for part in range(2):
            kv_got[i][1][part] = copies.start(kv.at[i, 0, part], kv.at[i, 1, part], seq_peer[1])

    def queries(i):
        q[seq_rows(i), :] = (dot(lnb[i], wqkv[0]) + qvb[0:1, :]).astype(LOW)
        q_got[i] = copies.start(q.at[seq_rows(i), :], q_far.at[i, 0], seq_peer[2])
        flip(lnb.at[i], i, first_t)

    seg_got = [None] * 4

    def meet():
        pl.semaphore_wait(barrier, len(partners))
        for m in (1, 2, 3):
            seg_got[m] = copies.start(segs.at[0], segs.at[m], seq_peer[m])

    def key_lanes(p):
        lane = lax.rem(p, 2) * LANES
        return p // 2, pl.ds(pl.multiple_of(lane, LANES), LANES), pl.ds(pl.multiple_of(half_w + lane, LANES), LANES)

    def attend_blocks(i, blocks, begin, end, start, stop):
        seg_q = segs[0, i:i + 1, :].astype(F32)

        def pair(p):
            lanes = span(p, LANES)
            part, k_lanes, v_lanes = key_lanes(p)
            qp = q[seq_rows(i), lanes] * jnp.asarray(0.125, LOW)
            vts = [kv[i, m, part, :, v_lanes].T for m in blocks]
            for head in range(2):
                at = pl.ds(pl.multiple_of(p * LANES + head * HEAD_DIM, HEAD_DIM), HEAD_DIM)
                qh = jnp.where(half_lanes(qp.shape, head), qp, jnp.zeros_like(qp))
                parts = []
                top = None if begin else st[i, p, head:head + 1, :]
                old = top
                for m in blocks:
                    score = dot(kv[i, m, part, :, k_lanes], qh, NT)
                    score = jnp.where(segk[m, :, i:i + 1] == seg_q, score, MASKED)
                    peak = jnp.max(score, axis=0, keepdims=True)
                    top = peak if top is None else jnp.maximum(top, peak)
                    parts.append(score)
                total = mixed = 0.0
                for score, vt in zip(parts, vts):
                    w = jnp.exp(score - top)
                    total = total + jnp.sum(w, axis=0, keepdims=True)
                    mixed = mixed + dot(vt[head * HEAD_DIM:(head + 1) * HEAD_DIM, :], w.astype(LOW))
                if not begin:
                    scale = jnp.exp(old - top)
                    total = total + scale * st[i, p, 2 + head:3 + head, :]
                    mixed = mixed + scale * attn_t[i, at, :]
                if end:
                    mixed = mixed / total
                    st[i, p, 4 + head:5 + head, :] = top + jnp.log(total)
                else:
                    st[i, p, head:head + 1, :] = top
                    st[i, p, 2 + head:3 + head, :] = total
                attn_t[i, at, :] = mixed
            if end:
                to = pl.ds(pl.multiple_of(h * heads_w + p * LANES, LANES), LANES)
                attn[seq_rows(i), to] = attn_t[i, lanes, :].T.astype(LOW)

        lax.fori_loop(start, stop, lambda p, c: (pair(p), c)[1], 0)

    def seg_columns(m):
        segk[m] = segs[m].astype(F32).T

    own_heads = pl.ds(pl.multiple_of(h * heads_w, heads_w), heads_w)
    attn_got = [None, None]

    def forward_keys(i, part):
        kv_got[i][2][part].wait_recv()
        kv_got[i][3][part] = copies.start(kv.at[i, 2, part], kv.at[i, 3, part], seq_peer[1])

    def forward_queries(i):
        q_got[i].wait_recv()
        q_next[i] = copies.start(q_far.at[i, 0], q_far.at[i, 1], seq_peer[1])

    def attend_far(i, part):
        kv_got[i][3][part].wait_recv()
        attend_blocks(i, (2, 3), False, True, part * pairs // 2, (part + 1) * pairs // 2)

    def send_heads(i):
        mine = attn.at[seq_rows(i), own_heads]
        attn_got[i] = copies.start(mine, mine, across)
        heads_sent[i] = copies.start(mine, heads_r.at[seq_rows(i), :], seq_peer[1])

    heads_sent = [None, None]

    def middle(i):
        attn_got[i].wait_recv()

        def tile(j):
            at = span(j, WIDE)
            mid[seq_rows(i), at] = (
                dot(attn[seq_rows(i), :], outw[:, at])
                + tok[seq_rows(i), at].astype(F32)
                + outb[:, at]
            )

        loop(width // WIDE, tile)

        def norm(c):
            at = pl.ds(pl.multiple_of(i * rows + c * CHUNK, CHUNK), CHUNK)
            v = mid[at, :]
            center = jnp.mean(v, axis=-1, keepdims=True)
            v = v - center
            inverse = lax.rsqrt(jnp.mean(v * v, axis=-1, keepdims=True) + EPSILON)
            stat[1, at, 0:1] = center
            stat[1, at, 1:2] = inverse
            lnb[i, span(c, CHUNK), :] = (v * inverse * g2[...] + b2[...]).astype(LOW)

        loop(rows // CHUNK, norm)

    gs_got, ffn_got, act_got, gh_got = [None] * 2, [None] * 2, [None] * 2, [None] * 2

    def cot_down(i):
        def tile(j):
            at = span(j, 2 * WIDE)
            gh[seq_rows(i), at] = dot(cot[seq_rows(i), :], down[at, :], NT).astype(LOW)

        loop(hidden // (2 * WIDE), tile)

    def feed(i):
        at_rows = seq_rows(i)

        def tile(j):
            at = span(j, WIDE)
            value, slope = gelu_pair(dot(lnb[i], up[:, at]) + upb[:, at])
            act[at_rows, at] = value.astype(LOW)
            g = (gh[at_rows, at].astype(F32) * slope).astype(LOW)
            gh[at_rows, at] = g
            upacc[:, at] += fold(g.astype(F32))

        loop(hidden // WIDE, tile)

        def back(j):
            gs[at_rows, span(j, WIDE)] = dot(gh[at_rows, :], up[span(j, WIDE), :], NT).astype(LOW)

        loop(width // WIDE, back)
        gs_got[i] = copies.start(gs.at[at_rows, :], gs_r.at[at_rows, :], across)
        act_got[i] = copies.start(act.at[at_rows, :], act_r.at[at_rows, :], seq_peer[1])
        gh_got[i] = copies.start(gh.at[at_rows, :], gh_r.at[at_rows, :], seq_peer[1])
        flip(lnb.at[i], i, second_t)

    def feed_out(i):
        at_rows = seq_rows(i)

        def tile(j):
            ffn[at_rows, span(j, WIDE)] = dot(act[at_rows, :], down[:, span(j, WIDE)]).astype(LOW)

        loop(width // WIDE, tile)

    def send_feed_out(i):
        ffn_got[i] = copies.start(ffn.at[seq_rows(i), :], ffn_r.at[seq_rows(i), :], across)

    def finish_output(i):
        ffn_got[i].wait()

        def part(c):
            at = pl.ds(pl.multiple_of(i * rows + c * CHUNK, CHUNK), CHUNK)
            both = ffn[at, :].astype(F32) + ffn_r[at, :].astype(F32)
            ffn[at, :] = (mid[at, :] + both + downb[...]).astype(LOW)

        loop(rows // CHUNK, part)
        load(ffn.at[seq_rows(i), :], out_h.at[seq_rows(i), :])

    gb = down.at[2 * rows:4 * rows, :]
    parts_kv = [[down.at[(4 + 2 * i + m) * rows:(5 + 2 * i + m) * rows, :] for m in range(2)] for i in range(2)]
    dqkv = up.at[2 * rows:4 * rows, :]

    def norm2_back(i):
        gs_got[i].wait_recv()

        def part(c):
            at = pl.ds(pl.multiple_of(i * rows + c * CHUNK, CHUNK), CHUNK)
            g = gs[at, :].astype(F32) + gs_r[at, :].astype(F32)
            inverse = stat[1, at, 1:2]
            normed = (mid[at, :] - stat[1, at, 0:1]) * inverse
            vec[3] += fold(g * normed)
            vec[4] += fold(g)
            e = g * g2[...]
            e = e - jnp.mean(e, axis=-1, keepdims=True) - normed * jnp.mean(e * normed, axis=-1, keepdims=True)
            low = (cot[at, :].astype(F32) + inverse * e).astype(LOW)
            gb[at, :] = low
            vec[2] += fold(low.astype(F32))

        loop(rows // CHUNK, part)

        w_rows = pl.ds(pl.multiple_of(h * heads_w, heads_w), heads_w)
        g_attn[i] = dot(gb[seq_rows(i), :], outw[w_rows, :], NT).astype(LOW)

        def delta(p):
            g = g_attn[i, :, span(p, LANES)].astype(F32).T
            each = g * attn_t[i, span(p, LANES), :]
            for head in range(2):
                part = each[head * HEAD_DIM:(head + 1) * HEAD_DIM, :]
                st[i, p, 6 + head:7 + head, :] = jnp.sum(part, axis=0, keepdims=True)

        loop(pairs, delta)
        g_got[i] = [
            copies.start(g_attn.at[i], g_far.at[i, 0], seq_peer[2]),
            copies.start(st.at[i], st_far.at[i, 0], seq_peer[2]),
        ]

    g_got, g_next = [None] * 2, [None] * 2

    def forward_grads(i):
        for copy in g_got[i]:
            copy.wait_recv()
        g_next[i] = [
            copies.start(g_far.at[i, 0], g_far.at[i, 1], seq_peer[1]),
            copies.start(st_far.at[i, 0], st_far.at[i, 1], seq_peer[1]),
        ]

    def heads_of(pair_value, scale=None):
        if scale is not None:
            pair_value = pair_value * jnp.asarray(scale, LOW)
        zeros = jnp.zeros_like(pair_value)
        return [jnp.where(half_lanes(pair_value.shape, head), pair_value, zeros) for head in range(2)]

    def backward_terms(allowed, k, v, q_scaled, g, stats, head):
        score = dot(k, q_scaled[head], NT)
        probs = jnp.exp(jnp.where(allowed, score - stats[4 + head:5 + head, :], MASKED))
        return probs.astype(LOW), (probs * (dot(v, g[head], NT) - stats[6 + head:7 + head, :])).astype(LOW)

    def back_own(i):
        seg_q = segs[0, i:i + 1, :].astype(F32)

        def pair(p):
            lanes = span(p, LANES)
            v_lanes = pl.ds(pl.multiple_of(heads_w + p * LANES, LANES), LANES)
            part, k_in, v_in = key_lanes(p)
            qs = heads_of(q[seq_rows(i), lanes])
            q_scaled = heads_of(q[seq_rows(i), lanes], 0.125)
            g = heads_of(g_attn[i, :, lanes])
            stats = st[i, p]
            dqt = [0.0, 0.0]
            for m in range(4):
                k = kv[i, m, part, :, k_in]
                kt = k.T
                v = kv[i, m, part, :, v_in]
                allowed = segk[m, :, i:i + 1] == seg_q
                dk = dv = 0.0
                for head in range(2):
                    probs, ds = backward_terms(allowed, k, v, q_scaled, g, stats, head)
                    if m < 2:
                        dk = dk + dot(ds, qs[head])
                        dv = dv + dot(probs, g[head])
                    dqt[head] = dqt[head] + dot(kt[head * HEAD_DIM:(head + 1) * HEAD_DIM, :], ds)
                if m < 2:
                    parts_kv[i][m][:, lanes] = (dk * 0.125).astype(LOW)
                    parts_kv[i][m][:, v_lanes] = dv.astype(LOW)
            dq = (jnp.concatenate(dqt, axis=0).T * 0.125).astype(LOW)
            dqkv[seq_rows(i), lanes] = dq
            qvacc[:, lanes] += fold(dq.astype(F32))

        loop(pairs, pair)
        near_got[i] = copies.start(parts_kv[i][1], dkv_r.at[i], seq_peer[1])
        at = (seq_rows(i), pl.ds(0, heads_w))
        dq_got[i] = copies.start(dqkv.at[at], dqkv_r.at[at], seq_peer[1])

    def back_far(i):
        q_next[i].wait_recv()
        for copy in g_next[i]:
            copy.wait_recv()
        near_got[i].wait_recv()
        seg_q = [segs[2 + b, i:i + 1, :].astype(F32) for b in range(2)]
        at_rows = seq_rows(i)

        def pair(p):
            lanes = span(p, LANES)
            v_lanes = pl.ds(pl.multiple_of(heads_w + p * LANES, LANES), LANES)
            part, k_in, v_in = key_lanes(p)
            k = kv[i, 0, part, :, k_in]
            v = kv[i, 0, part, :, v_in]
            dk = dv = 0.0
            for b in range(2):
                qs = heads_of(q_far[i, b, :, lanes])
                q_scaled = heads_of(q_far[i, b, :, lanes], 0.125)
                g = heads_of(g_far[i, b, :, lanes])
                allowed = segk[0, :, i:i + 1] == seg_q[b]
                for head in range(2):
                    probs, ds = backward_terms(allowed, k, v, q_scaled, g, st_far[i, b, p], head)
                    dk = dk + dot(ds, qs[head])
                    dv = dv + dot(probs, g[head])
            near = lambda to: parts_kv[i][0][:, to].astype(F32) + dkv_r[i, :, to].astype(F32)
            k_at = pl.ds(pl.multiple_of(heads_w + p * LANES, LANES), LANES)
            v_at = pl.ds(pl.multiple_of(2 * heads_w + p * LANES, LANES), LANES)
            dqkv[at_rows, k_at] = (dk * 0.125 + near(lanes)).astype(LOW)
            low = (dv + near(v_lanes)).astype(LOW)
            dqkv[at_rows, v_at] = low
            qvacc[:, k_at] += fold(low.astype(F32))

        loop(pairs, pair)
        at = (at_rows, kv_cols)
        dkv_got[i] = copies.start(dqkv.at[at], dqkv_r.at[at], seq_peer[1])

    near_got, dq_got = [None] * 2, [None] * 2
    kv_cols = pl.ds(heads_w, 2 * heads_w)

    dkv_got, gf_got = [None] * 2, [None] * 2

    def first_back(i):
        gs_got[i].wait_send()

        def tile(j):
            at = span(j, WIDE)
            total = 0.0
            for c in range(3):
                total = total + dot(dqkv[seq_rows(i), c * heads_w:(c + 1) * heads_w], wqkv[c, at, :], NT)
            gs[seq_rows(i), at] = total.astype(LOW)

        loop(width // WIDE, tile)
        def sums(c):
            at = pl.ds(pl.multiple_of(i * rows + c * CHUNK, CHUNK), CHUNK)
            g = gs[at, :].astype(F32)
            normed = (tok[at, :].astype(F32) - stat[0, at, 0:1]) * stat[0, at, 1:2]
            vec[0] += fold(g * normed)
            vec[1] += fold(g)

        loop(rows // CHUNK, sums)

    def send_first_back(i):
        gf_got[i] = copies.start(gs.at[seq_rows(i), :], gf_r.at[seq_rows(i), :], across)

    def norm1_back(i):
        gf_got[i].wait()

        def part(c):
            at = pl.ds(pl.multiple_of(i * rows + c * CHUNK, CHUNK), CHUNK)
            g = gs[at, :].astype(F32) + gf_r[at, :].astype(F32)
            inverse = stat[0, at, 1:2]
            normed = (tok[at, :].astype(F32) - stat[0, at, 0:1]) * inverse
            e = g * g1[...]
            e = e - jnp.mean(e, axis=-1, keepdims=True) - normed * jnp.mean(e * normed, axis=-1, keepdims=True)
            gs[at, :] = (gb[at, :].astype(F32) + inverse * e).astype(LOW)

        loop(rows // CHUNK, part)
        load(gs.at[seq_rows(i), :], tg_h.at[seq_rows(i), :])

    def tiles(piece, chip, body):
        left, left_r, right, right_r, cols = piece
        at_rows = pl.ds(pl.multiple_of(chip * 2 * quarter + core * quarter, quarter), quarter)
        step = min(cols, 2 * WIDE)

        def tile(j):
            at = span(j, step)
            body(at, dot(left[at_rows, :], right[:, at]) + dot(left_r[chip], right_r[:, at]))

        loop(cols // step, tile)

    def block_rows(index):
        return pl.ds(pl.multiple_of(index * block, block), block)

    def send_beside(hold, arrive):
        further = lax.rem(next_z + 2, 4)
        return [
            copies.start(hold.at[block_rows(next_z), :], arrive[0], beside),
            copies.start(hold.at[block_rows(further), :], arrive[1], beside),
        ]

    def send_beyond(hold, arrive):
        at = block_rows(far_z)
        hold[at, :] = (hold[at, :].astype(F32) + arrive[1][...].astype(F32)).astype(LOW)
        return copies.start(hold.at[at, :], arrive[2], beyond)

    def own_block(hold, arrive, at=slice(None)):
        total = hold[block_rows(z), at].astype(F32)
        return total + arrive[0][:, at].astype(F32) + arrive[2][:, at].astype(F32)

    def hand_out(place, target, value):
        size = target.shape[1]
        top, left = place // 2 * block, place % 2 * (width // 2)
        mid[top:top + block, left:left + size] = value(slice(None))
        load(mid.at[top:top + block, left:left + size], target)
        return place + size * 2 // width

    class AcrossFirst:
        def __init__(self, piece, hold, offset, arrivals):
            self.piece, self.hold, self.arrivals = piece, hold, arrivals
            cols = pl.ds(offset, piece[4])
            self.xr = xr.at[:, cols]
            self.zr = [zr.at[d, :, cols] for d in range(3)]

        def prepare(self):
            for copy in self.arrivals():
                copy.wait_recv()

            def keep(at, value):
                self.hold[:, at] = value.astype(LOW)

            tiles(self.piece, 1 - x, keep)

        def across(self):
            self.far = copies.start(self.hold, self.xr, seq_peer[2])

        def beside(self):
            self.far.wait()

            def keep(at, value):
                self.hold[:, at] = (value + self.xr[:, at].astype(F32)).astype(LOW)

            tiles(self.piece, x, keep)
            self.near = send_beside(self.hold, self.zr)

        def beyond(self):
            for copy in self.near:
                copy.wait_recv()
            self.last = send_beyond(self.hold, self.zr)

        def done(self, place, target):
            self.last.wait_recv()
            return hand_out(place, target, lambda at: own_block(self.hold, self.zr, at))

    class AlongFirst:
        def __init__(self, piece, holds, offset, arrivals):
            self.piece, self.holds, self.arrivals = piece, holds, arrivals
            cols = pl.ds(offset, piece[4])
            self.zz = [[zz.at[r, d, :, cols] for d in range(3)] for r in range(2)]
            self.xz = xz.at[:, cols]

        def beside(self):
            for copy in self.arrivals():
                copy.wait_recv()
            self.near = []
            for r in (1, 0):

                def keep(at, value, r=r):
                    self.holds[r][:, at] = value.astype(LOW)

                tiles(self.piece, x ^ r, keep)
                self.near += send_beside(self.holds[r], self.zz[r])

        def beyond(self):
            for copy in self.near:
                copy.wait_recv()
            self.last = [send_beyond(self.holds[r], self.zz[r]) for r in (1, 0)]

        def across(self):
            for copy in self.last:
                copy.wait_recv()
            mine = block_rows(z)
            self.holds[1][mine, :] = own_block(self.holds[1], self.zz[1]).astype(LOW)
            self.far = copies.start(self.holds[1].at[mine, :], self.xz, seq_peer[2])

        def done(self, place, target):
            self.far.wait_recv()

            def value(at):
                return own_block(self.holds[0], self.zz[0], at) + self.xz[:, at].astype(F32)

            return hand_out(place, target, value)

    attn_own = attn.at[:, own_heads]
    q_cols, k_cols, v_cols = (slice(c * heads_w, (c + 1) * heads_w) for c in range(3))
    flips = {}
    down_piece = lambda at, n: (cot_t, cot_r, act.at[:, at:at + n], act_r.at[:, at:at + n], n)
    up_piece = lambda at, n: (second_t, second_r, gh.at[:, at:at + n], gh_r.at[:, at:at + n], n)
    proj_piece = lambda at: (first_t, first_r, dqkv.at[:, at], dqkv_r.at[:, at], heads_w)
    quarter_h = hidden // 4
    from_cot, from_second = lambda: flips["cot"] + act_got, lambda: flips["second"] + gh_got
    downs = [
        AcrossFirst(down_piece(at, n), up.at[0:rows, at:at + n], at, from_cot)
        for at, n in ((0, 2 * quarter_h), (2 * quarter_h, quarter_h), (3 * quarter_h, quarter_h))
    ]
    ups = [
        AlongFirst(
            up_piece(at, n), [up.at[rows:2 * rows, at:at + n], lnb.at[k, :, 0:n]], at, from_second
        )
        for k, (at, n) in enumerate(((0, 2 * quarter_h), (2 * quarter_h, quarter_h)))
    ]
    up_last = AcrossFirst(
        up_piece(3 * quarter_h, quarter_h), up.at[rows:2 * rows, 3 * quarter_h:hidden], hidden, from_second
    )
    base = hidden + quarter_h
    proj_out = AcrossFirst(
        (gb_t, gb_r, attn_own, heads_r, heads_w),
        down.at[0:rows, 0:heads_w],
        base,
        lambda: flips["gb"] + heads_sent,
    )
    proj_q = AcrossFirst(
        proj_piece(q_cols),
        down.at[0:rows, heads_w:2 * heads_w],
        base + heads_w,
        lambda: flips["first"] + dq_got,
    )
    proj_k, proj_v = (
        AcrossFirst(
            proj_piece(cols),
            down.at[rows:2 * rows, c * heads_w:(c + 1) * heads_w],
            base + (2 + c) * heads_w,
            lambda: flips["first"] + dkv_got,
        )
        for c, cols in enumerate((k_cols, v_cols))
    )

    def share_out():
        half = heads_w // 2
        get_out.wait()
        mine = pl.ds(pl.multiple_of(h * heads_w + core * half, half), half)
        return copies.start(outw.at[mine, :], outw.at[mine, :], across)

    def forward_out():
        out_got.wait_recv()
        half = heads_w // 2
        theirs = pl.ds(pl.multiple_of((1 - h) * heads_w + core * half, half), half)
        return copies.start(outw.at[theirs, :], outw.at[theirs, :], seq_peer[1])

    def scenes():
        for m in (1, 2, 3):
            seg_got[m].wait_recv()
        for m in range(4):
            seg_columns(m)

    def attend_near(i):
        for copy in kv_got[i][1]:
            copy.wait_recv()
        attend_blocks(i, (0, 1), True, False, 0, pairs)

    def prepare_cot():
        get_cot.wait()

        def part(c):
            vec[5] += fold(cot[span(c, CHUNK), :].astype(F32))

        loop(2 * rows // CHUNK, part)
        for i in range(2):
            flip(cot.at[seq_rows(i), :], i, cot_t)
        flips["cot"] = swap_rows(cot_t, cot_r)

    def flip_branch():
        for i in range(2):
            flip(gb.at[seq_rows(i), :], i, gb_t)
        flips["gb"] = swap_rows(gb_t, gb_r)

    def vectors():
        ln1_got.wait_recv()
        lines = [jnp.sum(vec[k] + ln1_r[k], axis=0, keepdims=True) for k in range(2)]
        lines += [jnp.sum(vec[k], axis=0, keepdims=True) for k in range(2, 6)]
        lines += [jnp.sum(qvacc[...], axis=0, keepdims=True)]
        sums = jnp.sum(upacc[...], axis=0, keepdims=True)
        lines += [sums[:, c * width:(c + 1) * width] for c in range(hidden // width)]
        lines += [jnp.zeros((16 - len(lines), width), F32)]
        vs[0] = jnp.concatenate(lines, axis=0)
        return copies.start(vs.at[0], vr.at[0], seq_peer[1])

    def vectors_on(k, copy, device):
        copy.wait_recv()
        vs[k] = vs[k - 1] + vr[k - 1]
        return copies.start(vs.at[k], vr.at[k], device)

    def vectors_done():
        vec_4.wait_recv()
        vec_o[...] = vs[3] + vr[3]

    spans = [(0, 2 * quarter_h), (2 * quarter_h, quarter_h), (3 * quarter_h, quarter_h)]

    get_tok.wait()
    first_norm(0)
    get_qkv.wait()
    keys_values(0)
    meet()
    send_keys(0)
    get_out, get_cot = load(outw_h, outw.at[own_out, :]), load(cot_h, cot)
    get_down, get_up = load(down_h, down), load(up_h, up)
    first_norm(1)
    keys_values(1)
    send_keys(1)
    queries(0)
    queries(1)
    flips["first"] = swap_rows(first_t, first_r)
    out_got = share_out()
    scenes()
    attend_near(0)
    attend_near(1)
    forward_keys(0, 0)
    prepare_cot()
    forward_keys(0, 1)
    attend_far(0, 0)
    attend_far(0, 1)
    send_heads(0)
    out_near = forward_out()
    get_down.wait()
    cot_down(0)
    forward_keys(1, 0)
    cot_down(1)
    attend_far(1, 0)
    forward_keys(1, 1)
    attend_far(1, 1)
    send_heads(1)
    out_near.wait_recv()
    get_up.wait()
    middle(0)
    feed(0)
    middle(1)
    feed(1)
    flips["second"] = swap_rows(second_t, second_r)
    downs[0].prepare()
    downs[0].across()
    ups[0].beside()
    ups[1].beside()
    feed_out(0)
    send_feed_out(0)
    feed_out(1)
    forward_queries(0)
    forward_queries(1)
    norm2_back(0)
    downs[1].prepare()
    downs[1].across()
    back_own(0)
    norm2_back(1)
    downs[0].beside()
    forward_grads(0)
    downs[2].prepare()
    downs[2].across()
    flip_branch()
    ups[0].beyond()
    ups[1].beyond()
    back_far(0)
    first_back(0)
    send_first_back(0)
    proj_out.prepare()
    proj_out.across()
    back_own(1)
    forward_grads(1)
    downs[0].beyond()
    downs[1].beside()
    up_last.prepare()
    up_last.across()
    downs[2].beside()
    back_far(1)
    first_back(1)
    ln1_got = copies.start(vec.at[0:2], ln1_r, across)
    send_first_back(1)
    send_feed_out(1)
    proj_q.prepare()
    proj_q.across()
    proj_k.prepare()
    proj_k.across()
    proj_v.prepare()
    proj_v.across()
    downs[1].beyond()
    downs[2].beyond()
    ups[0].across()
    ups[1].across()
    proj_out.beside()
    norm1_back(0)
    finish_output(0)
    vec_1 = vectors()
    up_last.beside()
    proj_out.beyond()
    vec_2 = vectors_on(1, vec_1, seq_peer[2])
    proj_q.beside()
    up_last.beyond()
    norm1_back(1)
    proj_k.beside()
    proj_q.beyond()
    proj_v.beside()
    proj_k.beyond()
    vec_3 = vectors_on(2, vec_2, beside)
    finish_output(1)
    proj_v.beyond()
    vec_4 = vectors_on(3, vec_3, beyond)
    place = 0
    for group, (at, n) in zip(downs, spans): place = group.done(place, downg_h.at[:, at:at + n])
    for group, (at, n) in zip(ups + [up_last], spans): place = group.done(place, upg_h.at[:, at:at + n])
    place = proj_out.done(place, outg_h)
    place = proj_q.done(place, qkvg_h.at[0])
    place = proj_k.done(place, qkvg_h.at[1])
    place = proj_v.done(place, qkvg_h.at[2])
    vectors_done()
    copies.finish()


def one_kernel(args):
    (
        tokens, segment_ids, ln1_gain, ln1_bias, qkv_weight, qv_bias, out_weight, out_bias,
        ln2_gain, ln2_bias, up_weight, up_bias, down_weight, down_bias, out_cotangent,
    ) = args
    count, rows, width = tokens.shape
    heads_w, hidden = qkv_weight.shape[2], up_weight.shape[1]
    n_dp = axis_size("dp")
    block = width // (4 * n_dp)
    total = count * rows
    grads = hidden + hidden // 4 + 4 * heads_w
    line = lambda v: v.reshape(1, -1)
    low = lambda *shape: pltpu.VMEM(shape, LOW)
    full = lambda *shape: pltpu.VMEM(shape, F32)
    shape = jax.ShapeDtypeStruct
    vmem, anywhere = pl.BlockSpec(memory_space=pltpu.VMEM), pl.BlockSpec(memory_space=pl.ANY)
    return pl.pallas_call(
        functools.partial(layer_kernel, n_dp),
        in_specs=[anywhere, vmem, vmem, vmem, anywhere, vmem, anywhere, vmem, vmem, vmem, anywhere, vmem, anywhere, vmem, anywhere],
        out_specs=[anywhere] * 6 + [vmem],
        out_shape=[
            shape((total, width), LOW),
            shape((total, width), LOW),
            shape((block, hidden), F32),
            shape((block, hidden), F32),
            shape((block, heads_w), F32),
            shape((3, block, heads_w), F32),
            shape((16, width), F32),
        ],
        scratch_shapes=[
            low(total, width), low(total, width), low(3, width, heads_w), low(2 * heads_w, width),
            low(width, hidden), low(hidden, width), low(total, heads_w), low(2, 4, 2, rows, heads_w),
            full(2, heads_w, rows), low(total, width), full(total, width), low(2, rows, width),
            low(total, hidden), low(total, hidden),
            low(width, total), low(width, total), low(width, total), low(width, total),
            low(2, rows, heads_w), low(total, width), low(total, width),
            full(2, total, 2), full(2, heads_w // LANES, 8, rows),
            low(total, width), low(total, width), low(total, width), low(2, rows, 2 * heads_w),
            low(2, 2, rows, heads_w), low(2, 2, rows, heads_w), full(2, 2, heads_w // LANES, 8, rows),
            low(total, hidden), low(total, hidden),
            low(2, width // 4, total), low(2, width // 4, total), low(2, width // 4, total), low(2, width // 4, total),
            low(total, heads_w), low(total, 3 * heads_w), low(width // 4, grads), low(3, block, grads),
            low(block, 3 * hidden // 4), low(2, 3, block, 3 * hidden // 4),
            pltpu.VMEM((4, 8, rows), jnp.int32), full(4, rows, 8), full(6, 8, width), full(8, 2 * heads_w), full(8, hidden),
            full(2, 8, width), full(4, 16, width), full(4, 16, width),
            pltpu.SemaphoreType.DMA((N_COPIES,)), pltpu.SemaphoreType.DMA((N_COPIES,)), pltpu.SemaphoreType.DMA((N_LOCAL,)),
        ],
        compiler_params=pltpu.CompilerParams(
            collective_id=0, has_side_effects=True, vmem_limit_bytes=FAST_VMEM
        ),
    )(
        tokens.reshape(total, width), segment_ids, line(ln1_gain), line(ln1_bias), jnp.transpose(qkv_weight, (1, 0, 2)),
        qv_bias, out_weight, line(out_bias), line(ln2_gain), line(ln2_bias), up_weight, line(up_bias),
        down_weight, line(down_bias), out_cotangent.reshape(total, width),
    )


FAST_VMEM = 62 * 2**20


def fits(args):
    tokens, qkv_weight, up_weight = args[0], args[4], args[10]
    count, rows, width = tokens.shape
    heads_w, hidden = qkv_weight.shape[2], up_weight.shape[1]
    return (
        (axis_size("seq"), axis_size("head"), axis_size("dp")) == (4, 2, 4)
        and (count, rows) == (2, 256)
        and (width, heads_w, hidden) == (1024, 512, 2048)
    )


def split_kernel(parts, index_ref, vec_ref, *refs):
    big = (len(refs) - 1 - 8) // 3
    sources, targets, small = refs[:big], refs[big:2 * big], refs[2 * big:2 * big + 8]
    held, sem = refs[2 * big + 8:-1], refs[-1]
    moves = [pltpu.make_async_copy(a, b, sem.at[0, k]) for k, (a, b) in enumerate(zip(sources, held))]
    for move in moves:
        move.start()
    back = [pltpu.make_async_copy(a, b, sem.at[1, k]) for k, (a, b) in enumerate(zip(held, targets))]
    for move, out in zip(moves, back):
        move.wait()
        out.start()
    at = index_ref[0]
    width = vec_ref.shape[1]

    def piece(row, size):
        shift = lax.rem(width - lax.rem(at * size, width), width)
        return pltpu.roll(vec_ref[row:row + 1, :], shift, 1)[:, :size]

    size = width // parts
    for ref, row in zip(small[:6], (0, 1, 2, 3, 4, 5)):
        ref[...] = piece(row, size)
    half = vec_ref[6:7, :]
    shift = lax.rem(width - at * (size // 2), width)
    turned = pltpu.roll(half, shift, 1)
    small[6][0:1, :] = turned[:, :size // 2]
    small[6][1:2, :] = pltpu.roll(turned, width // 2, 1)[:, :size // 2]
    size = small[7].shape[1]
    low, high = piece(7, size), piece(8, size)
    small[7][...] = jnp.where(at * size < width, low, high)
    for out in back:
        out.wait()


def split(parts, big, vec):
    at = lax.axis_index("seq") * axis_size("dp") + lax.axis_index("dp")
    size = vec.shape[1] // parts
    shape = jax.ShapeDtypeStruct
    smalls = [shape((1, size), F32)] * 6 + [shape((2, size // 2), F32), shape((1, 2 * size), F32)]
    vmem, anywhere = pl.BlockSpec(memory_space=pltpu.VMEM), pl.BlockSpec(memory_space=pl.ANY)
    out = pl.pallas_call(
        functools.partial(split_kernel, parts),
        in_specs=[pl.BlockSpec(memory_space=pltpu.SMEM), vmem] + [anywhere] * len(big),
        out_specs=[anywhere] * len(big) + [vmem] * 8,
        out_shape=[shape(v.shape, v.dtype) for v in big] + smalls,
        scratch_shapes=[pltpu.VMEM(v.shape, v.dtype) for v in big] + [pltpu.SemaphoreType.DMA((2, len(big)))],
        compiler_params=pltpu.CompilerParams(vmem_limit_bytes=FAST_VMEM),
    )(at.astype(jnp.int32).reshape(1), vec, *big)
    return out[:len(big)], out[len(big):]


def fast(*args):
    tokens = args[0]
    *big, vec = one_kernel(args)
    big, small = split(axis_size("seq") * axis_size("dp"), big, vec)
    out, tokens_grad, down_grad, up_grad, out_grad, qkv_grad = big
    flat = [v.reshape(-1) for v in small]
    return (
        out.reshape(tokens.shape),
        tokens_grad.reshape(tokens.shape),
        flat[0],
        flat[1],
        jnp.transpose(qkv_grad, (1, 0, 2)),
        small[6],
        out_grad.T,
        flat[2],
        flat[3],
        flat[4],
        up_grad,
        flat[7],
        down_grad.T,
        flat[5],
    )


def shards(*args):
    return fast(*args) if fits(args) else general(*args)


def general(
    tokens,
    segment_ids,
    ln1_gain,
    ln1_bias,
    qkv_weight,
    qv_bias,
    out_weight,
    out_bias,
    ln2_gain,
    ln2_bias,
    up_weight,
    up_bias,
    down_weight,
    down_bias,
    out_cotangent,
):
    count, rows, features = tokens.shape
    local = qkv_weight.shape[2]
    hidden_local = up_weight.shape[1]
    n_seq, n_dp = axis_size("seq"), axis_size("dp")
    every = range(count)
    wq, wk, wv = (qkv_weight[:, c, :] for c in range(3))

    seg = gather_seq(segment_ids)
    seg_rows = [jnp.broadcast_to(segment_ids[s][None, :], (8, rows)) for s in every]
    seg_cols = [jnp.stack([part[s] for part in seg])[:, :, None] for s in every]

    half = out_weight.shape[0] // 2
    core = lax.axis_index("seq") & 1
    fetched = other_head(lax.dynamic_slice_in_dim(out_weight, core * half, half, 0))
    swapped = swap(fetched, "seq", 1)
    out_other = jnp.where(
        core == 0,
        jnp.concatenate([fetched, swapped], 0),
        jnp.concatenate([swapped, fetched], 0),
    )
    out_full = by_head(out_weight, out_other, 0)

    inputs, first, normed1, inverse1, queries, kvs = [], [], [], [], [], []
    for s in every:
        x = tokens[s].astype(F32)
        pre, normed, inverse = layer_norm(x, ln1_gain, ln1_bias)
        low = pre.astype(LOW)
        k = dot(low, wk).astype(LOW)
        v = (dot(low, wv) + qv_bias[1]).astype(LOW)
        kvs.append(gather_seq(jnp.stack([k, v])))
        queries.append((dot(low, wq) + qv_bias[0]).astype(LOW))
        inputs.append(x)
        first.append(low)
        normed1.append(normed)
        inverse1.append(inverse)

    attended = [attend(queries[s], seg_rows[s], seg_cols[s], kvs[s]) for s in every]

    outputs, second, act, g_hidden, g_middle, heads = [], [], [], [], [], []
    g_queries, g_kv = [], []
    vec = {
        name: 0.0 for name in ("out_b", "ln2_g", "ln2_b", "down_b", "up_b", "q_b", "v_b", "ln1_g", "ln1_b")
    }
    add = lambda name, value: vec.__setitem__(name, vec[name] + jnp.sum(value, axis=0))
    state = []
    for s in every:
        weights, attn_full, attn_low, inv_total = attended[s]
        mixed = by_head(attn_low, other_head(attn_low), 1)
        middle = inputs[s] + dot(mixed, out_full) + out_bias
        pre, normed2, inverse2 = layer_norm(middle, ln2_gain, ln2_bias)
        low = pre.astype(LOW)
        hidden = dot(low, up_weight) + up_bias
        activated, slope = gelu_pair(hidden)
        act_low = activated.astype(LOW)
        cot = out_cotangent[s]
        gh = (dot(cot, down_weight, NT) * slope).astype(LOW)
        g_second = head_sum(dot(gh, up_weight, NT))
        mlp = head_sum(dot(act_low, down_weight))
        outputs.append((middle + mlp + down_bias).astype(LOW))
        second.append(low)
        act.append(act_low)
        g_hidden.append(gh)
        heads.append(attn_low)
        state.append((normed2, inverse2, g_second))
        add("down_b", cot.astype(F32))
        add("up_b", gh.astype(F32))

    g_branch, g_first_parts = [], []
    for s in every:
        normed2, inverse2, g_second = state[s]
        weights, attn_full, attn_low, inv_total = attended[s]
        add("ln2_g", g_second * normed2)
        add("ln2_b", g_second)
        gm = out_cotangent[s].astype(F32) + norm_backward(g_second, normed2, inverse2, ln2_gain)
        gb = gm.astype(LOW)
        add("out_b", gb.astype(F32))
        g_attn = dot(gb, out_weight, NT).astype(LOW)
        dq, dkv = attend_back(queries[s], g_attn, attn_full, inv_total, weights, kvs[s])
        g_queries.append(dq)
        g_kv.append(scatter_seq(dkv).astype(LOW))
        g_middle.append(gm)
        g_branch.append(gb)

    join = lambda items: jnp.concatenate(items, axis=0)
    cot_all = out_cotangent.reshape(count * rows, features)
    cot_rel = relative_columns(cot_all)
    down_grad = weight_grad(cot_rel, join(act))
    up_grad = weight_grad(relative_columns(join(second)), join(g_hidden))
    out_grad = weight_grad(relative_columns(join(g_branch)), join(heads))

    tokens_grads = []
    for s in every:
        gq, gk, gv = g_queries[s], g_kv[s][0], g_kv[s][1]
        part = (dot(gq, wq, NT) + dot(gk, wk, NT) + dot(gv, wv, NT)).astype(LOW)
        add("q_b", gq.astype(F32))
        add("v_b", gv.astype(F32))
        add("ln1_g", part.astype(F32) * normed1[s])
        add("ln1_b", part.astype(F32))
        g_first = part.astype(F32) + other_head(part).astype(F32)
        tokens_grads.append(
            (g_middle[s] + norm_backward(g_first, normed1[s], inverse1[s], ln1_gain)).astype(LOW)
        )
    first_rel = relative_columns(join(first))
    g_proj = [join(g_queries), join([g[0] for g in g_kv]), join([g[1] for g in g_kv])]
    qkv_grad = jnp.stack([weight_grad(first_rel, g) for g in g_proj], axis=1)

    ln1 = jnp.stack([vec["ln1_g"], vec["ln1_b"]])
    ln1 = ln1 + other_head(ln1)
    wide = [ln1[0], ln1[1], vec["out_b"], vec["ln2_g"], vec["ln2_b"], vec["down_b"]]
    blocks = [v.reshape(n_seq, n_dp, -1) for v in wide + [vec["q_b"], vec["v_b"], vec["up_b"]]]
    sizes = [b.shape[2] for b in blocks]
    small = scatter_small(jnp.concatenate(blocks, axis=2))
    pieces, at = [], 0
    for size in sizes:
        pieces.append(small[at:at + size])
        at += size

    return (
        jnp.stack(outputs),
        jnp.stack(tokens_grads),
        pieces[0],
        pieces[1],
        qkv_grad,
        jnp.stack([pieces[6], pieces[7]]),
        out_grad.T,
        pieces[2],
        pieces[3],
        pieces[4],
        up_grad,
        pieces[8],
        down_grad.T,
        pieces[5],
    )


def solution(mesh):
    in_specs = (
        P("dp", "seq", None),
        P("dp", "seq"),
        P(),
        P(),
        P(None, None, "head"),
        P(None, "head"),
        P("head", None),
        P(),
        P(),
        P(),
        P(None, "head"),
        P("head"),
        P("head", None),
        P(),
        P("dp", "seq", None),
    )
    out_specs = (
        P("dp", "seq", None),
        P("dp", "seq", None),
        P(("seq", "dp")),
        P(("seq", "dp")),
        P(("seq", "dp"), None, "head"),
        P(None, ("head", "seq", "dp")),
        P("head", ("seq", "dp")),
        P(("seq", "dp")),
        P(("seq", "dp")),
        P(("seq", "dp")),
        P(("seq", "dp"), "head"),
        P(("head", "seq", "dp")),
        P("head", ("seq", "dp")),
        P(("seq", "dp")),
    )
    return jax.shard_map(shards, mesh=mesh, in_specs=in_specs, out_specs=out_specs, check_vma=False)
```

```python
import functools

import jax
import jax.numpy as jnp
from jax import lax
from jax.experimental import pallas as pl
from jax.experimental.pallas import tpu as pltpu
from jax.sharding import PartitionSpec as P

HEAD_DIM = 64
LANES = 128
EPSILON = 1e-05
MASKED = -1e30
F32 = jnp.float32
LOW = jnp.bfloat16
NN = (((1,), (0,)), ((), ()))
NT = (((1,), (1,)), ((), ()))
TN = (((0,), (0,)), ((), ()))
VMEM_LIMIT = 60 * 2**20


def dot(a, b, dims=NN):
    return lax.dot_general(a, b, dims, preferred_element_type=F32)


def axis_size(name):
    return lax.axis_size(name)


def swap(value, axis, mask):
    return lax.ppermute(value, axis, [(i, i ^ mask) for i in range(axis_size(axis))])


def bits_of(count):
    return [1 << b for b in range(count.bit_length() - 1)]


def layer_norm(inputs, gain, shift):
    center = jnp.mean(inputs, axis=-1, keepdims=True)
    centred = inputs - center
    spread = jnp.mean(centred * centred, axis=-1, keepdims=True)
    inverse = lax.rsqrt(spread + EPSILON)
    normed = centred * inverse
    return (normed * gain + shift, normed, inverse)


def norm_backward(upstream, normed, inverse, gain):
    scaled = upstream * gain
    centred = scaled - jnp.mean(scaled, axis=-1, keepdims=True)
    return inverse * (centred - normed * jnp.mean(scaled * normed, axis=-1, keepdims=True))


def gelu_pair(v):
    c = 0.7978845608028654
    square = v * v
    t = jnp.tanh(c * v * (1.0 + 0.044715 * square))
    half = 0.5 * (1.0 + t)
    return v * half, half + (0.5 * c) * v * (1.0 - t * t) * (1.0 + 3.0 * 0.044715 * square)


def half_lanes(shape, head):
    lane = lax.broadcasted_iota(jnp.int32, shape, 1)
    return (lane < HEAD_DIM) if head == 0 else (lane >= HEAD_DIM)


def attend_kernel(n, q_ref, seg_ref, segk_ref, *refs):
    kv_refs = refs[:n]
    w_ref, attn_ref, low_ref, inv_ref = refs[n:]
    q = q_ref[...] * jnp.asarray(0.125, LOW)
    seg_q = seg_ref[0:1, :]
    for head in range(2):
        qh = jnp.where(half_lanes(q.shape, head), q, jnp.zeros_like(q))
        parts, top = [], None
        for m in range(n):
            s = dot(kv_refs[m][0], qh, NT)
            s = jnp.where(segk_ref[m] == seg_q, s, MASKED)
            peak = jnp.max(s, axis=0, keepdims=True)
            top = peak if top is None else jnp.maximum(top, peak)
            parts.append(s)
        total, mixed = 0.0, 0.0
        for m in range(n):
            w = jnp.exp(parts[m] - top)
            total = total + jnp.sum(w, axis=0, keepdims=True)
            wl = w.astype(LOW)
            w_ref[head, m] = wl
            vt = kv_refs[m][1].T[head * HEAD_DIM:(head + 1) * HEAD_DIM, :]
            mixed = mixed + dot(vt, wl)
        inverse = 1.0 / total
        inv_ref[0, head:head + 1, :] = inverse
        attn_ref[head * HEAD_DIM:(head + 1) * HEAD_DIM, :] = mixed * inverse
    low_ref[...] = attn_ref[...].T.astype(LOW)


def attend(q, seg_rows, seg_cols, kvs):
    n, (rows, width) = len(kvs), q.shape
    pairs = width // LANES
    step = lambda p: (0, p)
    kv_spec = pl.BlockSpec((2, rows, LANES), lambda p: (0, 0, p))
    return pl.pallas_call(
        functools.partial(attend_kernel, n),
        grid=(pairs,),
        in_specs=[
            pl.BlockSpec((rows, LANES), step),
            pl.BlockSpec((8, rows), lambda p: (0, 0)),
            pl.BlockSpec((n, rows, 1), lambda p: (0, 0, 0)),
        ]
        + [kv_spec] * n,
        out_specs=[
            pl.BlockSpec((2, n, rows, rows), lambda p: (p, 0, 0, 0)),
            pl.BlockSpec((LANES, rows), lambda p: (p, 0)),
            pl.BlockSpec((rows, LANES), step),
            pl.BlockSpec((1, 2, rows), lambda p: (p, 0, 0)),
        ],
        out_shape=[
            jax.ShapeDtypeStruct((2 * pairs, n, rows, rows), LOW),
            jax.ShapeDtypeStruct((width, rows), F32),
            jax.ShapeDtypeStruct((rows, width), LOW),
            jax.ShapeDtypeStruct((pairs, 2, rows), F32),
        ],
        compiler_params=pltpu.CompilerParams(vmem_limit_bytes=VMEM_LIMIT),
        cost_estimate=pl.CostEstimate(
            flops=2 * pairs * n * rows * rows * 256 * 4,
            bytes_accessed=2 * pairs * n * rows * rows * 2,
            transcendentals=2 * pairs * n * rows * rows,
        ),
    )(q, seg_rows, seg_cols, *kvs)


def attend_back_kernel(n, q_ref, g_ref, attn_ref, inv_ref, w_ref, *refs):
    kv_refs = refs[:n]
    dq_ref = refs[n]
    dkv_refs = refs[n + 1:2 * n + 1]
    dqt_ref = refs[2 * n + 1]
    q = q_ref[...]
    gt = g_ref[...].astype(F32).T
    qs, gs, gts, deltas = [], [], [], []
    for head in range(2):
        rows_h = slice(head * HEAD_DIM, (head + 1) * HEAD_DIM)
        part = (gt[rows_h] * inv_ref[0, head:head + 1, :]).astype(LOW)
        deltas.append(jnp.sum(part.astype(F32) * attn_ref[rows_h, :], axis=0, keepdims=True))
        zeros = jnp.zeros_like(part)
        full = jnp.concatenate([part, zeros] if head == 0 else [zeros, part], axis=0)
        gts.append(full)
        gs.append(full.T)
        qs.append(jnp.where(half_lanes(q.shape, head), q, jnp.zeros_like(q)))
    dqt = [0.0, 0.0]
    for m in range(n):
        kt = kv_refs[m][0].T
        v = kv_refs[m][1]
        dk = dv = 0.0
        for head in range(2):
            w = w_ref[head, m]
            ds = (w.astype(F32) * (dot(v, gts[head]) - deltas[head])).astype(LOW)
            dk = dk + dot(ds, qs[head])
            dv = dv + dot(w, gs[head])
            dqt[head] = dqt[head] + dot(kt[head * HEAD_DIM:(head + 1) * HEAD_DIM, :], ds)
        dkv_refs[m][0] = (dk * 0.125).astype(LOW)
        dkv_refs[m][1] = dv.astype(LOW)
    dqt_ref[0:HEAD_DIM, :] = dqt[0]
    dqt_ref[HEAD_DIM:LANES, :] = dqt[1]
    dq_ref[...] = (dqt_ref[...].T * 0.125).astype(LOW)


def attend_back(q, g, attn, inverse, weights, kvs):
    n, (rows, width) = len(kvs), q.shape
    pairs = width // LANES
    step = lambda p: (0, p)
    kv_spec = pl.BlockSpec((2, rows, LANES), lambda p: (0, 0, p))
    out = pl.pallas_call(
        functools.partial(attend_back_kernel, n),
        grid=(pairs,),
        in_specs=[
            pl.BlockSpec((rows, LANES), step),
            pl.BlockSpec((rows, LANES), step),
            pl.BlockSpec((LANES, rows), lambda p: (p, 0)),
            pl.BlockSpec((1, 2, rows), lambda p: (p, 0, 0)),
            pl.BlockSpec((2, n, rows, rows), lambda p: (p, 0, 0, 0)),
        ]
        + [kv_spec] * n,
        out_specs=[pl.BlockSpec((rows, LANES), step)] + [kv_spec] * n,
        out_shape=[jax.ShapeDtypeStruct((rows, width), LOW)]
        + [jax.ShapeDtypeStruct((2, rows, width), LOW)] * n,
        scratch_shapes=[pltpu.VMEM((LANES, rows), F32)],
        compiler_params=pltpu.CompilerParams(vmem_limit_bytes=VMEM_LIMIT),
        cost_estimate=pl.CostEstimate(
            flops=2 * pairs * n * rows * rows * 256 * 8,
            bytes_accessed=2 * pairs * n * rows * rows * 2,
            transcendentals=0,
        ),
    )(q, g, attn, inverse, weights, *kvs)
    return out[0], out[1:]


def gather_seq(block):
    bits = bits_of(axis_size("seq"))
    blocks = {0: block}
    for bit in reversed(bits):
        for m in list(blocks):
            blocks[m | bit] = swap(blocks[m], "seq", bit)
    return [blocks[m] for m in range(len(blocks))]


def scatter_seq(parts):
    parts = dict(enumerate(parts))
    for bit in bits_of(axis_size("seq")):
        for m in [m for m in sorted(parts, reverse=True) if m & bit]:
            got = swap(parts.pop(m).astype(LOW), "seq", bit)
            parts[m ^ bit] = parts[m ^ bit].astype(F32) + got.astype(F32)
    return parts[0].astype(F32)


def scatter_line(term):
    n = axis_size("dp")
    me = lax.axis_index("dp")
    rows = term.shape[0] // n
    block = lambda i: lax.dynamic_slice_in_dim(term, jnp.clip(i, 0, n - 1) * rows, rows, 0)
    up = down = None
    for k in range(n - 1, 0, -1):
        send_up = block(me + k) if up is None else block(me + k) + up
        send_down = block(me - k) if down is None else block(me - k) + down
        up = lax.ppermute(
            send_up.astype(LOW), "dp", [(i, i + 1) for i in range(n) if i + k < n]
        ).astype(F32)
        down = lax.ppermute(
            send_down.astype(LOW), "dp", [(i, i - 1) for i in range(n) if i - k >= 0]
        ).astype(F32)
    out = block(me)
    return out if n == 1 else out + up + down


def relative_columns(rows):
    n = axis_size("seq")
    me = lax.axis_index("seq")
    width = rows.shape[1] // n
    return [lax.dynamic_slice_in_dim(rows, (me ^ m) * width, width, 1) for m in range(n)]


def weight_grad(left, right):
    return scatter_line(scatter_seq([dot(part, right, TN) for part in left]))


def scatter_small(blocks):
    for axis in ("seq", "dp"):
        n = axis_size(axis)
        me = lax.axis_index(axis)
        bits = bits_of(n)
        rest = blocks.shape[1:]
        for bit in reversed(bits):
            low, high = blocks[:bit], blocks[bit:]
            mine = (me & bit) != 0
            send = jnp.where(mine, low, high)
            blocks = jnp.where(mine, high, low) + swap(send, axis, bit)
        blocks = blocks.reshape(rest)
    return blocks


def other_head(value):
    return swap(value, "head", 1)


def head_sum(value):
    value = value.astype(LOW)
    return value.astype(F32) + other_head(value).astype(F32)


def by_head(mine, other, axis):
    first = lax.axis_index("head") == 0
    return jnp.where(
        first,
        jnp.concatenate([mine, other], axis),
        jnp.concatenate([other, mine], axis),
    )


MESH = pl.DeviceIdType.MESH
CHUNK = 32
WIDE = 512


def loop(count, body, unroll=1, start=0):
    def step(i, carry):
        body(i)
        return carry

    lax.fori_loop(start, start + count, step, 0, unroll=unroll)


def span(i, size):
    return pl.ds(pl.multiple_of(i * size, size), size)


def fold(value):
    return jnp.sum(value.reshape(value.shape[0] // 8, 8, value.shape[1]), axis=0)


class Copy:
    def __init__(self, copy, remote):
        self.copy, self.remote = copy, remote
        self.sent = self.got = False

    def wait_recv(self):
        if not self.got:
            self.got = True
            if self.remote:
                self.copy.wait_recv()
            else:
                self.copy.wait()

    def wait_send(self):
        if self.remote and not self.sent:
            self.copy.wait_send()
        self.sent = True

    def wait(self):
        self.wait_send()
        self.wait_recv()


class Copies:
    def __init__(self, send, recv, local):
        self.sems, self.all = (send, recv, local), []
        self.n_remote = self.n_local = 0

    def start(self, src, dst, device):
        copy = pltpu.make_async_remote_copy(
            src_ref=src,
            dst_ref=dst,
            send_sem=self.sems[0].at[self.n_remote],
            recv_sem=self.sems[1].at[self.n_remote],
            device_id=device,
            device_id_type=MESH,
        )
        self.n_remote += 1
        return self.begin(copy, True)

    def load(self, src, dst):
        copy = pltpu.make_async_copy(src, dst, self.sems[2].at[self.n_local])
        self.n_local += 1
        return self.begin(copy, False)

    def begin(self, copy, remote):
        copy.start()
        self.all.append(Copy(copy, remote))
        return self.all[-1]

    def finish(self):
        for copy in self.all:
            copy.wait()


N_COPIES = 128
N_LOCAL = 24


def layer_kernel(n_dp, *refs):
    (
        tok_h, seg_in, g1, b1, wqkv_h, qvb, outw_h, outb, g2, b2, up_h, upb, down_h, downb, cot_h,
        out_h, tg_h, downg_h, upg_h, outg_h, qkvg_h, vec_o,
        tok, cot, wqkv, outw, up, down, q, kv, attn_t, attn, mid, lnb, act, gh,
        first_t, second_t, cot_t, gb_t, g_attn, gs, ffn, stat, st,
        gs_r, ffn_r, gf_r, dkv_r, q_far, g_far, st_far, act_r, gh_r, first_r, second_r, cot_r, gb_r, heads_r, dqkv_r,
        xr, zr, xz, zz,
        segs, segk, vec, qvacc, upacc, ln1_r, vs, vr,
        send, recv, local,
    ) = refs
    rows = tok.shape[0] // 2
    width = tok.shape[1]
    heads_w = q.shape[1]
    hidden = act.shape[1]
    pairs = heads_w // LANES
    quarter = width // 4
    block = quarter // n_dp
    s = lax.axis_index("seq")
    h = lax.axis_index("head")
    z = lax.axis_index("dp")
    x, core = s // 2, s % 2
    seq_peer = [None] + [((x ^ (m >> 1)) * 2 + (core ^ (m & 1)), h, z) for m in (1, 2, 3)]
    across = (s, 1 - h, z)
    next_z, far_z = z + 1 - 2 * lax.rem(z, 2), lax.rem(z + 2, 4)
    beside, beyond = (s, h, next_z), (s, h, far_z)
    half_w = heads_w // 2
    copies = Copies(send, recv, local)
    load = copies.load

    own_out = pl.ds(pl.multiple_of(h * heads_w, heads_w), heads_w)
    get_tok = load(tok_h, tok)
    get_qkv = load(wqkv_h, wqkv)

    barrier = pltpu.get_barrier_semaphore()
    partners = seq_peer[1:] + [across, beside, beyond]
    for device in partners:
        pl.semaphore_signal(barrier, inc=1, device_id=device, device_id_type=MESH)

    vec[...] = jnp.zeros_like(vec)
    qvacc[...] = jnp.zeros_like(qvacc)
    upacc[...] = jnp.zeros_like(upacc)
    segs[0] = jnp.zeros_like(segs[0])
    segs[0, 0:2, :] = seg_in[...]
    def seq_rows(i):
        return slice(i * rows, (i + 1) * rows)

    def flip(src, i, dst):
        def part(c):
            dst[span(c, 256), seq_rows(i)] = src[:, span(c, 256)].T

        loop(width // 256, part)

    def swap_rows(flipped, target):
        return [
            copies.start(
                flipped.at[pl.ds(pl.multiple_of(c * 2 * quarter + (1 - core) * quarter, quarter), quarter), :],
                target.at[c],
                seq_peer[1],
            )
            for c in range(2)
        ]

    kv_got = [[[None] * 2 for _ in range(4)] for _ in range(2)]
    q_got, q_next = [None] * 2, [None] * 2

    def first_norm(i):
        def norm(c):
            at = pl.ds(pl.multiple_of(i * rows + c * CHUNK, CHUNK), CHUNK)
            v = tok[at, :].astype(F32)
            center = jnp.mean(v, axis=-1, keepdims=True)
            v = v - center
            inverse = lax.rsqrt(jnp.mean(v * v, axis=-1, keepdims=True) + EPSILON)
            stat[0, at, 0:1] = center
            stat[0, at, 1:2] = inverse
            lnb[i, span(c, CHUNK), :] = (v * inverse * g1[...] + b1[...]).astype(LOW)

        loop(rows // CHUNK, norm, 4)

    def keys_values(i):
        k = dot(lnb[i], wqkv[1]).astype(LOW)
        v = (dot(lnb[i], wqkv[2]) + qvb[1:2, :]).astype(LOW)
        for part in range(2):
            cols = slice(part * half_w, (part + 1) * half_w)
            kv[i, 0, part, :, 0:half_w] = k[:, cols]
            kv[i, 0, part, :, half_w:heads_w] = v[:, cols]

    def send_keys(i):
        for part in range(2):
            kv_got[i][2][part] = copies.start(kv.at[i, 0, part], kv.at[i, 2, part], seq_peer[2])
        for part in range(2):
            kv_got[i][1][part] = copies.start(kv.at[i, 0, part], kv.at[i, 1, part], seq_peer[1])

    def queries(i):
        q[seq_rows(i), :] = (dot(lnb[i], wqkv[0]) + qvb[0:1, :]).astype(LOW)
        q_got[i] = copies.start(q.at[seq_rows(i), :], q_far.at[i, 0], seq_peer[2])
        flip(lnb.at[i], i, first_t)

    seg_got = [None] * 4

    def meet():
        pl.semaphore_wait(barrier, len(partners))
        for m in (1, 2, 3):
            seg_got[m] = copies.start(segs.at[0], segs.at[m], seq_peer[m])

    def key_lanes(p):
        lane = lax.rem(p, 2) * LANES
        return p // 2, pl.ds(pl.multiple_of(lane, LANES), LANES), pl.ds(pl.multiple_of(half_w + lane, LANES), LANES)

    def twice(row):
        return jnp.concatenate([row, row], axis=1)

    def both(stats, k):
        return jnp.concatenate([stats[k:k + 1, :], stats[k + 1:k + 2, :]], axis=1)

    def cols_of(head):
        return slice(head * rows, (head + 1) * rows)

    def heads_of(pair_value, scale=None):
        if scale is not None:
            pair_value = pair_value * jnp.asarray(scale, LOW)
        zeros = jnp.zeros_like(pair_value)
        return [jnp.where(half_lanes(pair_value.shape, head), pair_value, zeros) for head in range(2)]

    def attend_blocks(i, blocks, begin, end, start, stop):
        seg_q = twice(segs[0, i:i + 1, :].astype(F32))

        def pair(p):
            lanes = span(p, LANES)
            part, k_lanes, v_lanes = key_lanes(p)
            qs = jnp.concatenate(heads_of(q[seq_rows(i), lanes], 0.125), axis=0)
            old = top = None if begin else both(st[i, p], 0)
            scores = []
            for m in blocks:
                score = dot(kv[i, m, part, :, k_lanes], qs, NT)
                score = jnp.where(segk[m, :, i:i + 1] == seg_q, score, MASKED)
                peak = jnp.max(score, axis=0, keepdims=True)
                top = peak if top is None else jnp.maximum(top, peak)
                scores.append(score)
            total, mixed = 0.0, [0.0, 0.0]
            for m, score in zip(blocks, scores):
                w = jnp.exp(score - top)
                total = total + jnp.sum(w, axis=0, keepdims=True)
                low = w.astype(LOW)
                vt = kv[i, m, part, :, v_lanes].T
                for head in range(2):
                    mixed[head] = mixed[head] + dot(vt[head * HEAD_DIM:(head + 1) * HEAD_DIM, :], low[:, cols_of(head)])
            if not begin:
                scale = jnp.exp(old - top)
                total = total + scale * both(st[i, p], 2)
            if end:
                inverse, lse = 1.0 / total, top + jnp.log(total)
            for head in range(2):
                at = pl.ds(pl.multiple_of(p * LANES + head * HEAD_DIM, HEAD_DIM), HEAD_DIM)
                value = mixed[head]
                if not begin:
                    value = value + scale[:, cols_of(head)] * attn_t[i, at, :]
                if end:
                    value = value * inverse[:, cols_of(head)]
                    st[i, p, 4 + head:5 + head, :] = lse[:, cols_of(head)]
                else:
                    st[i, p, head:head + 1, :] = top[:, cols_of(head)]
                    st[i, p, 2 + head:3 + head, :] = total[:, cols_of(head)]
                attn_t[i, at, :] = value
            if end:
                to = pl.ds(pl.multiple_of(h * heads_w + p * LANES, LANES), LANES)
                attn[seq_rows(i), to] = attn_t[i, lanes, :].T.astype(LOW)

        lax.fori_loop(start, stop, lambda p, c: (pair(p), c)[1], 0)

    def seg_columns(m):
        segk[m] = segs[m].astype(F32).T

    own_heads = pl.ds(pl.multiple_of(h * heads_w, heads_w), heads_w)
    attn_got = [None, None]

    def forward_keys(i, part):
        kv_got[i][2][part].wait_recv()
        kv_got[i][3][part] = copies.start(kv.at[i, 2, part], kv.at[i, 3, part], seq_peer[1])

    def forward_queries(i):
        q_got[i].wait_recv()
        q_next[i] = copies.start(q_far.at[i, 0], q_far.at[i, 1], seq_peer[1])

    def attend_far(i, part):
        kv_got[i][3][part].wait_recv()
        attend_blocks(i, (2, 3), False, True, part * pairs // 2, (part + 1) * pairs // 2)

    def send_heads(i):
        mine = attn.at[seq_rows(i), own_heads]
        attn_got[i] = copies.start(mine, mine, across)
        heads_sent[i] = copies.start(mine, heads_r.at[seq_rows(i), :], seq_peer[1])

    heads_sent = [None, None]

    def middle(i):
        attn_got[i].wait_recv()

        def tile(j):
            at = span(j, WIDE)
            mid[seq_rows(i), at] = (
                dot(attn[seq_rows(i), :], outw[:, at])
                + tok[seq_rows(i), at].astype(F32)
                + outb[:, at]
            )

        loop(width // WIDE, tile)

        def norm(c):
            at = pl.ds(pl.multiple_of(i * rows + c * CHUNK, CHUNK), CHUNK)
            v = mid[at, :]
            center = jnp.mean(v, axis=-1, keepdims=True)
            v = v - center
            inverse = lax.rsqrt(jnp.mean(v * v, axis=-1, keepdims=True) + EPSILON)
            stat[1, at, 0:1] = center
            stat[1, at, 1:2] = inverse
            lnb[i, span(c, CHUNK), :] = (v * inverse * g2[...] + b2[...]).astype(LOW)

        loop(rows // CHUNK, norm, 4)

    gs_got, ffn_got = [None] * 2, [None] * 2
    act_got, gh_got = [[None] * 2, [None] * 2], [[None] * 2, [None] * 2]

    def cot_down(i):
        def tile(j):
            at = span(j, 2 * WIDE)
            gh[seq_rows(i), at] = dot(cot[seq_rows(i), :], down[at, :], NT).astype(LOW)

        loop(hidden // (2 * WIDE), tile)

    def feed(i, part):
        at_rows = seq_rows(i)

        def tile(j):
            at = span(j, WIDE)
            value, slope = gelu_pair(dot(lnb[i], up[:, at]) + upb[:, at])
            act[at_rows, at] = value.astype(LOW)
            g = (gh[at_rows, at].astype(F32) * slope).astype(LOW)
            gh[at_rows, at] = g
            upacc[:, at] += fold(g.astype(F32))

        tiles_each = hidden // WIDE // 2
        loop(tiles_each, tile, 1, part * tiles_each)
        cols = slice(part * hidden // 2, (part + 1) * hidden // 2)
        act_got[i][part] = copies.start(act.at[at_rows, cols], act_r.at[at_rows, cols], seq_peer[1])
        gh_got[i][part] = copies.start(gh.at[at_rows, cols], gh_r.at[at_rows, cols], seq_peer[1])

    def feed_back(i):
        at_rows = seq_rows(i)

        def back(j):
            gs[at_rows, span(j, WIDE)] = dot(gh[at_rows, :], up[span(j, WIDE), :], NT).astype(LOW)

        loop(width // WIDE, back)
        gs_got[i] = copies.start(gs.at[at_rows, :], gs_r.at[at_rows, :], across)
        flip(lnb.at[i], i, second_t)

    def feed_out(i):
        at_rows = seq_rows(i)

        def tile(j):
            ffn[at_rows, span(j, WIDE)] = dot(act[at_rows, :], down[:, span(j, WIDE)]).astype(LOW)

        loop(width // WIDE, tile)

    def send_feed_out(i):
        ffn_got[i] = copies.start(ffn.at[seq_rows(i), :], ffn_r.at[seq_rows(i), :], across)

    def finish_output(i):
        ffn_got[i].wait()

        def part(c):
            at = pl.ds(pl.multiple_of(i * rows + c * CHUNK, CHUNK), CHUNK)
            both = ffn[at, :].astype(F32) + ffn_r[at, :].astype(F32)
            ffn[at, :] = (mid[at, :] + both + downb[...]).astype(LOW)

        loop(rows // CHUNK, part, 4)
        load(ffn.at[seq_rows(i), :], out_h.at[seq_rows(i), :])

    gb = down.at[2 * rows:4 * rows, :]
    parts_kv = [[down.at[(4 + 2 * i + m) * rows:(5 + 2 * i + m) * rows, :] for m in range(2)] for i in range(2)]
    dqkv = up.at[2 * rows:4 * rows, :]

    def norm2_back(i):
        gs_got[i].wait_recv()

        def part(c):
            at = pl.ds(pl.multiple_of(i * rows + c * CHUNK, CHUNK), CHUNK)
            g = gs[at, :].astype(F32) + gs_r[at, :].astype(F32)
            inverse = stat[1, at, 1:2]
            normed = (mid[at, :] - stat[1, at, 0:1]) * inverse
            vec[3] += fold(g * normed)
            vec[4] += fold(g)
            e = g * g2[...]
            e = e - jnp.mean(e, axis=-1, keepdims=True) - normed * jnp.mean(e * normed, axis=-1, keepdims=True)
            low = (cot[at, :].astype(F32) + inverse * e).astype(LOW)
            gb[at, :] = low
            vec[2] += fold(low.astype(F32))

        loop(rows // CHUNK, part, 4)

        w_rows = pl.ds(pl.multiple_of(h * heads_w, heads_w), heads_w)
        g_attn[i] = dot(gb[seq_rows(i), :], outw[w_rows, :], NT).astype(LOW)

        def delta(p):
            g = g_attn[i, :, span(p, LANES)].astype(F32).T
            each = g * attn_t[i, span(p, LANES), :]
            for head in range(2):
                part = each[head * HEAD_DIM:(head + 1) * HEAD_DIM, :]
                st[i, p, 6 + head:7 + head, :] = jnp.sum(part, axis=0, keepdims=True)

        loop(pairs, delta)
        g_got[i] = [
            copies.start(g_attn.at[i], g_far.at[i, 0], seq_peer[2]),
            copies.start(st.at[i], st_far.at[i, 0], seq_peer[2]),
        ]

    g_got, g_next = [None] * 2, [None] * 2

    def forward_grads(i):
        for copy in g_got[i]:
            copy.wait_recv()
        g_next[i] = [
            copies.start(g_far.at[i, 0], g_far.at[i, 1], seq_peer[1]),
            copies.start(st_far.at[i, 0], st_far.at[i, 1], seq_peer[1]),
        ]

    def backward_terms(allowed, k, v, q_scaled, g, lse, delta):
        probs = jnp.exp(jnp.where(allowed, dot(k, q_scaled, NT) - lse, MASKED))
        return probs.astype(LOW), (probs * (dot(v, g, NT) - delta)).astype(LOW)

    def back_own(i):
        seg_q = twice(segs[0, i:i + 1, :].astype(F32))

        def pair(p):
            lanes = span(p, LANES)
            v_lanes = pl.ds(pl.multiple_of(heads_w + p * LANES, LANES), LANES)
            part, k_in, v_in = key_lanes(p)
            qs = jnp.concatenate(heads_of(q[seq_rows(i), lanes]), axis=0)
            q_scaled = qs * jnp.asarray(0.125, LOW)
            g = jnp.concatenate(heads_of(g_attn[i, :, lanes]), axis=0)
            lse, delta = both(st[i, p], 4), both(st[i, p], 6)
            dqt = [0.0, 0.0]
            for m in range(4):
                k = kv[i, m, part, :, k_in]
                kt = k.T
                v = kv[i, m, part, :, v_in]
                probs, ds = backward_terms(segk[m, :, i:i + 1] == seg_q, k, v, q_scaled, g, lse, delta)
                if m < 2:
                    parts_kv[i][m][:, lanes] = (dot(ds, qs) * 0.125).astype(LOW)
                    parts_kv[i][m][:, v_lanes] = dot(probs, g).astype(LOW)
                for head in range(2):
                    dqt[head] = dqt[head] + dot(kt[head * HEAD_DIM:(head + 1) * HEAD_DIM, :], ds[:, cols_of(head)])
            dq = (jnp.concatenate(dqt, axis=0).T * 0.125).astype(LOW)
            dqkv[seq_rows(i), lanes] = dq
            qvacc[:, lanes] += fold(dq.astype(F32))

        loop(pairs, pair)
        near_got[i] = copies.start(parts_kv[i][1], dkv_r.at[i], seq_peer[1])
        at = (seq_rows(i), pl.ds(0, heads_w))
        dq_got[i] = copies.start(dqkv.at[at], dqkv_r.at[at], seq_peer[1])

    def back_far(i):
        q_next[i].wait_recv()
        for copy in g_next[i]:
            copy.wait_recv()
        near_got[i].wait_recv()
        seg_q = [twice(segs[2 + b, i:i + 1, :].astype(F32)) for b in range(2)]
        at_rows = seq_rows(i)

        def pair(p):
            lanes = span(p, LANES)
            v_lanes = pl.ds(pl.multiple_of(heads_w + p * LANES, LANES), LANES)
            part, k_in, v_in = key_lanes(p)
            k = kv[i, 0, part, :, k_in]
            v = kv[i, 0, part, :, v_in]
            dk = dv = 0.0
            for b in range(2):
                qs = jnp.concatenate(heads_of(q_far[i, b, :, lanes]), axis=0)
                q_scaled = qs * jnp.asarray(0.125, LOW)
                g = jnp.concatenate(heads_of(g_far[i, b, :, lanes]), axis=0)
                lse, delta = both(st_far[i, b, p], 4), both(st_far[i, b, p], 6)
                probs, ds = backward_terms(segk[0, :, i:i + 1] == seg_q[b], k, v, q_scaled, g, lse, delta)
                dk = dk + dot(ds, qs)
                dv = dv + dot(probs, g)
            near = lambda to: parts_kv[i][0][:, to].astype(F32) + dkv_r[i, :, to].astype(F32)
            k_at = pl.ds(pl.multiple_of(heads_w + p * LANES, LANES), LANES)
            v_at = pl.ds(pl.multiple_of(2 * heads_w + p * LANES, LANES), LANES)
            dqkv[at_rows, k_at] = (dk * 0.125 + near(lanes)).astype(LOW)
            low = (dv + near(v_lanes)).astype(LOW)
            dqkv[at_rows, v_at] = low
            qvacc[:, k_at] += fold(low.astype(F32))

        loop(pairs, pair)
        at = (at_rows, kv_cols)
        dkv_got[i] = copies.start(dqkv.at[at], dqkv_r.at[at], seq_peer[1])

    near_got, dq_got = [None] * 2, [None] * 2
    kv_cols = pl.ds(heads_w, 2 * heads_w)

    dkv_got, gf_got = [None] * 2, [None] * 2

    def first_back(i):
        gs_got[i].wait_send()

        def tile(j):
            at = span(j, WIDE)
            total = 0.0
            for c in range(3):
                total = total + dot(dqkv[seq_rows(i), c * heads_w:(c + 1) * heads_w], wqkv[c, at, :], NT)
            gs[seq_rows(i), at] = total.astype(LOW)

        loop(width // WIDE, tile)
        def sums(c):
            at = pl.ds(pl.multiple_of(i * rows + c * CHUNK, CHUNK), CHUNK)
            g = gs[at, :].astype(F32)
            normed = (tok[at, :].astype(F32) - stat[0, at, 0:1]) * stat[0, at, 1:2]
            vec[0] += fold(g * normed)
            vec[1] += fold(g)

        loop(rows // CHUNK, sums, 4)

    def send_first_back(i):
        gf_got[i] = copies.start(gs.at[seq_rows(i), :], gf_r.at[seq_rows(i), :], across)

    def norm1_back(i):
        gf_got[i].wait()

        def part(c):
            at = pl.ds(pl.multiple_of(i * rows + c * CHUNK, CHUNK), CHUNK)
            g = gs[at, :].astype(F32) + gf_r[at, :].astype(F32)
            inverse = stat[0, at, 1:2]
            normed = (tok[at, :].astype(F32) - stat[0, at, 0:1]) * inverse
            e = g * g1[...]
            e = e - jnp.mean(e, axis=-1, keepdims=True) - normed * jnp.mean(e * normed, axis=-1, keepdims=True)
            gs[at, :] = (gb[at, :].astype(F32) + inverse * e).astype(LOW)

        loop(rows // CHUNK, part, 4)
        load(gs.at[seq_rows(i), :], tg_h.at[seq_rows(i), :])

    def tiles(piece, chip, body):
        left, left_r, right, right_r, cols = piece
        at_rows = pl.ds(pl.multiple_of(chip * 2 * quarter + core * quarter, quarter), quarter)
        step = min(cols, 2 * WIDE)

        def tile(j):
            at = span(j, step)
            body(at, dot(left[at_rows, :], right[:, at]) + dot(left_r[chip], right_r[:, at]))

        loop(cols // step, tile)

    def block_rows(index):
        return pl.ds(pl.multiple_of(index * block, block), block)

    def send_beside(hold, arrive):
        further = lax.rem(next_z + 2, 4)
        return [
            copies.start(hold.at[block_rows(next_z), :], arrive[0], beside),
            copies.start(hold.at[block_rows(further), :], arrive[1], beside),
        ]

    def send_beyond(hold, arrive):
        at = block_rows(far_z)
        hold[at, :] = (hold[at, :].astype(F32) + arrive[1][...].astype(F32)).astype(LOW)
        return copies.start(hold.at[at, :], arrive[2], beyond)

    def own_block(hold, arrive, at=slice(None)):
        total = hold[block_rows(z), at].astype(F32)
        return total + arrive[0][:, at].astype(F32) + arrive[2][:, at].astype(F32)

    def hand_out(place, target, value):
        size = target.shape[1]
        top, left = place // 2 * block, place % 2 * (width // 2)
        mid[top:top + block, left:left + size] = value(slice(None))
        load(mid.at[top:top + block, left:left + size], target)
        return place + size * 2 // width

    class AcrossFirst:
        def __init__(self, piece, hold, offset, arrivals):
            self.piece, self.hold, self.arrivals = piece, hold, arrivals
            cols = pl.ds(offset, piece[4])
            self.xr = xr.at[:, cols]
            self.zr = [zr.at[d, :, cols] for d in range(3)]

        def prepare(self):
            for copy in self.arrivals():
                copy.wait_recv()

            def keep(at, value):
                self.hold[:, at] = value.astype(LOW)

            tiles(self.piece, 1 - x, keep)

        def across(self):
            self.far = copies.start(self.hold, self.xr, seq_peer[2])

        def beside(self):
            self.far.wait()

            def keep(at, value):
                self.hold[:, at] = (value + self.xr[:, at].astype(F32)).astype(LOW)

            tiles(self.piece, x, keep)
            self.near = send_beside(self.hold, self.zr)

        def beyond(self):
            for copy in self.near:
                copy.wait_recv()
            self.last = send_beyond(self.hold, self.zr)

        def done(self, place, target):
            self.last.wait_recv()
            return hand_out(place, target, lambda at: own_block(self.hold, self.zr, at))

    class AlongFirst:
        def __init__(self, piece, holds, offset, arrivals):
            self.piece, self.holds, self.arrivals = piece, holds, arrivals
            cols = pl.ds(offset, piece[4])
            self.zz = [[zz.at[r, d, :, cols] for d in range(3)] for r in range(2)]
            self.xz = xz.at[:, cols]

        def beside(self):
            for copy in self.arrivals():
                copy.wait_recv()
            self.near = []
            for r in (1, 0):

                def keep(at, value, r=r):
                    self.holds[r][:, at] = value.astype(LOW)

                tiles(self.piece, x ^ r, keep)
                self.near += send_beside(self.holds[r], self.zz[r])

        def beyond(self):
            for copy in self.near:
                copy.wait_recv()
            self.last = [send_beyond(self.holds[r], self.zz[r]) for r in (1, 0)]

        def across(self):
            for copy in self.last:
                copy.wait_recv()
            mine = block_rows(z)
            self.holds[1][mine, :] = own_block(self.holds[1], self.zz[1]).astype(LOW)
            self.far = copies.start(self.holds[1].at[mine, :], self.xz, seq_peer[2])

        def done(self, place, target):
            self.far.wait_recv()

            def value(at):
                return own_block(self.holds[0], self.zz[0], at) + self.xz[:, at].astype(F32)

            return hand_out(place, target, value)

    attn_own = attn.at[:, own_heads]
    q_cols, k_cols, v_cols = (slice(c * heads_w, (c + 1) * heads_w) for c in range(3))
    flips = {}
    down_piece = lambda at, n: (cot_t, cot_r, act.at[:, at:at + n], act_r.at[:, at:at + n], n)
    up_piece = lambda at, n: (second_t, second_r, gh.at[:, at:at + n], gh_r.at[:, at:at + n], n)
    proj_piece = lambda at: (first_t, first_r, dqkv.at[:, at], dqkv_r.at[:, at], heads_w)
    quarter_h = hidden // 4
    halves_of = lambda got, at: [got[i][at // (2 * quarter_h)] for i in range(2)]
    from_cot = lambda at: lambda: flips["cot"] + halves_of(act_got, at)
    from_second = lambda at: lambda: flips["second"] + halves_of(gh_got, at)
    spans = [(0, 2 * quarter_h), (2 * quarter_h, quarter_h), (3 * quarter_h, quarter_h)]
    downs = [
        AcrossFirst(down_piece(at, n), lnb.at[0] if k == 0 else up.at[0:rows, at:at + n], at, from_cot(at))
        for k, (at, n) in enumerate(spans)
    ]
    ups = [
        AlongFirst(
            up_piece(at, n),
            [up.at[rows:2 * rows, at:at + n], up.at[0:rows, 0:n] if k == 0 else lnb.at[1, :, 0:n]],
            at,
            from_second(at),
        )
        for k, (at, n) in enumerate(spans[:2])
    ]
    up_last = AcrossFirst(
        up_piece(3 * quarter_h, quarter_h), up.at[rows:2 * rows, 3 * quarter_h:hidden], hidden, from_second(3 * quarter_h)
    )
    base = hidden + quarter_h
    proj_out = AcrossFirst(
        (gb_t, gb_r, attn_own, heads_r, heads_w),
        down.at[0:rows, 0:heads_w],
        base,
        lambda: flips["gb"] + heads_sent,
    )
    proj_q = AcrossFirst(
        proj_piece(q_cols),
        down.at[0:rows, heads_w:2 * heads_w],
        base + heads_w,
        lambda: flips["first"] + dq_got,
    )
    proj_k, proj_v = (
        AcrossFirst(
            proj_piece(cols),
            down.at[rows:2 * rows, c * heads_w:(c + 1) * heads_w],
            base + (2 + c) * heads_w,
            lambda: flips["first"] + dkv_got,
        )
        for c, cols in enumerate((k_cols, v_cols))
    )

    def share_out():
        half = heads_w // 2
        get_out.wait()
        mine = pl.ds(pl.multiple_of(h * heads_w + core * half, half), half)
        return copies.start(outw.at[mine, :], outw.at[mine, :], across)

    def forward_out():
        out_got.wait_recv()
        half = heads_w // 2
        theirs = pl.ds(pl.multiple_of((1 - h) * heads_w + core * half, half), half)
        return copies.start(outw.at[theirs, :], outw.at[theirs, :], seq_peer[1])

    def scenes():
        for m in (1, 2, 3):
            seg_got[m].wait_recv()
        for m in range(4):
            seg_columns(m)

    def attend_near(i):
        for copy in kv_got[i][1]:
            copy.wait_recv()
        attend_blocks(i, (0, 1), True, False, 0, pairs)

    def prepare_cot():
        get_cot.wait()

        def part(c):
            vec[5] += fold(cot[span(c, CHUNK), :].astype(F32))

        loop(2 * rows // CHUNK, part, 4)
        for i in range(2):
            flip(cot.at[seq_rows(i), :], i, cot_t)
        flips["cot"] = swap_rows(cot_t, cot_r)

    def flip_branch():
        for i in range(2):
            flip(gb.at[seq_rows(i), :], i, gb_t)
        flips["gb"] = swap_rows(gb_t, gb_r)

    def vectors():
        ln1_got.wait_recv()
        lines = [jnp.sum(vec[k] + ln1_r[k], axis=0, keepdims=True) for k in range(2)]
        lines += [jnp.sum(vec[k], axis=0, keepdims=True) for k in range(2, 6)]
        lines += [jnp.sum(qvacc[...], axis=0, keepdims=True)]
        sums = jnp.sum(upacc[...], axis=0, keepdims=True)
        lines += [sums[:, c * width:(c + 1) * width] for c in range(hidden // width)]
        lines += [jnp.zeros((16 - len(lines), width), F32)]
        vs[0] = jnp.concatenate(lines, axis=0)
        return copies.start(vs.at[0], vr.at[0], seq_peer[1])

    def vectors_on(k, copy, device):
        copy.wait_recv()
        vs[k] = vs[k - 1] + vr[k - 1]
        return copies.start(vs.at[k], vr.at[k], device)

    def vectors_done():
        vec_4.wait_recv()
        vec_o[...] = vs[3] + vr[3]

    get_tok.wait()
    first_norm(0)
    get_qkv.wait()
    keys_values(0)
    meet()
    send_keys(0)
    get_out, get_cot = load(outw_h, outw.at[own_out, :]), load(cot_h, cot)
    get_down, get_up = load(down_h, down), load(up_h, up)
    first_norm(1)
    keys_values(1)
    send_keys(1)
    queries(0)
    queries(1)
    flips["first"] = swap_rows(first_t, first_r)
    out_got = share_out()
    scenes()
    attend_near(0)
    attend_near(1)
    forward_keys(0, 0)
    prepare_cot()
    forward_keys(0, 1)
    attend_far(0, 0)
    attend_far(0, 1)
    send_heads(0)
    out_near = forward_out()
    get_down.wait()
    cot_down(0)
    forward_keys(1, 0)
    cot_down(1)
    attend_far(1, 0)
    forward_keys(1, 1)
    attend_far(1, 1)
    send_heads(1)
    out_near.wait_recv()
    get_up.wait()
    middle(0)
    feed(0, 0)
    feed(0, 1)
    feed_back(0)
    middle(1)
    feed(1, 0)
    feed(1, 1)
    downs[0].prepare()
    downs[0].across()
    feed_back(1)
    flips["second"] = swap_rows(second_t, second_r)
    ups[0].beside()
    ups[1].beside()
    feed_out(0)
    send_feed_out(0)
    feed_out(1)
    forward_queries(0)
    forward_queries(1)
    norm2_back(0)
    downs[1].prepare()
    downs[1].across()
    back_own(0)
    norm2_back(1)
    downs[0].beside()
    forward_grads(0)
    downs[2].prepare()
    downs[2].across()
    flip_branch()
    ups[0].beyond()
    ups[1].beyond()
    back_far(0)
    first_back(0)
    send_first_back(0)
    proj_out.prepare()
    proj_out.across()
    up_last.prepare()
    up_last.across()
    back_own(1)
    forward_grads(1)
    downs[0].beyond()
    downs[1].beside()
    downs[2].beside()
    back_far(1)
    first_back(1)
    ln1_got = copies.start(vec.at[0:2], ln1_r, across)
    send_first_back(1)
    send_feed_out(1)
    proj_q.prepare()
    proj_q.across()
    proj_k.prepare()
    proj_k.across()
    proj_v.prepare()
    proj_v.across()
    downs[1].beyond()
    downs[2].beyond()
    ups[0].across()
    ups[1].across()
    proj_out.beside()
    norm1_back(0)
    finish_output(0)
    vec_1 = vectors()
    up_last.beside()
    proj_out.beyond()
    vec_2 = vectors_on(1, vec_1, seq_peer[2])
    proj_q.beside()
    up_last.beyond()
    norm1_back(1)
    proj_k.beside()
    proj_q.beyond()
    proj_v.beside()
    proj_k.beyond()
    vec_3 = vectors_on(2, vec_2, beside)
    finish_output(1)
    proj_v.beyond()
    vec_4 = vectors_on(3, vec_3, beyond)
    place = 0
    for group, (at, n) in zip(downs, spans): place = group.done(place, downg_h.at[:, at:at + n])
    for group, (at, n) in zip(ups + [up_last], spans): place = group.done(place, upg_h.at[:, at:at + n])
    place = proj_out.done(place, outg_h)
    place = proj_q.done(place, qkvg_h.at[0])
    place = proj_k.done(place, qkvg_h.at[1])
    place = proj_v.done(place, qkvg_h.at[2])
    vectors_done()
    copies.finish()


def one_kernel(args):
    (
        tokens, segment_ids, ln1_gain, ln1_bias, qkv_weight, qv_bias, out_weight, out_bias,
        ln2_gain, ln2_bias, up_weight, up_bias, down_weight, down_bias, out_cotangent,
    ) = args
    count, rows, width = tokens.shape
    heads_w, hidden = qkv_weight.shape[2], up_weight.shape[1]
    n_dp = axis_size("dp")
    block = width // (4 * n_dp)
    total = count * rows
    grads = hidden + hidden // 4 + 4 * heads_w
    line = lambda v: v.reshape(1, -1)
    low = lambda *shape: pltpu.VMEM(shape, LOW)
    full = lambda *shape: pltpu.VMEM(shape, F32)
    shape = jax.ShapeDtypeStruct
    vmem, anywhere = pl.BlockSpec(memory_space=pltpu.VMEM), pl.BlockSpec(memory_space=pl.ANY)
    return pl.pallas_call(
        functools.partial(layer_kernel, n_dp),
        in_specs=[anywhere, vmem, vmem, vmem, anywhere, vmem, anywhere, vmem, vmem, vmem, anywhere, vmem, anywhere, vmem, anywhere],
        out_specs=[anywhere] * 6 + [vmem],
        out_shape=[
            shape((total, width), LOW),
            shape((total, width), LOW),
            shape((block, hidden), F32),
            shape((block, hidden), F32),
            shape((block, heads_w), F32),
            shape((3, block, heads_w), F32),
            shape((16, width), F32),
        ],
        scratch_shapes=[
            low(total, width), low(total, width), low(3, width, heads_w), low(2 * heads_w, width),
            low(width, hidden), low(hidden, width), low(total, heads_w), low(2, 4, 2, rows, heads_w),
            full(2, heads_w, rows), low(total, width), full(total, width), low(2, rows, width),
            low(total, hidden), low(total, hidden),
            low(width, total), low(width, total), low(width, total), low(width, total),
            low(2, rows, heads_w), low(total, width), low(total, width),
            full(2, total, 2), full(2, heads_w // LANES, 8, rows),
            low(total, width), low(total, width), low(total, width), low(2, rows, 2 * heads_w),
            low(2, 2, rows, heads_w), low(2, 2, rows, heads_w), full(2, 2, heads_w // LANES, 8, rows),
            low(total, hidden), low(total, hidden),
            low(2, width // 4, total), low(2, width // 4, total), low(2, width // 4, total), low(2, width // 4, total),
            low(total, heads_w), low(total, 3 * heads_w), low(width // 4, grads), low(3, block, grads),
            low(block, 3 * hidden // 4), low(2, 3, block, 3 * hidden // 4),
            pltpu.VMEM((4, 8, rows), jnp.int32), full(4, rows, 8), full(6, 8, width), full(8, 2 * heads_w), full(8, hidden),
            full(2, 8, width), full(4, 16, width), full(4, 16, width),
            pltpu.SemaphoreType.DMA((N_COPIES,)), pltpu.SemaphoreType.DMA((N_COPIES,)), pltpu.SemaphoreType.DMA((N_LOCAL,)),
        ],
        compiler_params=pltpu.CompilerParams(
            collective_id=0, has_side_effects=True, vmem_limit_bytes=FAST_VMEM
        ),
    )(
        tokens.reshape(total, width), segment_ids, line(ln1_gain), line(ln1_bias), jnp.transpose(qkv_weight, (1, 0, 2)),
        qv_bias, out_weight, line(out_bias), line(ln2_gain), line(ln2_bias), up_weight, line(up_bias),
        down_weight, line(down_bias), out_cotangent.reshape(total, width),
    )


FAST_VMEM = 62 * 2**20


def fits(args):
    tokens, qkv_weight, up_weight = args[0], args[4], args[10]
    count, rows, width = tokens.shape
    heads_w, hidden = qkv_weight.shape[2], up_weight.shape[1]
    return (
        (axis_size("seq"), axis_size("head"), axis_size("dp")) == (4, 2, 4)
        and (count, rows) == (2, 256)
        and (width, heads_w, hidden) == (1024, 512, 2048)
    )


def split_kernel(parts, index_ref, vec_ref, *refs):
    big = (len(refs) - 1 - 8) // 3
    sources, targets, small = refs[:big], refs[big:2 * big], refs[2 * big:2 * big + 8]
    held, sem = refs[2 * big + 8:-1], refs[-1]
    moves = [pltpu.make_async_copy(a, b, sem.at[0, k]) for k, (a, b) in enumerate(zip(sources, held))]
    for move in moves:
        move.start()
    back = [pltpu.make_async_copy(a, b, sem.at[1, k]) for k, (a, b) in enumerate(zip(held, targets))]
    for move, out in zip(moves, back):
        move.wait()
        out.start()
    at = index_ref[0]
    width = vec_ref.shape[1]

    def piece(row, size):
        shift = lax.rem(width - lax.rem(at * size, width), width)
        return pltpu.roll(vec_ref[row:row + 1, :], shift, 1)[:, :size]

    size = width // parts
    for ref, row in zip(small[:6], (0, 1, 2, 3, 4, 5)):
        ref[...] = piece(row, size)
    half = vec_ref[6:7, :]
    shift = lax.rem(width - at * (size // 2), width)
    turned = pltpu.roll(half, shift, 1)
    small[6][0:1, :] = turned[:, :size // 2]
    small[6][1:2, :] = pltpu.roll(turned, width // 2, 1)[:, :size // 2]
    size = small[7].shape[1]
    low, high = piece(7, size), piece(8, size)
    small[7][...] = jnp.where(at * size < width, low, high)
    for out in back:
        out.wait()


def split(parts, big, vec):
    at = lax.axis_index("seq") * axis_size("dp") + lax.axis_index("dp")
    size = vec.shape[1] // parts
    shape = jax.ShapeDtypeStruct
    smalls = [shape((1, size), F32)] * 6 + [shape((2, size // 2), F32), shape((1, 2 * size), F32)]
    vmem, anywhere = pl.BlockSpec(memory_space=pltpu.VMEM), pl.BlockSpec(memory_space=pl.ANY)
    out = pl.pallas_call(
        functools.partial(split_kernel, parts),
        in_specs=[pl.BlockSpec(memory_space=pltpu.SMEM), vmem] + [anywhere] * len(big),
        out_specs=[anywhere] * len(big) + [vmem] * 8,
        out_shape=[shape(v.shape, v.dtype) for v in big] + smalls,
        scratch_shapes=[pltpu.VMEM(v.shape, v.dtype) for v in big] + [pltpu.SemaphoreType.DMA((2, len(big)))],
        compiler_params=pltpu.CompilerParams(vmem_limit_bytes=FAST_VMEM),
    )(at.astype(jnp.int32).reshape(1), vec, *big)
    return out[:len(big)], out[len(big):]


def fast(*args):
    tokens = args[0]
    *big, vec = one_kernel(args)
    big, small = split(axis_size("seq") * axis_size("dp"), big, vec)
    out, tokens_grad, down_grad, up_grad, out_grad, qkv_grad = big
    flat = [v.reshape(-1) for v in small]
    return (
        out.reshape(tokens.shape),
        tokens_grad.reshape(tokens.shape),
        flat[0],
        flat[1],
        jnp.transpose(qkv_grad, (1, 0, 2)),
        small[6],
        out_grad.T,
        flat[2],
        flat[3],
        flat[4],
        up_grad,
        flat[7],
        down_grad.T,
        flat[5],
    )


def shards(*args):
    return fast(*args) if fits(args) else general(*args)


def general(
    tokens,
    segment_ids,
    ln1_gain,
    ln1_bias,
    qkv_weight,
    qv_bias,
    out_weight,
    out_bias,
    ln2_gain,
    ln2_bias,
    up_weight,
    up_bias,
    down_weight,
    down_bias,
    out_cotangent,
):
    count, rows, features = tokens.shape
    local = qkv_weight.shape[2]
    hidden_local = up_weight.shape[1]
    n_seq, n_dp = axis_size("seq"), axis_size("dp")
    every = range(count)
    wq, wk, wv = (qkv_weight[:, c, :] for c in range(3))

    seg = gather_seq(segment_ids)
    seg_rows = [jnp.broadcast_to(segment_ids[s][None, :], (8, rows)) for s in every]
    seg_cols = [jnp.stack([part[s] for part in seg])[:, :, None] for s in every]

    half = out_weight.shape[0] // 2
    core = lax.axis_index("seq") & 1
    fetched = other_head(lax.dynamic_slice_in_dim(out_weight, core * half, half, 0))
    swapped = swap(fetched, "seq", 1)
    out_other = jnp.where(
        core == 0,
        jnp.concatenate([fetched, swapped], 0),
        jnp.concatenate([swapped, fetched], 0),
    )
    out_full = by_head(out_weight, out_other, 0)

    inputs, first, normed1, inverse1, queries, kvs = [], [], [], [], [], []
    for s in every:
        x = tokens[s].astype(F32)
        pre, normed, inverse = layer_norm(x, ln1_gain, ln1_bias)
        low = pre.astype(LOW)
        k = dot(low, wk).astype(LOW)
        v = (dot(low, wv) + qv_bias[1]).astype(LOW)
        kvs.append(gather_seq(jnp.stack([k, v])))
        queries.append((dot(low, wq) + qv_bias[0]).astype(LOW))
        inputs.append(x)
        first.append(low)
        normed1.append(normed)
        inverse1.append(inverse)

    attended = [attend(queries[s], seg_rows[s], seg_cols[s], kvs[s]) for s in every]

    outputs, second, act, g_hidden, g_middle, heads = [], [], [], [], [], []
    g_queries, g_kv = [], []
    vec = {
        name: 0.0 for name in ("out_b", "ln2_g", "ln2_b", "down_b", "up_b", "q_b", "v_b", "ln1_g", "ln1_b")
    }
    add = lambda name, value: vec.__setitem__(name, vec[name] + jnp.sum(value, axis=0))
    state = []
    for s in every:
        weights, attn_full, attn_low, inv_total = attended[s]
        mixed = by_head(attn_low, other_head(attn_low), 1)
        middle = inputs[s] + dot(mixed, out_full) + out_bias
        pre, normed2, inverse2 = layer_norm(middle, ln2_gain, ln2_bias)
        low = pre.astype(LOW)
        hidden = dot(low, up_weight) + up_bias
        activated, slope = gelu_pair(hidden)
        act_low = activated.astype(LOW)
        cot = out_cotangent[s]
        gh = (dot(cot, down_weight, NT) * slope).astype(LOW)
        g_second = head_sum(dot(gh, up_weight, NT))
        mlp = head_sum(dot(act_low, down_weight))
        outputs.append((middle + mlp + down_bias).astype(LOW))
        second.append(low)
        act.append(act_low)
        g_hidden.append(gh)
        heads.append(attn_low)
        state.append((normed2, inverse2, g_second))
        add("down_b", cot.astype(F32))
        add("up_b", gh.astype(F32))

    g_branch, g_first_parts = [], []
    for s in every:
        normed2, inverse2, g_second = state[s]
        weights, attn_full, attn_low, inv_total = attended[s]
        add("ln2_g", g_second * normed2)
        add("ln2_b", g_second)
        gm = out_cotangent[s].astype(F32) + norm_backward(g_second, normed2, inverse2, ln2_gain)
        gb = gm.astype(LOW)
        add("out_b", gb.astype(F32))
        g_attn = dot(gb, out_weight, NT).astype(LOW)
        dq, dkv = attend_back(queries[s], g_attn, attn_full, inv_total, weights, kvs[s])
        g_queries.append(dq)
        g_kv.append(scatter_seq(dkv).astype(LOW))
        g_middle.append(gm)
        g_branch.append(gb)

    join = lambda items: jnp.concatenate(items, axis=0)
    cot_all = out_cotangent.reshape(count * rows, features)
    cot_rel = relative_columns(cot_all)
    down_grad = weight_grad(cot_rel, join(act))
    up_grad = weight_grad(relative_columns(join(second)), join(g_hidden))
    out_grad = weight_grad(relative_columns(join(g_branch)), join(heads))

    tokens_grads = []
    for s in every:
        gq, gk, gv = g_queries[s], g_kv[s][0], g_kv[s][1]
        part = (dot(gq, wq, NT) + dot(gk, wk, NT) + dot(gv, wv, NT)).astype(LOW)
        add("q_b", gq.astype(F32))
        add("v_b", gv.astype(F32))
        add("ln1_g", part.astype(F32) * normed1[s])
        add("ln1_b", part.astype(F32))
        g_first = part.astype(F32) + other_head(part).astype(F32)
        tokens_grads.append(
            (g_middle[s] + norm_backward(g_first, normed1[s], inverse1[s], ln1_gain)).astype(LOW)
        )
    first_rel = relative_columns(join(first))
    g_proj = [join(g_queries), join([g[0] for g in g_kv]), join([g[1] for g in g_kv])]
    qkv_grad = jnp.stack([weight_grad(first_rel, g) for g in g_proj], axis=1)

    ln1 = jnp.stack([vec["ln1_g"], vec["ln1_b"]])
    ln1 = ln1 + other_head(ln1)
    wide = [ln1[0], ln1[1], vec["out_b"], vec["ln2_g"], vec["ln2_b"], vec["down_b"]]
    blocks = [v.reshape(n_seq, n_dp, -1) for v in wide + [vec["q_b"], vec["v_b"], vec["up_b"]]]
    sizes = [b.shape[2] for b in blocks]
    small = scatter_small(jnp.concatenate(blocks, axis=2))
    pieces, at = [], 0
    for size in sizes:
        pieces.append(small[at:at + size])
        at += size

    return (
        jnp.stack(outputs),
        jnp.stack(tokens_grads),
        pieces[0],
        pieces[1],
        qkv_grad,
        jnp.stack([pieces[6], pieces[7]]),
        out_grad.T,
        pieces[2],
        pieces[3],
        pieces[4],
        up_grad,
        pieces[8],
        down_grad.T,
        pieces[5],
    )


def solution(mesh):
    in_specs = (
        P("dp", "seq", None),
        P("dp", "seq"),
        P(),
        P(),
        P(None, None, "head"),
        P(None, "head"),
        P("head", None),
        P(),
        P(),
        P(),
        P(None, "head"),
        P("head"),
        P("head", None),
        P(),
        P("dp", "seq", None),
    )
    out_specs = (
        P("dp", "seq", None),
        P("dp", "seq", None),
        P(("seq", "dp")),
        P(("seq", "dp")),
        P(("seq", "dp"), None, "head"),
        P(None, ("head", "seq", "dp")),
        P("head", ("seq", "dp")),
        P(("seq", "dp")),
        P(("seq", "dp")),
        P(("seq", "dp")),
        P(("seq", "dp"), "head"),
        P(("head", "seq", "dp")),
        P("head", ("seq", "dp")),
        P(("seq", "dp")),
    )
    return jax.shard_map(shards, mesh=mesh, in_specs=in_specs, out_specs=out_specs, check_vma=False)
```

```python
import functools

import jax
import jax.numpy as jnp
from jax import lax
from jax.experimental import pallas as pl
from jax.experimental.pallas import tpu as pltpu
from jax.sharding import PartitionSpec as P

HEAD_DIM = 64
LANES = 128
EPSILON = 1e-05
MASKED = -1e30
F32 = jnp.float32
LOW = jnp.bfloat16
NN = (((1,), (0,)), ((), ()))
NT = (((1,), (1,)), ((), ()))
TN = (((0,), (0,)), ((), ()))
VMEM_LIMIT = 60 * 2**20


def dot(a, b, dims=NN):
    return lax.dot_general(a, b, dims, preferred_element_type=F32)


def axis_size(name):
    return lax.axis_size(name)


def swap(value, axis, mask):
    return lax.ppermute(value, axis, [(i, i ^ mask) for i in range(axis_size(axis))])


def bits_of(count):
    return [1 << b for b in range(count.bit_length() - 1)]


def layer_norm(inputs, gain, shift):
    center = jnp.mean(inputs, axis=-1, keepdims=True)
    centred = inputs - center
    spread = jnp.mean(centred * centred, axis=-1, keepdims=True)
    inverse = lax.rsqrt(spread + EPSILON)
    normed = centred * inverse
    return (normed * gain + shift, normed, inverse)


def norm_backward(upstream, normed, inverse, gain):
    scaled = upstream * gain
    centred = scaled - jnp.mean(scaled, axis=-1, keepdims=True)
    return inverse * (centred - normed * jnp.mean(scaled * normed, axis=-1, keepdims=True))


def gelu_pair(v):
    c = 0.7978845608028654
    square = v * v
    t = jnp.tanh(c * v * (1.0 + 0.044715 * square))
    half = 0.5 * (1.0 + t)
    return v * half, half + (0.5 * c) * v * (1.0 - t * t) * (1.0 + 3.0 * 0.044715 * square)


def half_lanes(shape, head):
    lane = lax.broadcasted_iota(jnp.int32, shape, 1)
    return (lane < HEAD_DIM) if head == 0 else (lane >= HEAD_DIM)


def attend_kernel(n, q_ref, seg_ref, segk_ref, *refs):
    kv_refs = refs[:n]
    w_ref, attn_ref, low_ref, inv_ref = refs[n:]
    q = q_ref[...] * jnp.asarray(0.125, LOW)
    seg_q = seg_ref[0:1, :]
    for head in range(2):
        qh = jnp.where(half_lanes(q.shape, head), q, jnp.zeros_like(q))
        parts, top = [], None
        for m in range(n):
            s = dot(kv_refs[m][0], qh, NT)
            s = jnp.where(segk_ref[m] == seg_q, s, MASKED)
            peak = jnp.max(s, axis=0, keepdims=True)
            top = peak if top is None else jnp.maximum(top, peak)
            parts.append(s)
        total, mixed = 0.0, 0.0
        for m in range(n):
            w = jnp.exp(parts[m] - top)
            total = total + jnp.sum(w, axis=0, keepdims=True)
            wl = w.astype(LOW)
            w_ref[head, m] = wl
            vt = kv_refs[m][1].T[head * HEAD_DIM:(head + 1) * HEAD_DIM, :]
            mixed = mixed + dot(vt, wl)
        inverse = 1.0 / total
        inv_ref[0, head:head + 1, :] = inverse
        attn_ref[head * HEAD_DIM:(head + 1) * HEAD_DIM, :] = mixed * inverse
    low_ref[...] = attn_ref[...].T.astype(LOW)


def attend(q, seg_rows, seg_cols, kvs):
    n, (rows, width) = len(kvs), q.shape
    pairs = width // LANES
    step = lambda p: (0, p)
    kv_spec = pl.BlockSpec((2, rows, LANES), lambda p: (0, 0, p))
    return pl.pallas_call(
        functools.partial(attend_kernel, n),
        grid=(pairs,),
        in_specs=[
            pl.BlockSpec((rows, LANES), step),
            pl.BlockSpec((8, rows), lambda p: (0, 0)),
            pl.BlockSpec((n, rows, 1), lambda p: (0, 0, 0)),
        ]
        + [kv_spec] * n,
        out_specs=[
            pl.BlockSpec((2, n, rows, rows), lambda p: (p, 0, 0, 0)),
            pl.BlockSpec((LANES, rows), lambda p: (p, 0)),
            pl.BlockSpec((rows, LANES), step),
            pl.BlockSpec((1, 2, rows), lambda p: (p, 0, 0)),
        ],
        out_shape=[
            jax.ShapeDtypeStruct((2 * pairs, n, rows, rows), LOW),
            jax.ShapeDtypeStruct((width, rows), F32),
            jax.ShapeDtypeStruct((rows, width), LOW),
            jax.ShapeDtypeStruct((pairs, 2, rows), F32),
        ],
        compiler_params=pltpu.CompilerParams(vmem_limit_bytes=VMEM_LIMIT),
        cost_estimate=pl.CostEstimate(
            flops=2 * pairs * n * rows * rows * 256 * 4,
            bytes_accessed=2 * pairs * n * rows * rows * 2,
            transcendentals=2 * pairs * n * rows * rows,
        ),
    )(q, seg_rows, seg_cols, *kvs)


def attend_back_kernel(n, q_ref, g_ref, attn_ref, inv_ref, w_ref, *refs):
    kv_refs = refs[:n]
    dq_ref = refs[n]
    dkv_refs = refs[n + 1:2 * n + 1]
    dqt_ref = refs[2 * n + 1]
    q = q_ref[...]
    gt = g_ref[...].astype(F32).T
    qs, gs, gts, deltas = [], [], [], []
    for head in range(2):
        rows_h = slice(head * HEAD_DIM, (head + 1) * HEAD_DIM)
        part = (gt[rows_h] * inv_ref[0, head:head + 1, :]).astype(LOW)
        deltas.append(jnp.sum(part.astype(F32) * attn_ref[rows_h, :], axis=0, keepdims=True))
        zeros = jnp.zeros_like(part)
        full = jnp.concatenate([part, zeros] if head == 0 else [zeros, part], axis=0)
        gts.append(full)
        gs.append(full.T)
        qs.append(jnp.where(half_lanes(q.shape, head), q, jnp.zeros_like(q)))
    dqt = [0.0, 0.0]
    for m in range(n):
        kt = kv_refs[m][0].T
        v = kv_refs[m][1]
        dk = dv = 0.0
        for head in range(2):
            w = w_ref[head, m]
            ds = (w.astype(F32) * (dot(v, gts[head]) - deltas[head])).astype(LOW)
            dk = dk + dot(ds, qs[head])
            dv = dv + dot(w, gs[head])
            dqt[head] = dqt[head] + dot(kt[head * HEAD_DIM:(head + 1) * HEAD_DIM, :], ds)
        dkv_refs[m][0] = (dk * 0.125).astype(LOW)
        dkv_refs[m][1] = dv.astype(LOW)
    dqt_ref[0:HEAD_DIM, :] = dqt[0]
    dqt_ref[HEAD_DIM:LANES, :] = dqt[1]
    dq_ref[...] = (dqt_ref[...].T * 0.125).astype(LOW)


def attend_back(q, g, attn, inverse, weights, kvs):
    n, (rows, width) = len(kvs), q.shape
    pairs = width // LANES
    step = lambda p: (0, p)
    kv_spec = pl.BlockSpec((2, rows, LANES), lambda p: (0, 0, p))
    out = pl.pallas_call(
        functools.partial(attend_back_kernel, n),
        grid=(pairs,),
        in_specs=[
            pl.BlockSpec((rows, LANES), step),
            pl.BlockSpec((rows, LANES), step),
            pl.BlockSpec((LANES, rows), lambda p: (p, 0)),
            pl.BlockSpec((1, 2, rows), lambda p: (p, 0, 0)),
            pl.BlockSpec((2, n, rows, rows), lambda p: (p, 0, 0, 0)),
        ]
        + [kv_spec] * n,
        out_specs=[pl.BlockSpec((rows, LANES), step)] + [kv_spec] * n,
        out_shape=[jax.ShapeDtypeStruct((rows, width), LOW)]
        + [jax.ShapeDtypeStruct((2, rows, width), LOW)] * n,
        scratch_shapes=[pltpu.VMEM((LANES, rows), F32)],
        compiler_params=pltpu.CompilerParams(vmem_limit_bytes=VMEM_LIMIT),
        cost_estimate=pl.CostEstimate(
            flops=2 * pairs * n * rows * rows * 256 * 8,
            bytes_accessed=2 * pairs * n * rows * rows * 2,
            transcendentals=0,
        ),
    )(q, g, attn, inverse, weights, *kvs)
    return out[0], out[1:]


def gather_seq(block):
    bits = bits_of(axis_size("seq"))
    blocks = {0: block}
    for bit in reversed(bits):
        for m in list(blocks):
            blocks[m | bit] = swap(blocks[m], "seq", bit)
    return [blocks[m] for m in range(len(blocks))]


def scatter_seq(parts):
    parts = dict(enumerate(parts))
    for bit in bits_of(axis_size("seq")):
        for m in [m for m in sorted(parts, reverse=True) if m & bit]:
            got = swap(parts.pop(m).astype(LOW), "seq", bit)
            parts[m ^ bit] = parts[m ^ bit].astype(F32) + got.astype(F32)
    return parts[0].astype(F32)


def scatter_line(term):
    n = axis_size("dp")
    me = lax.axis_index("dp")
    rows = term.shape[0] // n
    block = lambda i: lax.dynamic_slice_in_dim(term, jnp.clip(i, 0, n - 1) * rows, rows, 0)
    up = down = None
    for k in range(n - 1, 0, -1):
        send_up = block(me + k) if up is None else block(me + k) + up
        send_down = block(me - k) if down is None else block(me - k) + down
        up = lax.ppermute(
            send_up.astype(LOW), "dp", [(i, i + 1) for i in range(n) if i + k < n]
        ).astype(F32)
        down = lax.ppermute(
            send_down.astype(LOW), "dp", [(i, i - 1) for i in range(n) if i - k >= 0]
        ).astype(F32)
    out = block(me)
    return out if n == 1 else out + up + down


def relative_columns(rows):
    n = axis_size("seq")
    me = lax.axis_index("seq")
    width = rows.shape[1] // n
    return [lax.dynamic_slice_in_dim(rows, (me ^ m) * width, width, 1) for m in range(n)]


def weight_grad(left, right):
    return scatter_line(scatter_seq([dot(part, right, TN) for part in left]))


def scatter_small(blocks):
    for axis in ("seq", "dp"):
        n = axis_size(axis)
        me = lax.axis_index(axis)
        bits = bits_of(n)
        rest = blocks.shape[1:]
        for bit in reversed(bits):
            low, high = blocks[:bit], blocks[bit:]
            mine = (me & bit) != 0
            send = jnp.where(mine, low, high)
            blocks = jnp.where(mine, high, low) + swap(send, axis, bit)
        blocks = blocks.reshape(rest)
    return blocks


def other_head(value):
    return swap(value, "head", 1)


def head_sum(value):
    value = value.astype(LOW)
    return value.astype(F32) + other_head(value).astype(F32)


def by_head(mine, other, axis):
    first = lax.axis_index("head") == 0
    return jnp.where(
        first,
        jnp.concatenate([mine, other], axis),
        jnp.concatenate([other, mine], axis),
    )


MESH = pl.DeviceIdType.MESH
CHUNK = 32
WIDE = 512


def loop(count, body, unroll=1, start=0):
    def step(i, carry):
        body(i)
        return carry

    lax.fori_loop(start, start + count, step, 0, unroll=unroll)


def span(i, size):
    return pl.ds(pl.multiple_of(i * size, size), size)


def fold(value):
    return jnp.sum(value.reshape(value.shape[0] // 8, 8, value.shape[1]), axis=0)


class Copy:
    def __init__(self, copy, remote):
        self.copy, self.remote = copy, remote
        self.sent = self.got = False

    def wait_recv(self):
        if not self.got:
            self.got = True
            if self.remote:
                self.copy.wait_recv()
            else:
                self.copy.wait()

    def wait_send(self):
        if self.remote and not self.sent:
            self.copy.wait_send()
        self.sent = True

    def wait(self):
        self.wait_send()
        self.wait_recv()


class Copies:
    def __init__(self, send, recv, local):
        self.sems, self.all = (send, recv, local), []
        self.n_remote = self.n_local = 0

    def start(self, src, dst, device):
        copy = pltpu.make_async_remote_copy(
            src_ref=src,
            dst_ref=dst,
            send_sem=self.sems[0].at[self.n_remote],
            recv_sem=self.sems[1].at[self.n_remote],
            device_id=device,
            device_id_type=MESH,
        )
        self.n_remote += 1
        return self.begin(copy, True)

    def load(self, src, dst):
        copy = pltpu.make_async_copy(src, dst, self.sems[2].at[self.n_local])
        self.n_local += 1
        return self.begin(copy, False)

    def begin(self, copy, remote):
        copy.start()
        self.all.append(Copy(copy, remote))
        return self.all[-1]

    def finish(self):
        for copy in self.all:
            copy.wait()


N_COPIES = 128
N_LOCAL = 24


def layer_kernel(n_dp, *refs):
    (
        tok_h, seg_in, g1, b1, wqkv_h, qvb, outw_h, outb, g2, b2, up_h, upb, down_h, downb, cot_h,
        out_h, tg_h, downg_h, upg_h, outg_h, qkvg_h, vec_o,
        tok, cot, wqkv, outw, up, down, q, kv, attn_t, attn, mid, lnb, act, gh,
        first_t, second_t, cot_t, gb_t, g_attn, gs, ffn, stat, st,
        gs_r, ffn_r, gf_r, dkv_r, q_far, g_far, st_far, act_r, gh_r, first_r, second_r, cot_r, gb_r, heads_r, dqkv_r,
        xr, zr, xz, zz,
        segs, segk, vec, qvacc, upacc, ln1_r, vs, vr,
        send, recv, local,
    ) = refs
    rows = tok.shape[0] // 2
    width = tok.shape[1]
    heads_w = q.shape[1]
    hidden = act.shape[1]
    pairs = heads_w // LANES
    quarter = width // 4
    block = quarter // n_dp
    s = lax.axis_index("seq")
    h = lax.axis_index("head")
    z = lax.axis_index("dp")
    x, core = s // 2, s % 2
    seq_peer = [None] + [((x ^ (m >> 1)) * 2 + (core ^ (m & 1)), h, z) for m in (1, 2, 3)]
    across = (s, 1 - h, z)
    next_z, far_z = z + 1 - 2 * lax.rem(z, 2), lax.rem(z + 2, 4)
    beside, beyond = (s, h, next_z), (s, h, far_z)
    half_w = heads_w // 2
    copies = Copies(send, recv, local)
    load = copies.load

    own_out = pl.ds(pl.multiple_of(h * heads_w, heads_w), heads_w)
    get_tok = load(tok_h, tok)
    get_qkv = load(wqkv_h, wqkv)

    barrier = pltpu.get_barrier_semaphore()
    partners = seq_peer[1:] + [across, beside, beyond]
    for device in partners:
        pl.semaphore_signal(barrier, inc=1, device_id=device, device_id_type=MESH)

    vec[...] = jnp.zeros_like(vec)
    qvacc[...] = jnp.zeros_like(qvacc)
    upacc[...] = jnp.zeros_like(upacc)
    segs[0] = jnp.zeros_like(segs[0])
    segs[0, 0:2, :] = seg_in[...]
    def seq_rows(i):
        return slice(i * rows, (i + 1) * rows)

    def flip(src, i, dst):
        def part(c):
            dst[span(c, 256), seq_rows(i)] = src[:, span(c, 256)].T

        loop(width // 256, part)

    def swap_rows(flipped, target):
        return [
            copies.start(
                flipped.at[pl.ds(pl.multiple_of(c * 2 * quarter + (1 - core) * quarter, quarter), quarter), :],
                target.at[c],
                seq_peer[1],
            )
            for c in range(2)
        ]

    kv_got = [[[None] * 2 for _ in range(4)] for _ in range(2)]
    q_got, q_next = [None] * 2, [None] * 2

    def first_norm(i):
        def norm(c):
            at = pl.ds(pl.multiple_of(i * rows + c * CHUNK, CHUNK), CHUNK)
            v = tok[at, :].astype(F32)
            center = jnp.mean(v, axis=-1, keepdims=True)
            v = v - center
            inverse = lax.rsqrt(jnp.mean(v * v, axis=-1, keepdims=True) + EPSILON)
            stat[0, at, 0:1] = center
            stat[0, at, 1:2] = inverse
            lnb[i, span(c, CHUNK), :] = (v * inverse * g1[...] + b1[...]).astype(LOW)

        loop(rows // CHUNK, norm, 4)

    def keys_values(i, part):
        cols = slice(part * half_w, (part + 1) * half_w)
        kv[i, 0, part, :, 0:half_w] = dot(lnb[i], wqkv[1, :, cols]).astype(LOW)
        kv[i, 0, part, :, half_w:heads_w] = (dot(lnb[i], wqkv[2, :, cols]) + qvb[1:2, cols]).astype(LOW)

    def send_keys(i, part):
        for m in (2, 1):
            kv_got[i][m][part] = copies.start(kv.at[i, 0, part], kv.at[i, m, part], seq_peer[m])

    def queries(i):
        q[seq_rows(i), :] = (dot(lnb[i], wqkv[0]) + qvb[0:1, :]).astype(LOW)
        q_got[i] = copies.start(q.at[seq_rows(i), :], q_far.at[i, 0], seq_peer[2])
        flip(lnb.at[i], i, first_t)

    seg_got = [None] * 4

    def meet():
        pl.semaphore_wait(barrier, len(partners))
        for m in (1, 2, 3):
            seg_got[m] = copies.start(segs.at[0], segs.at[m], seq_peer[m])

    def key_lanes(p):
        lane = lax.rem(p, 2) * LANES
        return p // 2, pl.ds(pl.multiple_of(lane, LANES), LANES), pl.ds(pl.multiple_of(half_w + lane, LANES), LANES)

    def twice(row):
        return jnp.concatenate([row, row], axis=1)

    def both(stats, k):
        return jnp.concatenate([stats[k:k + 1, :], stats[k + 1:k + 2, :]], axis=1)

    def cols_of(head):
        return slice(head * rows, (head + 1) * rows)

    def heads_of(pair_value, scale=None):
        if scale is not None:
            pair_value = pair_value * jnp.asarray(scale, LOW)
        zeros = jnp.zeros_like(pair_value)
        return [jnp.where(half_lanes(pair_value.shape, head), pair_value, zeros) for head in range(2)]

    def attend_blocks(i, blocks, begin, end, start, stop):
        seg_q = twice(segs[0, i:i + 1, :].astype(F32))

        def pair(p):
            lanes = span(p, LANES)
            part, k_lanes, v_lanes = key_lanes(p)
            qs = jnp.concatenate(heads_of(q[seq_rows(i), lanes], 0.125), axis=0)
            old = top = None if begin else both(st[i, p], 0)
            scores = []
            for m in blocks:
                score = dot(kv[i, m, part, :, k_lanes], qs, NT)
                score = jnp.where(segk[m, :, i:i + 1] == seg_q, score, MASKED)
                peak = jnp.max(score, axis=0, keepdims=True)
                top = peak if top is None else jnp.maximum(top, peak)
                scores.append(score)
            total, mixed = 0.0, [0.0, 0.0]
            for m, score in zip(blocks, scores):
                w = jnp.exp(score - top)
                total = total + jnp.sum(w, axis=0, keepdims=True)
                low = w.astype(LOW)
                vt = kv[i, m, part, :, v_lanes].T
                for head in range(2):
                    mixed[head] = mixed[head] + dot(vt[head * HEAD_DIM:(head + 1) * HEAD_DIM, :], low[:, cols_of(head)])
            if not begin:
                scale = jnp.exp(old - top)
                total = total + scale * both(st[i, p], 2)
            if end:
                inverse, lse = 1.0 / total, top + jnp.log(total)
            for head in range(2):
                at = pl.ds(pl.multiple_of(p * LANES + head * HEAD_DIM, HEAD_DIM), HEAD_DIM)
                value = mixed[head]
                if not begin:
                    value = value + scale[:, cols_of(head)] * attn_t[i, at, :]
                if end:
                    value = value * inverse[:, cols_of(head)]
                    st[i, p, 4 + head:5 + head, :] = lse[:, cols_of(head)]
                else:
                    st[i, p, head:head + 1, :] = top[:, cols_of(head)]
                    st[i, p, 2 + head:3 + head, :] = total[:, cols_of(head)]
                attn_t[i, at, :] = value
            if end:
                to = pl.ds(pl.multiple_of(h * heads_w + p * LANES, LANES), LANES)
                attn[seq_rows(i), to] = attn_t[i, lanes, :].T.astype(LOW)

        lax.fori_loop(start, stop, lambda p, c: (pair(p), c)[1], 0)

    def seg_columns(m):
        segk[m] = segs[m].astype(F32).T

    own_heads = pl.ds(pl.multiple_of(h * heads_w, heads_w), heads_w)
    attn_got = [[], []]

    def forward_keys(i, part):
        kv_got[i][2][part].wait_recv()
        kv_got[i][3][part] = copies.start(kv.at[i, 2, part], kv.at[i, 3, part], seq_peer[1])

    def forward_queries(i):
        q_got[i].wait_recv()
        q_next[i] = copies.start(q_far.at[i, 0], q_far.at[i, 1], seq_peer[1])

    def attend_far(i, part):
        kv_got[i][3][part].wait_recv()
        attend_blocks(i, (2, 3), False, True, part * pairs // 2, (part + 1) * pairs // 2)

    def send_heads(i, part):
        to = pl.ds(pl.multiple_of(h * heads_w + part * half_w, half_w), half_w)
        mine = attn.at[seq_rows(i), to]
        attn_got[i].append(copies.start(mine, mine, across))
        there = heads_r.at[seq_rows(i), part * half_w:(part + 1) * half_w]
        heads_sent.append(copies.start(mine, there, seq_peer[1]))

    heads_sent = []

    def middle(i):
        for copy in attn_got[i]:
            copy.wait_recv()

        def tile(j):
            at = span(j, WIDE)
            mid[seq_rows(i), at] = (
                dot(attn[seq_rows(i), :], outw[:, at])
                + tok[seq_rows(i), at].astype(F32)
                + outb[:, at]
            )

        loop(width // WIDE, tile)

        def norm(c):
            at = pl.ds(pl.multiple_of(i * rows + c * CHUNK, CHUNK), CHUNK)
            v = mid[at, :]
            center = jnp.mean(v, axis=-1, keepdims=True)
            v = v - center
            inverse = lax.rsqrt(jnp.mean(v * v, axis=-1, keepdims=True) + EPSILON)
            stat[1, at, 0:1] = center
            stat[1, at, 1:2] = inverse
            lnb[i, span(c, CHUNK), :] = (v * inverse * g2[...] + b2[...]).astype(LOW)

        loop(rows // CHUNK, norm, 4)

    gs_got, ffn_got = [None] * 2, [None] * 2
    act_got, gh_got = [[None] * 2, [None] * 2], [[None] * 2, [None] * 2]

    def cot_down(i):
        def tile(j):
            at = span(j, 2 * WIDE)
            gh[seq_rows(i), at] = dot(cot[seq_rows(i), :], down[at, :], NT).astype(LOW)

        loop(hidden // (2 * WIDE), tile)

    def feed(i, part):
        at_rows = seq_rows(i)

        def tile(j):
            at = span(j, WIDE)
            value, slope = gelu_pair(dot(lnb[i], up[:, at]) + upb[:, at])
            act[at_rows, at] = value.astype(LOW)
            g = (gh[at_rows, at].astype(F32) * slope).astype(LOW)
            gh[at_rows, at] = g
            upacc[:, at] += fold(g.astype(F32))

        tiles_each = hidden // WIDE // 2
        loop(tiles_each, tile, 1, part * tiles_each)
        cols = slice(part * hidden // 2, (part + 1) * hidden // 2)
        act_got[i][part] = copies.start(act.at[at_rows, cols], act_r.at[at_rows, cols], seq_peer[1])
        gh_got[i][part] = copies.start(gh.at[at_rows, cols], gh_r.at[at_rows, cols], seq_peer[1])

    def feed_back(i):
        at_rows = seq_rows(i)

        def back(j):
            gs[at_rows, span(j, WIDE)] = dot(gh[at_rows, :], up[span(j, WIDE), :], NT).astype(LOW)

        loop(width // WIDE, back)
        gs_got[i] = copies.start(gs.at[at_rows, :], gs_r.at[at_rows, :], across)
        flip(lnb.at[i], i, second_t)

    def feed_out(i):
        at_rows = seq_rows(i)

        def tile(j):
            ffn[at_rows, span(j, WIDE)] = dot(act[at_rows, :], down[:, span(j, WIDE)]).astype(LOW)

        loop(width // WIDE, tile)

    def send_feed_out(i):
        ffn_got[i] = copies.start(ffn.at[seq_rows(i), :], ffn_r.at[seq_rows(i), :], across)

    def finish_output(i):
        ffn_got[i].wait()

        def part(c):
            at = pl.ds(pl.multiple_of(i * rows + c * CHUNK, CHUNK), CHUNK)
            both = ffn[at, :].astype(F32) + ffn_r[at, :].astype(F32)
            ffn[at, :] = (mid[at, :] + both + downb[...]).astype(LOW)

        loop(rows // CHUNK, part, 4)
        load(ffn.at[seq_rows(i), :], out_h.at[seq_rows(i), :])

    gb = down.at[2 * rows:4 * rows, :]
    parts_kv = [[down.at[(4 + 2 * i + m) * rows:(5 + 2 * i + m) * rows, :] for m in range(2)] for i in range(2)]
    dqkv = up.at[2 * rows:4 * rows, :]

    def norm2_back(i):
        gs_got[i].wait_recv()

        def part(c):
            at = pl.ds(pl.multiple_of(i * rows + c * CHUNK, CHUNK), CHUNK)
            g = gs[at, :].astype(F32) + gs_r[at, :].astype(F32)
            inverse = stat[1, at, 1:2]
            normed = (mid[at, :] - stat[1, at, 0:1]) * inverse
            vec[3] += fold(g * normed)
            vec[4] += fold(g)
            e = g * g2[...]
            e = e - jnp.mean(e, axis=-1, keepdims=True) - normed * jnp.mean(e * normed, axis=-1, keepdims=True)
            low = (cot[at, :].astype(F32) + inverse * e).astype(LOW)
            gb[at, :] = low
            vec[2] += fold(low.astype(F32))

        loop(rows // CHUNK, part, 4)

        w_rows = pl.ds(pl.multiple_of(h * heads_w, heads_w), heads_w)
        g_attn[i] = dot(gb[seq_rows(i), :], outw[w_rows, :], NT).astype(LOW)

        def delta(p):
            g = g_attn[i, :, span(p, LANES)].astype(F32).T
            each = g * attn_t[i, span(p, LANES), :]
            for head in range(2):
                part = each[head * HEAD_DIM:(head + 1) * HEAD_DIM, :]
                st[i, p, 6 + head:7 + head, :] = jnp.sum(part, axis=0, keepdims=True)

        loop(pairs, delta)
        g_got[i] = [
            copies.start(g_attn.at[i], g_far.at[i, 0], seq_peer[2]),
            copies.start(st.at[i], st_far.at[i, 0], seq_peer[2]),
        ]

    g_got, g_next = [None] * 2, [None] * 2

    def forward_grads(i):
        for copy in g_got[i]:
            copy.wait_recv()
        g_next[i] = [
            copies.start(g_far.at[i, 0], g_far.at[i, 1], seq_peer[1]),
            copies.start(st_far.at[i, 0], st_far.at[i, 1], seq_peer[1]),
        ]

    def backward_terms(allowed, k, v, q_scaled, g, lse, delta):
        probs = jnp.exp(jnp.where(allowed, dot(k, q_scaled, NT) - lse, MASKED))
        return probs.astype(LOW), (probs * (dot(v, g, NT) - delta)).astype(LOW)

    def back_own(i):
        seg_q = twice(segs[0, i:i + 1, :].astype(F32))

        def pair(p):
            lanes = span(p, LANES)
            v_lanes = pl.ds(pl.multiple_of(heads_w + p * LANES, LANES), LANES)
            part, k_in, v_in = key_lanes(p)
            qs = jnp.concatenate(heads_of(q[seq_rows(i), lanes]), axis=0)
            q_scaled = qs * jnp.asarray(0.125, LOW)
            g = jnp.concatenate(heads_of(g_attn[i, :, lanes]), axis=0)
            lse, delta = both(st[i, p], 4), both(st[i, p], 6)
            dqt = [0.0, 0.0]
            for m in range(4):
                k = kv[i, m, part, :, k_in]
                kt = k.T
                v = kv[i, m, part, :, v_in]
                probs, ds = backward_terms(segk[m, :, i:i + 1] == seg_q, k, v, q_scaled, g, lse, delta)
                if m < 2:
                    parts_kv[i][m][:, lanes] = (dot(ds, qs) * 0.125).astype(LOW)
                    parts_kv[i][m][:, v_lanes] = dot(probs, g).astype(LOW)
                for head in range(2):
                    dqt[head] = dqt[head] + dot(kt[head * HEAD_DIM:(head + 1) * HEAD_DIM, :], ds[:, cols_of(head)])
            dq = (jnp.concatenate(dqt, axis=0).T * 0.125).astype(LOW)
            dqkv[seq_rows(i), lanes] = dq
            qvacc[:, lanes] += fold(dq.astype(F32))

        loop(pairs, pair)
        near_got[i] = copies.start(parts_kv[i][1], dkv_r.at[i], seq_peer[1])
        at = (seq_rows(i), pl.ds(0, heads_w))
        dq_got[i] = copies.start(dqkv.at[at], dqkv_r.at[at], seq_peer[1])

    def back_far(i):
        q_next[i].wait_recv()
        for copy in g_next[i]:
            copy.wait_recv()
        near_got[i].wait_recv()
        seg_q = [twice(segs[2 + b, i:i + 1, :].astype(F32)) for b in range(2)]
        at_rows = seq_rows(i)

        def pair(p):
            lanes = span(p, LANES)
            v_lanes = pl.ds(pl.multiple_of(heads_w + p * LANES, LANES), LANES)
            part, k_in, v_in = key_lanes(p)
            k = kv[i, 0, part, :, k_in]
            v = kv[i, 0, part, :, v_in]
            dk = dv = 0.0
            for b in range(2):
                qs = jnp.concatenate(heads_of(q_far[i, b, :, lanes]), axis=0)
                q_scaled = qs * jnp.asarray(0.125, LOW)
                g = jnp.concatenate(heads_of(g_far[i, b, :, lanes]), axis=0)
                lse, delta = both(st_far[i, b, p], 4), both(st_far[i, b, p], 6)
                probs, ds = backward_terms(segk[0, :, i:i + 1] == seg_q[b], k, v, q_scaled, g, lse, delta)
                dk = dk + dot(ds, qs)
                dv = dv + dot(probs, g)
            near = lambda to: parts_kv[i][0][:, to].astype(F32) + dkv_r[i, :, to].astype(F32)
            k_at = pl.ds(pl.multiple_of(heads_w + p * LANES, LANES), LANES)
            v_at = pl.ds(pl.multiple_of(2 * heads_w + p * LANES, LANES), LANES)
            dqkv[at_rows, k_at] = (dk * 0.125 + near(lanes)).astype(LOW)
            low = (dv + near(v_lanes)).astype(LOW)
            dqkv[at_rows, v_at] = low
            qvacc[:, k_at] += fold(low.astype(F32))

        loop(pairs, pair)
        at = (at_rows, kv_cols)
        dkv_got[i] = copies.start(dqkv.at[at], dqkv_r.at[at], seq_peer[1])

    near_got, dq_got = [None] * 2, [None] * 2
    kv_cols = pl.ds(heads_w, 2 * heads_w)

    dkv_got, gf_got = [None] * 2, [None] * 2

    def first_back(i):
        gs_got[i].wait_send()

        def tile(j):
            at = span(j, WIDE)
            total = 0.0
            for c in range(3):
                total = total + dot(dqkv[seq_rows(i), c * heads_w:(c + 1) * heads_w], wqkv[c, at, :], NT)
            gs[seq_rows(i), at] = total.astype(LOW)

        loop(width // WIDE, tile)
        def sums(c):
            at = pl.ds(pl.multiple_of(i * rows + c * CHUNK, CHUNK), CHUNK)
            g = gs[at, :].astype(F32)
            normed = (tok[at, :].astype(F32) - stat[0, at, 0:1]) * stat[0, at, 1:2]
            vec[0] += fold(g * normed)
            vec[1] += fold(g)

        loop(rows // CHUNK, sums, 4)

    def send_first_back(i):
        gf_got[i] = copies.start(gs.at[seq_rows(i), :], gf_r.at[seq_rows(i), :], across)

    def norm1_back(i):
        gf_got[i].wait()

        def part(c):
            at = pl.ds(pl.multiple_of(i * rows + c * CHUNK, CHUNK), CHUNK)
            g = gs[at, :].astype(F32) + gf_r[at, :].astype(F32)
            inverse = stat[0, at, 1:2]
            normed = (tok[at, :].astype(F32) - stat[0, at, 0:1]) * inverse
            e = g * g1[...]
            e = e - jnp.mean(e, axis=-1, keepdims=True) - normed * jnp.mean(e * normed, axis=-1, keepdims=True)
            gs[at, :] = (gb[at, :].astype(F32) + inverse * e).astype(LOW)

        loop(rows // CHUNK, part, 4)
        load(gs.at[seq_rows(i), :], tg_h.at[seq_rows(i), :])

    def tiles(piece, chip, body):
        left, left_r, right, right_r, cols = piece
        at_rows = pl.ds(pl.multiple_of(chip * 2 * quarter + core * quarter, quarter), quarter)
        step = min(cols, 2 * WIDE)

        def tile(j):
            at = span(j, step)
            body(at, dot(left[at_rows, :], right[:, at]) + dot(left_r[chip], right_r[:, at]))

        loop(cols // step, tile)

    def block_rows(index):
        return pl.ds(pl.multiple_of(index * block, block), block)

    def send_beside(hold, arrive):
        further = lax.rem(next_z + 2, 4)
        return [
            copies.start(hold.at[block_rows(next_z), :], arrive[0], beside),
            copies.start(hold.at[block_rows(further), :], arrive[1], beside),
        ]

    def send_beyond(hold, arrive):
        at = block_rows(far_z)
        hold[at, :] = (hold[at, :].astype(F32) + arrive[1][...].astype(F32)).astype(LOW)
        return copies.start(hold.at[at, :], arrive[2], beyond)

    def own_block(hold, arrive, at=slice(None)):
        total = hold[block_rows(z), at].astype(F32)
        return total + arrive[0][:, at].astype(F32) + arrive[2][:, at].astype(F32)

    def hand_out(place, target, value):
        size = target.shape[1]
        top, left = place // 4 * block, place % 4 * (width // 4)
        mid[top:top + block, left:left + size] = value(slice(None))
        load(mid.at[top:top + block, left:left + size], target)
        return place + size * 4 // width

    class AcrossFirst:
        def __init__(self, piece, hold, offset, arrivals):
            self.piece, self.hold, self.arrivals = piece, hold, arrivals
            cols = pl.ds(offset, piece[4])
            self.xr = xr.at[:, cols]
            self.zr = [zr.at[d, :, cols] for d in range(3)]

        def prepare(self):
            for copy in self.arrivals():
                copy.wait_recv()

            def keep(at, value):
                self.hold[:, at] = value.astype(LOW)

            tiles(self.piece, 1 - x, keep)

        def across(self):
            self.far = copies.start(self.hold, self.xr, seq_peer[2])

        def beside(self):
            self.far.wait()

            def keep(at, value):
                self.hold[:, at] = (value + self.xr[:, at].astype(F32)).astype(LOW)

            tiles(self.piece, x, keep)
            self.near = send_beside(self.hold, self.zr)

        def beyond(self):
            for copy in self.near:
                copy.wait_recv()
            self.last = send_beyond(self.hold, self.zr)

        def done(self, place, target):
            self.last.wait_recv()
            return hand_out(place, target, lambda at: own_block(self.hold, self.zr, at))

    class AlongFirst:
        def __init__(self, piece, holds, offset, arrivals):
            self.piece, self.holds, self.arrivals = piece, holds, arrivals
            cols = pl.ds(offset, piece[4])
            self.zz = [[zz.at[r, d, :, cols] for d in range(3)] for r in range(2)]
            self.xz = xz.at[:, cols]

        def beside(self):
            for copy in self.arrivals():
                copy.wait_recv()
            self.near = []
            for r in (1, 0):

                def keep(at, value, r=r):
                    self.holds[r][:, at] = value.astype(LOW)

                tiles(self.piece, x ^ r, keep)
                self.near += send_beside(self.holds[r], self.zz[r])

        def beyond(self):
            for copy in self.near:
                copy.wait_recv()
            self.last = [send_beyond(self.holds[r], self.zz[r]) for r in (1, 0)]

        def across(self):
            for copy in self.last:
                copy.wait_recv()
            mine = block_rows(z)
            self.holds[1][mine, :] = own_block(self.holds[1], self.zz[1]).astype(LOW)
            self.far = copies.start(self.holds[1].at[mine, :], self.xz, seq_peer[2])

        def done(self, place, target):
            self.far.wait_recv()

            def value(at):
                return own_block(self.holds[0], self.zz[0], at) + self.xz[:, at].astype(F32)

            return hand_out(place, target, value)

    attn_own = attn.at[:, own_heads]
    q_cols, k_cols, v_cols = (slice(c * heads_w, (c + 1) * heads_w) for c in range(3))
    flips = {}
    down_piece = lambda at, n: (cot_t, cot_r, act.at[:, at:at + n], act_r.at[:, at:at + n], n)
    up_piece = lambda at, n: (second_t, second_r, gh.at[:, at:at + n], gh_r.at[:, at:at + n], n)
    proj_piece = lambda at, n: (first_t, first_r, dqkv.at[:, at], dqkv_r.at[:, at], n)
    quarter_h = hidden // 4
    halves_of = lambda got, at: [got[i][at // (2 * quarter_h)] for i in range(2)]
    from_cot = lambda at: lambda: flips["cot"] + halves_of(act_got, at)
    from_second = lambda at: lambda: flips["second"] + halves_of(gh_got, at)
    spans = [(0, 2 * quarter_h), (2 * quarter_h, quarter_h), (3 * quarter_h, quarter_h)]
    downs = [
        AcrossFirst(down_piece(at, n), lnb.at[0] if k == 0 else up.at[0:rows, at:at + n], at, from_cot(at))
        for k, (at, n) in enumerate(spans)
    ]
    ups = [
        AlongFirst(
            up_piece(at, n),
            [up.at[rows:2 * rows, at:at + n], up.at[0:rows, 0:n] if k == 0 else lnb.at[1, :, 0:n]],
            at,
            from_second(at),
        )
        for k, (at, n) in enumerate(spans[:2])
    ]
    up_last = AcrossFirst(
        up_piece(3 * quarter_h, quarter_h), up.at[rows:2 * rows, 3 * quarter_h:hidden], hidden, from_second(3 * quarter_h)
    )
    base = hidden + quarter_h
    proj_out = AcrossFirst(
        (gb_t, gb_r, attn_own, heads_r, heads_w),
        down.at[0:rows, 0:heads_w],
        base,
        lambda: flips["gb"] + heads_sent,
    )
    proj_q = AcrossFirst(
        proj_piece(q_cols, heads_w),
        down.at[0:rows, heads_w:2 * heads_w],
        base + heads_w,
        lambda: flips["first"] + dq_got,
    )
    from_proj = lambda: flips["first"] + dkv_got
    proj_k = AcrossFirst(
        proj_piece(k_cols, heads_w), down.at[rows:2 * rows, 0:heads_w], base + 2 * heads_w, from_proj
    )
    v_halves = [slice(heads_w + c * half_w, heads_w + (c + 1) * half_w) for c in range(2)]
    proj_v = [
        AcrossFirst(
            proj_piece(slice(heads_w + at.start, heads_w + at.stop), half_w),
            down.at[rows:2 * rows, at],
            base + 2 * heads_w + at.start,
            from_proj,
        )
        for at in v_halves
    ]

    def share_out():
        half = heads_w // 2
        get_out.wait()
        mine = pl.ds(pl.multiple_of(h * heads_w + core * half, half), half)
        return copies.start(outw.at[mine, :], outw.at[mine, :], across)

    def forward_out():
        out_got.wait_recv()
        half = heads_w // 2
        theirs = pl.ds(pl.multiple_of((1 - h) * heads_w + core * half, half), half)
        return copies.start(outw.at[theirs, :], outw.at[theirs, :], seq_peer[1])

    def scenes():
        for m in (1, 2, 3):
            seg_got[m].wait_recv()
        for m in range(4):
            seg_columns(m)

    def attend_near(i):
        for copy in kv_got[i][1]:
            copy.wait_recv()
        attend_blocks(i, (0, 1), True, False, 0, pairs)

    def prepare_cot():
        get_cot.wait()

        def part(c):
            vec[5] += fold(cot[span(c, CHUNK), :].astype(F32))

        loop(2 * rows // CHUNK, part, 4)
        for i in range(2):
            flip(cot.at[seq_rows(i), :], i, cot_t)
        flips["cot"] = swap_rows(cot_t, cot_r)

    def flip_branch():
        for i in range(2):
            flip(gb.at[seq_rows(i), :], i, gb_t)
        flips["gb"] = swap_rows(gb_t, gb_r)

    def vectors():
        ln1_got.wait_recv()
        lines = [jnp.sum(vec[k] + ln1_r[k], axis=0, keepdims=True) for k in range(2)]
        lines += [jnp.sum(vec[k], axis=0, keepdims=True) for k in range(2, 6)]
        lines += [jnp.sum(qvacc[...], axis=0, keepdims=True)]
        sums = jnp.sum(upacc[...], axis=0, keepdims=True)
        lines += [sums[:, c * width:(c + 1) * width] for c in range(hidden // width)]
        lines += [jnp.zeros((16 - len(lines), width), F32)]
        vs[0] = jnp.concatenate(lines, axis=0)
        return copies.start(vs.at[0], vr.at[0], seq_peer[1])

    def vectors_on(k, copy, device):
        copy.wait_recv()
        vs[k] = vs[k - 1] + vr[k - 1]
        return copies.start(vs.at[k], vr.at[k], device)

    def vectors_done():
        vec_4.wait_recv()
        vec_o[...] = vs[3] + vr[3]

    get_tok.wait()
    first_norm(0)
    get_qkv.wait()
    keys_values(0, 0)
    meet()
    send_keys(0, 0)
    keys_values(0, 1)
    send_keys(0, 1)
    get_out, get_cot = load(outw_h, outw.at[own_out, :]), load(cot_h, cot)
    get_down, get_up = load(down_h, down), load(up_h, up)
    first_norm(1)
    keys_values(1, 0)
    send_keys(1, 0)
    keys_values(1, 1)
    send_keys(1, 1)
    queries(0)
    queries(1)
    flips["first"] = swap_rows(first_t, first_r)
    out_got = share_out()
    scenes()
    attend_near(0)
    attend_near(1)
    forward_keys(0, 0)
    prepare_cot()
    forward_keys(0, 1)
    attend_far(0, 0)
    send_heads(0, 0)
    attend_far(0, 1)
    send_heads(0, 1)
    out_near = forward_out()
    get_down.wait()
    cot_down(0)
    forward_keys(1, 0)
    cot_down(1)
    attend_far(1, 0)
    send_heads(1, 0)
    forward_keys(1, 1)
    attend_far(1, 1)
    send_heads(1, 1)
    out_near.wait_recv()
    get_up.wait()
    middle(0)
    feed(0, 0)
    feed(0, 1)
    feed_back(0)
    middle(1)
    feed(1, 0)
    feed(1, 1)
    downs[0].prepare()
    downs[0].across()
    feed_back(1)
    flips["second"] = swap_rows(second_t, second_r)
    ups[0].beside()
    ups[1].beside()
    feed_out(0)
    send_feed_out(0)
    feed_out(1)
    forward_queries(0)
    forward_queries(1)
    norm2_back(0)
    downs[1].prepare()
    downs[1].across()
    back_own(0)
    ups[0].beyond()
    norm2_back(1)
    downs[0].beside()
    forward_grads(0)
    downs[2].prepare()
    downs[2].across()
    flip_branch()
    back_far(0)
    ups[1].beyond()
    first_back(0)
    send_first_back(0)
    proj_out.prepare()
    proj_out.across()
    up_last.prepare()
    up_last.across()
    back_own(1)
    forward_grads(1)
    downs[1].beside()
    downs[2].beside()
    downs[0].beyond()
    back_far(1)
    first_back(1)
    ln1_got = copies.start(vec.at[0:2], ln1_r, across)
    send_first_back(1)
    send_feed_out(1)
    proj_q.prepare()
    proj_q.across()
    proj_k.prepare()
    proj_k.across()
    proj_v[0].prepare()
    proj_v[0].across()
    proj_v[1].prepare()
    proj_v[1].across()
    proj_out.beside()
    norm1_back(0)
    downs[1].beyond()
    downs[2].beyond()
    finish_output(0)
    vec_1 = vectors()
    up_last.beside()
    proj_out.beyond()
    vec_2 = vectors_on(1, vec_1, seq_peer[2])
    ups[0].across()
    ups[1].across()
    proj_q.beside()
    up_last.beyond()
    norm1_back(1)
    proj_k.beside()
    proj_q.beyond()
    proj_v[0].beside()
    proj_k.beyond()
    proj_v[1].beside()
    proj_v[0].beyond()
    vec_3 = vectors_on(2, vec_2, beside)
    finish_output(1)
    proj_v[1].beyond()
    vec_4 = vectors_on(3, vec_3, beyond)
    place = 0
    for group, (at, n) in zip(downs, spans): place = group.done(place, downg_h.at[:, at:at + n])
    for group, (at, n) in zip(ups + [up_last], spans): place = group.done(place, upg_h.at[:, at:at + n])
    place = proj_out.done(place, outg_h)
    place = proj_q.done(place, qkvg_h.at[0])
    place = proj_k.done(place, qkvg_h.at[1])
    for group, c in zip(proj_v, range(2)): place = group.done(place, qkvg_h.at[2, :, c * half_w:(c + 1) * half_w])
    vectors_done()
    copies.finish()


def one_kernel(args):
    (
        tokens, segment_ids, ln1_gain, ln1_bias, qkv_weight, qv_bias, out_weight, out_bias,
        ln2_gain, ln2_bias, up_weight, up_bias, down_weight, down_bias, out_cotangent,
    ) = args
    count, rows, width = tokens.shape
    heads_w, hidden = qkv_weight.shape[2], up_weight.shape[1]
    n_dp = axis_size("dp")
    block = width // (4 * n_dp)
    total = count * rows
    grads = hidden + hidden // 4 + 4 * heads_w
    line = lambda v: v.reshape(1, -1)
    low = lambda *shape: pltpu.VMEM(shape, LOW)
    full = lambda *shape: pltpu.VMEM(shape, F32)
    shape = jax.ShapeDtypeStruct
    vmem, anywhere = pl.BlockSpec(memory_space=pltpu.VMEM), pl.BlockSpec(memory_space=pl.ANY)
    return pl.pallas_call(
        functools.partial(layer_kernel, n_dp),
        in_specs=[anywhere, vmem, vmem, vmem, anywhere, vmem, anywhere, vmem, vmem, vmem, anywhere, vmem, anywhere, vmem, anywhere],
        out_specs=[anywhere] * 6 + [vmem],
        out_shape=[
            shape((total, width), LOW),
            shape((total, width), LOW),
            shape((block, hidden), F32),
            shape((block, hidden), F32),
            shape((block, heads_w), F32),
            shape((3, block, heads_w), F32),
            shape((16, width), F32),
        ],
        scratch_shapes=[
            low(total, width), low(total, width), low(3, width, heads_w), low(2 * heads_w, width),
            low(width, hidden), low(hidden, width), low(total, heads_w), low(2, 4, 2, rows, heads_w),
            full(2, heads_w, rows), low(total, width), full(total, width), low(2, rows, width),
            low(total, hidden), low(total, hidden),
            low(width, total), low(width, total), low(width, total), low(width, total),
            low(2, rows, heads_w), low(total, width), low(total, width),
            full(2, total, 2), full(2, heads_w // LANES, 8, rows),
            low(total, width), low(total, width), low(total, width), low(2, rows, 2 * heads_w),
            low(2, 2, rows, heads_w), low(2, 2, rows, heads_w), full(2, 2, heads_w // LANES, 8, rows),
            low(total, hidden), low(total, hidden),
            low(2, width // 4, total), low(2, width // 4, total), low(2, width // 4, total), low(2, width // 4, total),
            low(total, heads_w), low(total, 3 * heads_w), low(width // 4, grads), low(3, block, grads),
            low(block, 3 * hidden // 4), low(2, 3, block, 3 * hidden // 4),
            pltpu.VMEM((4, 8, rows), jnp.int32), full(4, rows, 8), full(6, 8, width), full(8, 2 * heads_w), full(8, hidden),
            full(2, 8, width), full(4, 16, width), full(4, 16, width),
            pltpu.SemaphoreType.DMA((N_COPIES,)), pltpu.SemaphoreType.DMA((N_COPIES,)), pltpu.SemaphoreType.DMA((N_LOCAL,)),
        ],
        compiler_params=pltpu.CompilerParams(
            collective_id=0, has_side_effects=True, vmem_limit_bytes=FAST_VMEM
        ),
    )(
        tokens.reshape(total, width), segment_ids, line(ln1_gain), line(ln1_bias), jnp.transpose(qkv_weight, (1, 0, 2)),
        qv_bias, out_weight, line(out_bias), line(ln2_gain), line(ln2_bias), up_weight, line(up_bias),
        down_weight, line(down_bias), out_cotangent.reshape(total, width),
    )


FAST_VMEM = 62 * 2**20


def fits(args):
    tokens, qkv_weight, up_weight = args[0], args[4], args[10]
    count, rows, width = tokens.shape
    heads_w, hidden = qkv_weight.shape[2], up_weight.shape[1]
    return (
        (axis_size("seq"), axis_size("head"), axis_size("dp")) == (4, 2, 4)
        and (count, rows) == (2, 256)
        and (width, heads_w, hidden) == (1024, 512, 2048)
    )


def split_kernel(parts, index_ref, vec_ref, *refs):
    big = (len(refs) - 1 - 8) // 3
    sources, targets, small = refs[:big], refs[big:2 * big], refs[2 * big:2 * big + 8]
    held, sem = refs[2 * big + 8:-1], refs[-1]
    moves = [pltpu.make_async_copy(a, b, sem.at[0, k]) for k, (a, b) in enumerate(zip(sources, held))]
    for move in moves:
        move.start()
    back = [pltpu.make_async_copy(a, b, sem.at[1, k]) for k, (a, b) in enumerate(zip(held, targets))]
    for move, out in zip(moves, back):
        move.wait()
        out.start()
    at = index_ref[0]
    width = vec_ref.shape[1]

    def piece(row, size):
        shift = lax.rem(width - lax.rem(at * size, width), width)
        return pltpu.roll(vec_ref[row:row + 1, :], shift, 1)[:, :size]

    size = width // parts
    for ref, row in zip(small[:6], (0, 1, 2, 3, 4, 5)):
        ref[...] = piece(row, size)
    half = vec_ref[6:7, :]
    shift = lax.rem(width - at * (size // 2), width)
    turned = pltpu.roll(half, shift, 1)
    small[6][0:1, :] = turned[:, :size // 2]
    small[6][1:2, :] = pltpu.roll(turned, width // 2, 1)[:, :size // 2]
    size = small[7].shape[1]
    low, high = piece(7, size), piece(8, size)
    small[7][...] = jnp.where(at * size < width, low, high)
    for out in back:
        out.wait()


def split(parts, big, vec):
    at = lax.axis_index("seq") * axis_size("dp") + lax.axis_index("dp")
    size = vec.shape[1] // parts
    shape = jax.ShapeDtypeStruct
    smalls = [shape((1, size), F32)] * 6 + [shape((2, size // 2), F32), shape((1, 2 * size), F32)]
    vmem, anywhere = pl.BlockSpec(memory_space=pltpu.VMEM), pl.BlockSpec(memory_space=pl.ANY)
    out = pl.pallas_call(
        functools.partial(split_kernel, parts),
        in_specs=[pl.BlockSpec(memory_space=pltpu.SMEM), vmem] + [anywhere] * len(big),
        out_specs=[anywhere] * len(big) + [vmem] * 8,
        out_shape=[shape(v.shape, v.dtype) for v in big] + smalls,
        scratch_shapes=[pltpu.VMEM(v.shape, v.dtype) for v in big] + [pltpu.SemaphoreType.DMA((2, len(big)))],
        compiler_params=pltpu.CompilerParams(vmem_limit_bytes=FAST_VMEM),
    )(at.astype(jnp.int32).reshape(1), vec, *big)
    return out[:len(big)], out[len(big):]


def fast(*args):
    tokens = args[0]
    *big, vec = one_kernel(args)
    big, small = split(axis_size("seq") * axis_size("dp"), big, vec)
    out, tokens_grad, down_grad, up_grad, out_grad, qkv_grad = big
    flat = [v.reshape(-1) for v in small]
    return (
        out.reshape(tokens.shape),
        tokens_grad.reshape(tokens.shape),
        flat[0],
        flat[1],
        jnp.transpose(qkv_grad, (1, 0, 2)),
        small[6],
        out_grad.T,
        flat[2],
        flat[3],
        flat[4],
        up_grad,
        flat[7],
        down_grad.T,
        flat[5],
    )


def shards(*args):
    return fast(*args) if fits(args) else general(*args)


def general(
    tokens,
    segment_ids,
    ln1_gain,
    ln1_bias,
    qkv_weight,
    qv_bias,
    out_weight,
    out_bias,
    ln2_gain,
    ln2_bias,
    up_weight,
    up_bias,
    down_weight,
    down_bias,
    out_cotangent,
):
    count, rows, features = tokens.shape
    local = qkv_weight.shape[2]
    hidden_local = up_weight.shape[1]
    n_seq, n_dp = axis_size("seq"), axis_size("dp")
    every = range(count)
    wq, wk, wv = (qkv_weight[:, c, :] for c in range(3))

    seg = gather_seq(segment_ids)
    seg_rows = [jnp.broadcast_to(segment_ids[s][None, :], (8, rows)) for s in every]
    seg_cols = [jnp.stack([part[s] for part in seg])[:, :, None] for s in every]

    half = out_weight.shape[0] // 2
    core = lax.axis_index("seq") & 1
    fetched = other_head(lax.dynamic_slice_in_dim(out_weight, core * half, half, 0))
    swapped = swap(fetched, "seq", 1)
    out_other = jnp.where(
        core == 0,
        jnp.concatenate([fetched, swapped], 0),
        jnp.concatenate([swapped, fetched], 0),
    )
    out_full = by_head(out_weight, out_other, 0)

    inputs, first, normed1, inverse1, queries, kvs = [], [], [], [], [], []
    for s in every:
        x = tokens[s].astype(F32)
        pre, normed, inverse = layer_norm(x, ln1_gain, ln1_bias)
        low = pre.astype(LOW)
        k = dot(low, wk).astype(LOW)
        v = (dot(low, wv) + qv_bias[1]).astype(LOW)
        kvs.append(gather_seq(jnp.stack([k, v])))
        queries.append((dot(low, wq) + qv_bias[0]).astype(LOW))
        inputs.append(x)
        first.append(low)
        normed1.append(normed)
        inverse1.append(inverse)

    attended = [attend(queries[s], seg_rows[s], seg_cols[s], kvs[s]) for s in every]

    outputs, second, act, g_hidden, g_middle, heads = [], [], [], [], [], []
    g_queries, g_kv = [], []
    vec = {
        name: 0.0 for name in ("out_b", "ln2_g", "ln2_b", "down_b", "up_b", "q_b", "v_b", "ln1_g", "ln1_b")
    }
    add = lambda name, value: vec.__setitem__(name, vec[name] + jnp.sum(value, axis=0))
    state = []
    for s in every:
        weights, attn_full, attn_low, inv_total = attended[s]
        mixed = by_head(attn_low, other_head(attn_low), 1)
        middle = inputs[s] + dot(mixed, out_full) + out_bias
        pre, normed2, inverse2 = layer_norm(middle, ln2_gain, ln2_bias)
        low = pre.astype(LOW)
        hidden = dot(low, up_weight) + up_bias
        activated, slope = gelu_pair(hidden)
        act_low = activated.astype(LOW)
        cot = out_cotangent[s]
        gh = (dot(cot, down_weight, NT) * slope).astype(LOW)
        g_second = head_sum(dot(gh, up_weight, NT))
        mlp = head_sum(dot(act_low, down_weight))
        outputs.append((middle + mlp + down_bias).astype(LOW))
        second.append(low)
        act.append(act_low)
        g_hidden.append(gh)
        heads.append(attn_low)
        state.append((normed2, inverse2, g_second))
        add("down_b", cot.astype(F32))
        add("up_b", gh.astype(F32))

    g_branch, g_first_parts = [], []
    for s in every:
        normed2, inverse2, g_second = state[s]
        weights, attn_full, attn_low, inv_total = attended[s]
        add("ln2_g", g_second * normed2)
        add("ln2_b", g_second)
        gm = out_cotangent[s].astype(F32) + norm_backward(g_second, normed2, inverse2, ln2_gain)
        gb = gm.astype(LOW)
        add("out_b", gb.astype(F32))
        g_attn = dot(gb, out_weight, NT).astype(LOW)
        dq, dkv = attend_back(queries[s], g_attn, attn_full, inv_total, weights, kvs[s])
        g_queries.append(dq)
        g_kv.append(scatter_seq(dkv).astype(LOW))
        g_middle.append(gm)
        g_branch.append(gb)

    join = lambda items: jnp.concatenate(items, axis=0)
    cot_all = out_cotangent.reshape(count * rows, features)
    cot_rel = relative_columns(cot_all)
    down_grad = weight_grad(cot_rel, join(act))
    up_grad = weight_grad(relative_columns(join(second)), join(g_hidden))
    out_grad = weight_grad(relative_columns(join(g_branch)), join(heads))

    tokens_grads = []
    for s in every:
        gq, gk, gv = g_queries[s], g_kv[s][0], g_kv[s][1]
        part = (dot(gq, wq, NT) + dot(gk, wk, NT) + dot(gv, wv, NT)).astype(LOW)
        add("q_b", gq.astype(F32))
        add("v_b", gv.astype(F32))
        add("ln1_g", part.astype(F32) * normed1[s])
        add("ln1_b", part.astype(F32))
        g_first = part.astype(F32) + other_head(part).astype(F32)
        tokens_grads.append(
            (g_middle[s] + norm_backward(g_first, normed1[s], inverse1[s], ln1_gain)).astype(LOW)
        )
    first_rel = relative_columns(join(first))
    g_proj = [join(g_queries), join([g[0] for g in g_kv]), join([g[1] for g in g_kv])]
    qkv_grad = jnp.stack([weight_grad(first_rel, g) for g in g_proj], axis=1)

    ln1 = jnp.stack([vec["ln1_g"], vec["ln1_b"]])
    ln1 = ln1 + other_head(ln1)
    wide = [ln1[0], ln1[1], vec["out_b"], vec["ln2_g"], vec["ln2_b"], vec["down_b"]]
    blocks = [v.reshape(n_seq, n_dp, -1) for v in wide + [vec["q_b"], vec["v_b"], vec["up_b"]]]
    sizes = [b.shape[2] for b in blocks]
    small = scatter_small(jnp.concatenate(blocks, axis=2))
    pieces, at = [], 0
    for size in sizes:
        pieces.append(small[at:at + size])
        at += size

    return (
        jnp.stack(outputs),
        jnp.stack(tokens_grads),
        pieces[0],
        pieces[1],
        qkv_grad,
        jnp.stack([pieces[6], pieces[7]]),
        out_grad.T,
        pieces[2],
        pieces[3],
        pieces[4],
        up_grad,
        pieces[8],
        down_grad.T,
        pieces[5],
    )


def solution(mesh):
    in_specs = (
        P("dp", "seq", None),
        P("dp", "seq"),
        P(),
        P(),
        P(None, None, "head"),
        P(None, "head"),
        P("head", None),
        P(),
        P(),
        P(),
        P(None, "head"),
        P("head"),
        P("head", None),
        P(),
        P("dp", "seq", None),
    )
    out_specs = (
        P("dp", "seq", None),
        P("dp", "seq", None),
        P(("seq", "dp")),
        P(("seq", "dp")),
        P(("seq", "dp"), None, "head"),
        P(None, ("head", "seq", "dp")),
        P("head", ("seq", "dp")),
        P(("seq", "dp")),
        P(("seq", "dp")),
        P(("seq", "dp")),
        P(("seq", "dp"), "head"),
        P(("head", "seq", "dp")),
        P("head", ("seq", "dp")),
        P(("seq", "dp")),
    )
    return jax.shard_map(shards, mesh=mesh, in_specs=in_specs, out_specs=out_specs, check_vma=False)
```

```python
import functools

import jax
import jax.numpy as jnp
from jax import lax
from jax.experimental import pallas as pl
from jax.experimental.pallas import tpu as pltpu
from jax.sharding import PartitionSpec as P

HEAD_DIM = 64
LANES = 128
EPSILON = 1e-05
MASKED = -1e30
F32 = jnp.float32
LOW = jnp.bfloat16
NN = (((1,), (0,)), ((), ()))
NT = (((1,), (1,)), ((), ()))
TN = (((0,), (0,)), ((), ()))
VMEM_LIMIT = 60 * 2**20


def dot(a, b, dims=NN):
    return lax.dot_general(a, b, dims, preferred_element_type=F32)


def axis_size(name):
    return lax.axis_size(name)


def swap(value, axis, mask):
    return lax.ppermute(value, axis, [(i, i ^ mask) for i in range(axis_size(axis))])


def bits_of(count):
    return [1 << b for b in range(count.bit_length() - 1)]


def layer_norm(inputs, gain, shift):
    center = jnp.mean(inputs, axis=-1, keepdims=True)
    centred = inputs - center
    spread = jnp.mean(centred * centred, axis=-1, keepdims=True)
    inverse = lax.rsqrt(spread + EPSILON)
    normed = centred * inverse
    return (normed * gain + shift, normed, inverse)


def norm_backward(upstream, normed, inverse, gain):
    scaled = upstream * gain
    centred = scaled - jnp.mean(scaled, axis=-1, keepdims=True)
    return inverse * (centred - normed * jnp.mean(scaled * normed, axis=-1, keepdims=True))


def gelu_pair(v):
    c = 0.7978845608028654
    square = v * v
    t = jnp.tanh(c * v * (1.0 + 0.044715 * square))
    half = 0.5 * (1.0 + t)
    return v * half, half + (0.5 * c) * v * (1.0 - t * t) * (1.0 + 3.0 * 0.044715 * square)


def half_lanes(shape, head):
    lane = lax.broadcasted_iota(jnp.int32, shape, 1)
    return (lane < HEAD_DIM) if head == 0 else (lane >= HEAD_DIM)


def attend_kernel(n, q_ref, seg_ref, segk_ref, *refs):
    kv_refs = refs[:n]
    w_ref, attn_ref, low_ref, inv_ref = refs[n:]
    q = q_ref[...] * jnp.asarray(0.125, LOW)
    seg_q = seg_ref[0:1, :]
    for head in range(2):
        qh = jnp.where(half_lanes(q.shape, head), q, jnp.zeros_like(q))
        parts, top = [], None
        for m in range(n):
            s = dot(kv_refs[m][0], qh, NT)
            s = jnp.where(segk_ref[m] == seg_q, s, MASKED)
            peak = jnp.max(s, axis=0, keepdims=True)
            top = peak if top is None else jnp.maximum(top, peak)
            parts.append(s)
        total, mixed = 0.0, 0.0
        for m in range(n):
            w = jnp.exp(parts[m] - top)
            total = total + jnp.sum(w, axis=0, keepdims=True)
            wl = w.astype(LOW)
            w_ref[head, m] = wl
            vt = kv_refs[m][1].T[head * HEAD_DIM:(head + 1) * HEAD_DIM, :]
            mixed = mixed + dot(vt, wl)
        inverse = 1.0 / total
        inv_ref[0, head:head + 1, :] = inverse
        attn_ref[head * HEAD_DIM:(head + 1) * HEAD_DIM, :] = mixed * inverse
    low_ref[...] = attn_ref[...].T.astype(LOW)


def attend(q, seg_rows, seg_cols, kvs):
    n, (rows, width) = len(kvs), q.shape
    pairs = width // LANES
    step = lambda p: (0, p)
    kv_spec = pl.BlockSpec((2, rows, LANES), lambda p: (0, 0, p))
    return pl.pallas_call(
        functools.partial(attend_kernel, n),
        grid=(pairs,),
        in_specs=[
            pl.BlockSpec((rows, LANES), step),
            pl.BlockSpec((8, rows), lambda p: (0, 0)),
            pl.BlockSpec((n, rows, 1), lambda p: (0, 0, 0)),
        ]
        + [kv_spec] * n,
        out_specs=[
            pl.BlockSpec((2, n, rows, rows), lambda p: (p, 0, 0, 0)),
            pl.BlockSpec((LANES, rows), lambda p: (p, 0)),
            pl.BlockSpec((rows, LANES), step),
            pl.BlockSpec((1, 2, rows), lambda p: (p, 0, 0)),
        ],
        out_shape=[
            jax.ShapeDtypeStruct((2 * pairs, n, rows, rows), LOW),
            jax.ShapeDtypeStruct((width, rows), F32),
            jax.ShapeDtypeStruct((rows, width), LOW),
            jax.ShapeDtypeStruct((pairs, 2, rows), F32),
        ],
        compiler_params=pltpu.CompilerParams(vmem_limit_bytes=VMEM_LIMIT),
        cost_estimate=pl.CostEstimate(
            flops=2 * pairs * n * rows * rows * 256 * 4,
            bytes_accessed=2 * pairs * n * rows * rows * 2,
            transcendentals=2 * pairs * n * rows * rows,
        ),
    )(q, seg_rows, seg_cols, *kvs)


def attend_back_kernel(n, q_ref, g_ref, attn_ref, inv_ref, w_ref, *refs):
    kv_refs = refs[:n]
    dq_ref = refs[n]
    dkv_refs = refs[n + 1:2 * n + 1]
    dqt_ref = refs[2 * n + 1]
    q = q_ref[...]
    gt = g_ref[...].astype(F32).T
    qs, gs, gts, deltas = [], [], [], []
    for head in range(2):
        rows_h = slice(head * HEAD_DIM, (head + 1) * HEAD_DIM)
        part = (gt[rows_h] * inv_ref[0, head:head + 1, :]).astype(LOW)
        deltas.append(jnp.sum(part.astype(F32) * attn_ref[rows_h, :], axis=0, keepdims=True))
        zeros = jnp.zeros_like(part)
        full = jnp.concatenate([part, zeros] if head == 0 else [zeros, part], axis=0)
        gts.append(full)
        gs.append(full.T)
        qs.append(jnp.where(half_lanes(q.shape, head), q, jnp.zeros_like(q)))
    dqt = [0.0, 0.0]
    for m in range(n):
        kt = kv_refs[m][0].T
        v = kv_refs[m][1]
        dk = dv = 0.0
        for head in range(2):
            w = w_ref[head, m]
            ds = (w.astype(F32) * (dot(v, gts[head]) - deltas[head])).astype(LOW)
            dk = dk + dot(ds, qs[head])
            dv = dv + dot(w, gs[head])
            dqt[head] = dqt[head] + dot(kt[head * HEAD_DIM:(head + 1) * HEAD_DIM, :], ds)
        dkv_refs[m][0] = (dk * 0.125).astype(LOW)
        dkv_refs[m][1] = dv.astype(LOW)
    dqt_ref[0:HEAD_DIM, :] = dqt[0]
    dqt_ref[HEAD_DIM:LANES, :] = dqt[1]
    dq_ref[...] = (dqt_ref[...].T * 0.125).astype(LOW)


def attend_back(q, g, attn, inverse, weights, kvs):
    n, (rows, width) = len(kvs), q.shape
    pairs = width // LANES
    step = lambda p: (0, p)
    kv_spec = pl.BlockSpec((2, rows, LANES), lambda p: (0, 0, p))
    out = pl.pallas_call(
        functools.partial(attend_back_kernel, n),
        grid=(pairs,),
        in_specs=[
            pl.BlockSpec((rows, LANES), step),
            pl.BlockSpec((rows, LANES), step),
            pl.BlockSpec((LANES, rows), lambda p: (p, 0)),
            pl.BlockSpec((1, 2, rows), lambda p: (p, 0, 0)),
            pl.BlockSpec((2, n, rows, rows), lambda p: (p, 0, 0, 0)),
        ]
        + [kv_spec] * n,
        out_specs=[pl.BlockSpec((rows, LANES), step)] + [kv_spec] * n,
        out_shape=[jax.ShapeDtypeStruct((rows, width), LOW)]
        + [jax.ShapeDtypeStruct((2, rows, width), LOW)] * n,
        scratch_shapes=[pltpu.VMEM((LANES, rows), F32)],
        compiler_params=pltpu.CompilerParams(vmem_limit_bytes=VMEM_LIMIT),
        cost_estimate=pl.CostEstimate(
            flops=2 * pairs * n * rows * rows * 256 * 8,
            bytes_accessed=2 * pairs * n * rows * rows * 2,
            transcendentals=0,
        ),
    )(q, g, attn, inverse, weights, *kvs)
    return out[0], out[1:]


def gather_seq(block):
    bits = bits_of(axis_size("seq"))
    blocks = {0: block}
    for bit in reversed(bits):
        for m in list(blocks):
            blocks[m | bit] = swap(blocks[m], "seq", bit)
    return [blocks[m] for m in range(len(blocks))]


def scatter_seq(parts):
    parts = dict(enumerate(parts))
    for bit in bits_of(axis_size("seq")):
        for m in [m for m in sorted(parts, reverse=True) if m & bit]:
            got = swap(parts.pop(m).astype(LOW), "seq", bit)
            parts[m ^ bit] = parts[m ^ bit].astype(F32) + got.astype(F32)
    return parts[0].astype(F32)


def scatter_line(term):
    n = axis_size("dp")
    me = lax.axis_index("dp")
    rows = term.shape[0] // n
    block = lambda i: lax.dynamic_slice_in_dim(term, jnp.clip(i, 0, n - 1) * rows, rows, 0)
    up = down = None
    for k in range(n - 1, 0, -1):
        send_up = block(me + k) if up is None else block(me + k) + up
        send_down = block(me - k) if down is None else block(me - k) + down
        up = lax.ppermute(
            send_up.astype(LOW), "dp", [(i, i + 1) for i in range(n) if i + k < n]
        ).astype(F32)
        down = lax.ppermute(
            send_down.astype(LOW), "dp", [(i, i - 1) for i in range(n) if i - k >= 0]
        ).astype(F32)
    out = block(me)
    return out if n == 1 else out + up + down


def relative_columns(rows):
    n = axis_size("seq")
    me = lax.axis_index("seq")
    width = rows.shape[1] // n
    return [lax.dynamic_slice_in_dim(rows, (me ^ m) * width, width, 1) for m in range(n)]


def weight_grad(left, right):
    return scatter_line(scatter_seq([dot(part, right, TN) for part in left]))


def scatter_small(blocks):
    for axis in ("seq", "dp"):
        n = axis_size(axis)
        me = lax.axis_index(axis)
        bits = bits_of(n)
        rest = blocks.shape[1:]
        for bit in reversed(bits):
            low, high = blocks[:bit], blocks[bit:]
            mine = (me & bit) != 0
            send = jnp.where(mine, low, high)
            blocks = jnp.where(mine, high, low) + swap(send, axis, bit)
        blocks = blocks.reshape(rest)
    return blocks


def other_head(value):
    return swap(value, "head", 1)


def head_sum(value):
    value = value.astype(LOW)
    return value.astype(F32) + other_head(value).astype(F32)


def by_head(mine, other, axis):
    first = lax.axis_index("head") == 0
    return jnp.where(
        first,
        jnp.concatenate([mine, other], axis),
        jnp.concatenate([other, mine], axis),
    )


MESH = pl.DeviceIdType.MESH
CHUNK = 32
WIDE = 512


def loop(count, body, unroll=1, start=0):
    def step(i, carry):
        body(i)
        return carry

    lax.fori_loop(start, start + count, step, 0, unroll=unroll)


def span(i, size):
    return pl.ds(pl.multiple_of(i * size, size), size)


def fold(value):
    return jnp.sum(value.reshape(value.shape[0] // 8, 8, value.shape[1]), axis=0)


class Copy:
    def __init__(self, copy, remote):
        self.copy, self.remote = copy, remote
        self.sent = self.got = False

    def wait_recv(self):
        if not self.got:
            self.got = True
            if self.remote:
                self.copy.wait_recv()
            else:
                self.copy.wait()

    def wait_send(self):
        if self.remote and not self.sent:
            self.copy.wait_send()
        self.sent = True

    def wait(self):
        self.wait_send()
        self.wait_recv()


class Copies:
    def __init__(self, send, recv, local):
        self.sems, self.all = (send, recv, local), []
        self.n_remote = self.n_local = 0

    def start(self, src, dst, device):
        copy = pltpu.make_async_remote_copy(
            src_ref=src,
            dst_ref=dst,
            send_sem=self.sems[0].at[self.n_remote],
            recv_sem=self.sems[1].at[self.n_remote],
            device_id=device,
            device_id_type=MESH,
        )
        self.n_remote += 1
        return self.begin(copy, True)

    def load(self, src, dst):
        copy = pltpu.make_async_copy(src, dst, self.sems[2].at[self.n_local])
        self.n_local += 1
        return self.begin(copy, False)

    def begin(self, copy, remote):
        copy.start()
        self.all.append(Copy(copy, remote))
        return self.all[-1]

    def finish(self):
        for copy in self.all:
            copy.wait()


N_COPIES = 128
N_LOCAL = 24


def layer_kernel(n_dp, *refs):
    (
        tok_h, seg_in, g1, b1, wqkv_h, qvb, outw_h, outb, g2, b2, up_h, upb, down_h, downb, cot_h,
        out_h, tg_h, downg_h, upg_h, outg_h, qkvg_h, vec_o,
        tok, cot, wqkv, outw, up, down, q, kv, attn_t, attn, mid, lnb, act, gh,
        first_t, second_t, cot_t, gb_t, g_attn, gs, ffn, stat, st,
        gs_r, ffn_r, gf_r, dkv_r, q_far, g_far, st_far, act_r, gh_r, first_r, second_r, cot_r, gb_r, heads_r, dqkv_r,
        xr, zr, xz, zz,
        segs, segk, vec, qvacc, upacc, ln1_r, vs, vr,
        send, recv, local,
    ) = refs
    rows = tok.shape[0] // 2
    width = tok.shape[1]
    heads_w = q.shape[1]
    hidden = act.shape[1]
    pairs = heads_w // LANES
    quarter = width // 4
    block = quarter // n_dp
    s = lax.axis_index("seq")
    h = lax.axis_index("head")
    z = lax.axis_index("dp")
    x, core = s // 2, s % 2
    seq_peer = [None] + [((x ^ (m >> 1)) * 2 + (core ^ (m & 1)), h, z) for m in (1, 2, 3)]
    across = (s, 1 - h, z)
    next_z, far_z = z + 1 - 2 * lax.rem(z, 2), lax.rem(z + 2, 4)
    beside, beyond = (s, h, next_z), (s, h, far_z)
    half_w = heads_w // 2
    copies = Copies(send, recv, local)
    load = copies.load

    own_out = pl.ds(pl.multiple_of(h * heads_w, heads_w), heads_w)
    get_tok = load(tok_h, tok)
    get_qkv = load(wqkv_h, wqkv)

    barrier = pltpu.get_barrier_semaphore()
    partners = seq_peer[1:] + [across, beside, beyond]
    for device in partners:
        pl.semaphore_signal(barrier, inc=1, device_id=device, device_id_type=MESH)

    vec[...] = jnp.zeros_like(vec)
    qvacc[...] = jnp.zeros_like(qvacc)
    upacc[...] = jnp.zeros_like(upacc)
    segs[0] = jnp.zeros_like(segs[0])
    segs[0, 0:2, :] = seg_in[...]
    def seq_rows(i):
        return slice(i * rows, (i + 1) * rows)

    def flip(src, i, dst):
        def part(c):
            dst[span(c, 256), seq_rows(i)] = src[:, span(c, 256)].T

        loop(width // 256, part)

    def swap_rows(flipped, target):
        return [
            copies.start(
                flipped.at[pl.ds(pl.multiple_of(c * 2 * quarter + (1 - core) * quarter, quarter), quarter), :],
                target.at[c],
                seq_peer[1],
            )
            for c in range(2)
        ]

    kv_got = [[[None] * 2 for _ in range(4)] for _ in range(2)]
    q_got, q_next = [None] * 2, [None] * 2

    def first_norm(i):
        def norm(c):
            at = pl.ds(pl.multiple_of(i * rows + c * CHUNK, CHUNK), CHUNK)
            v = tok[at, :].astype(F32)
            center = jnp.mean(v, axis=-1, keepdims=True)
            v = v - center
            inverse = lax.rsqrt(jnp.mean(v * v, axis=-1, keepdims=True) + EPSILON)
            stat[0, at, 0:1] = center
            stat[0, at, 1:2] = inverse
            lnb[i, span(c, CHUNK), :] = (v * inverse * g1[...] + b1[...]).astype(LOW)

        loop(rows // CHUNK, norm, 4)

    def keys_values(i, part):
        cols = slice(part * half_w, (part + 1) * half_w)
        kv[i, 0, part, :, 0:half_w] = dot(lnb[i], wqkv[1, :, cols]).astype(LOW)
        kv[i, 0, part, :, half_w:heads_w] = (dot(lnb[i], wqkv[2, :, cols]) + qvb[1:2, cols]).astype(LOW)

    def send_keys(i, part):
        for m in (2, 1):
            kv_got[i][m][part] = copies.start(kv.at[i, 0, part], kv.at[i, m, part], seq_peer[m])

    def queries(i):
        q[seq_rows(i), :] = (dot(lnb[i], wqkv[0]) + qvb[0:1, :]).astype(LOW)
        q_got[i] = copies.start(q.at[seq_rows(i), :], q_far.at[i, 0], seq_peer[2])
        flip(lnb.at[i], i, first_t)

    seg_got = [None] * 4

    def meet():
        pl.semaphore_wait(barrier, len(partners))
        for m in (1, 2, 3):
            seg_got[m] = copies.start(segs.at[0], segs.at[m], seq_peer[m])

    def key_lanes(p):
        lane = lax.rem(p, 2) * LANES
        return p // 2, pl.ds(pl.multiple_of(lane, LANES), LANES), pl.ds(pl.multiple_of(half_w + lane, LANES), LANES)

    def twice(row):
        return jnp.concatenate([row, row], axis=1)

    def both(stats, k):
        return jnp.concatenate([stats[k:k + 1, :], stats[k + 1:k + 2, :]], axis=1)

    def cols_of(head):
        return slice(head * rows, (head + 1) * rows)

    def heads_of(pair_value, scale=None):
        if scale is not None:
            pair_value = pair_value * jnp.asarray(scale, LOW)
        zeros = jnp.zeros_like(pair_value)
        return [jnp.where(half_lanes(pair_value.shape, head), pair_value, zeros) for head in range(2)]

    def attend_blocks(i, blocks, begin, end, start, stop):
        seg_q = twice(segs[0, i:i + 1, :].astype(F32))

        def pair(p):
            lanes = span(p, LANES)
            part, k_lanes, v_lanes = key_lanes(p)
            qs = jnp.concatenate(heads_of(q[seq_rows(i), lanes], 0.125), axis=0)
            old = top = None if begin else both(st[i, p], 0)
            scores = []
            for m in blocks:
                score = dot(kv[i, m, part, :, k_lanes], qs, NT)
                score = jnp.where(segk[m, :, i:i + 1] == seg_q, score, MASKED)
                peak = jnp.max(score, axis=0, keepdims=True)
                top = peak if top is None else jnp.maximum(top, peak)
                scores.append(score)
            total, mixed = 0.0, [0.0, 0.0]
            for m, score in zip(blocks, scores):
                w = jnp.exp(score - top)
                total = total + jnp.sum(w, axis=0, keepdims=True)
                low = w.astype(LOW)
                vt = kv[i, m, part, :, v_lanes].T
                for head in range(2):
                    mixed[head] = mixed[head] + dot(vt[head * HEAD_DIM:(head + 1) * HEAD_DIM, :], low[:, cols_of(head)])
            if not begin:
                scale = jnp.exp(old - top)
                total = total + scale * both(st[i, p], 2)
            if end:
                inverse, lse = 1.0 / total, top + jnp.log(total)
            for head in range(2):
                at = pl.ds(pl.multiple_of(p * LANES + head * HEAD_DIM, HEAD_DIM), HEAD_DIM)
                value = mixed[head]
                if not begin:
                    value = value + scale[:, cols_of(head)] * attn_t[i, at, :]
                if end:
                    value = value * inverse[:, cols_of(head)]
                    st[i, p, 4 + head:5 + head, :] = lse[:, cols_of(head)]
                else:
                    st[i, p, head:head + 1, :] = top[:, cols_of(head)]
                    st[i, p, 2 + head:3 + head, :] = total[:, cols_of(head)]
                attn_t[i, at, :] = value
            if end:
                to = pl.ds(pl.multiple_of(h * heads_w + p * LANES, LANES), LANES)
                attn[seq_rows(i), to] = attn_t[i, lanes, :].T.astype(LOW)

        lax.fori_loop(start, stop, lambda p, c: (pair(p), c)[1], 0)

    def seg_columns(m):
        segk[m] = segs[m].astype(F32).T

    own_heads = pl.ds(pl.multiple_of(h * heads_w, heads_w), heads_w)
    attn_got = [[], []]

    def forward_keys(i, part):
        kv_got[i][2][part].wait_recv()
        kv_got[i][3][part] = copies.start(kv.at[i, 2, part], kv.at[i, 3, part], seq_peer[1])

    def forward_queries(i):
        q_got[i].wait_recv()
        q_next[i] = copies.start(q_far.at[i, 0], q_far.at[i, 1], seq_peer[1])

    def attend_far(i, part):
        kv_got[i][3][part].wait_recv()
        attend_blocks(i, (2, 3), False, True, part * pairs // 2, (part + 1) * pairs // 2)

    def send_heads(i, part):
        to = pl.ds(pl.multiple_of(h * heads_w + part * half_w, half_w), half_w)
        mine = attn.at[seq_rows(i), to]
        attn_got[i].append(copies.start(mine, mine, across))
        there = heads_r.at[seq_rows(i), part * half_w:(part + 1) * half_w]
        heads_sent.append(copies.start(mine, there, seq_peer[1]))

    heads_sent = []

    def middle(i):
        for copy in attn_got[i]:
            copy.wait_recv()

        def tile(j):
            at = span(j, WIDE)
            mid[seq_rows(i), at] = (
                dot(attn[seq_rows(i), :], outw[:, at])
                + tok[seq_rows(i), at].astype(F32)
                + outb[:, at]
            )

        loop(width // WIDE, tile)

        def norm(c):
            at = pl.ds(pl.multiple_of(i * rows + c * CHUNK, CHUNK), CHUNK)
            v = mid[at, :]
            center = jnp.mean(v, axis=-1, keepdims=True)
            v = v - center
            inverse = lax.rsqrt(jnp.mean(v * v, axis=-1, keepdims=True) + EPSILON)
            stat[1, at, 0:1] = center
            stat[1, at, 1:2] = inverse
            lnb[i, span(c, CHUNK), :] = (v * inverse * g2[...] + b2[...]).astype(LOW)

        loop(rows // CHUNK, norm, 4)

    gs_got, ffn_got = [None] * 2, [None] * 2
    act_got, gh_got = [[None] * 2, [None] * 2], [[None] * 2, [None] * 2]

    def cot_down(i):
        def tile(j):
            at = span(j, 2 * WIDE)
            gh[seq_rows(i), at] = dot(cot[seq_rows(i), :], down[at, :], NT).astype(LOW)

        loop(hidden // (2 * WIDE), tile)

    def feed(i, part):
        at_rows = seq_rows(i)

        def tile(j):
            at = span(j, WIDE)
            value, slope = gelu_pair(dot(lnb[i], up[:, at]) + upb[:, at])
            act[at_rows, at] = value.astype(LOW)
            g = (gh[at_rows, at].astype(F32) * slope).astype(LOW)
            gh[at_rows, at] = g
            upacc[:, at] += fold(g.astype(F32))

        tiles_each = hidden // WIDE // 2
        loop(tiles_each, tile, 1, part * tiles_each)
        cols = slice(part * hidden // 2, (part + 1) * hidden // 2)
        act_got[i][part] = copies.start(act.at[at_rows, cols], act_r.at[at_rows, cols], seq_peer[1])
        gh_got[i][part] = copies.start(gh.at[at_rows, cols], gh_r.at[at_rows, cols], seq_peer[1])

    def feed_back(i):
        at_rows = seq_rows(i)

        def back(j):
            gs[at_rows, span(j, WIDE)] = dot(gh[at_rows, :], up[span(j, WIDE), :], NT).astype(LOW)

        loop(width // WIDE, back)
        gs_got[i] = copies.start(gs.at[at_rows, :], gs_r.at[at_rows, :], across)
        flip(lnb.at[i], i, second_t)

    def feed_out(i):
        at_rows = seq_rows(i)

        def tile(j):
            ffn[at_rows, span(j, WIDE)] = dot(act[at_rows, :], down[:, span(j, WIDE)]).astype(LOW)

        loop(width // WIDE, tile)

    def send_feed_out(i):
        ffn_got[i] = copies.start(ffn.at[seq_rows(i), :], ffn_r.at[seq_rows(i), :], across)

    def finish_output(i):
        ffn_got[i].wait()

        def part(c):
            at = pl.ds(pl.multiple_of(i * rows + c * CHUNK, CHUNK), CHUNK)
            both = ffn[at, :].astype(F32) + ffn_r[at, :].astype(F32)
            ffn[at, :] = (mid[at, :] + both + downb[...]).astype(LOW)

        loop(rows // CHUNK, part, 4)
        load(ffn.at[seq_rows(i), :], out_h.at[seq_rows(i), :])

    gb = down.at[2 * rows:4 * rows, :]
    parts_kv = [[down.at[(4 + 2 * i + m) * rows:(5 + 2 * i + m) * rows, :] for m in range(2)] for i in range(2)]
    dqkv = up.at[2 * rows:4 * rows, :]

    def norm2_back(i):
        gs_got[i].wait_recv()

        def part(c):
            at = pl.ds(pl.multiple_of(i * rows + c * CHUNK, CHUNK), CHUNK)
            g = gs[at, :].astype(F32) + gs_r[at, :].astype(F32)
            inverse = stat[1, at, 1:2]
            normed = (mid[at, :] - stat[1, at, 0:1]) * inverse
            vec[3] += fold(g * normed)
            vec[4] += fold(g)
            e = g * g2[...]
            e = e - jnp.mean(e, axis=-1, keepdims=True) - normed * jnp.mean(e * normed, axis=-1, keepdims=True)
            low = (cot[at, :].astype(F32) + inverse * e).astype(LOW)
            gb[at, :] = low
            vec[2] += fold(low.astype(F32))

        loop(rows // CHUNK, part, 4)

        w_rows = pl.ds(pl.multiple_of(h * heads_w, heads_w), heads_w)
        g_attn[i] = dot(gb[seq_rows(i), :], outw[w_rows, :], NT).astype(LOW)

        def delta(p):
            g = g_attn[i, :, span(p, LANES)].astype(F32).T
            each = g * attn_t[i, span(p, LANES), :]
            for head in range(2):
                part = each[head * HEAD_DIM:(head + 1) * HEAD_DIM, :]
                st[i, p, 6 + head:7 + head, :] = jnp.sum(part, axis=0, keepdims=True)

        loop(pairs, delta)
        g_got[i] = [
            copies.start(g_attn.at[i], g_far.at[i, 0], seq_peer[2]),
            copies.start(st.at[i], st_far.at[i, 0], seq_peer[2]),
        ]

    g_got, g_next = [None] * 2, [None] * 2

    def forward_grads(i):
        for copy in g_got[i]:
            copy.wait_recv()
        g_next[i] = [
            copies.start(g_far.at[i, 0], g_far.at[i, 1], seq_peer[1]),
            copies.start(st_far.at[i, 0], st_far.at[i, 1], seq_peer[1]),
        ]

    def backward_terms(allowed, k, v, q_scaled, g, lse, delta):
        probs = jnp.exp(jnp.where(allowed, dot(k, q_scaled, NT) - lse, MASKED))
        return probs.astype(LOW), (probs * (dot(v, g, NT) - delta)).astype(LOW)

    def back_own(i):
        seg_q = twice(segs[0, i:i + 1, :].astype(F32))

        def pair(p):
            lanes = span(p, LANES)
            v_lanes = pl.ds(pl.multiple_of(heads_w + p * LANES, LANES), LANES)
            part, k_in, v_in = key_lanes(p)
            qs = jnp.concatenate(heads_of(q[seq_rows(i), lanes]), axis=0)
            q_scaled = qs * jnp.asarray(0.125, LOW)
            g = jnp.concatenate(heads_of(g_attn[i, :, lanes]), axis=0)
            lse, delta = both(st[i, p], 4), both(st[i, p], 6)
            dqt = [0.0, 0.0]
            for m in range(4):
                k = kv[i, m, part, :, k_in]
                kt = k.T
                v = kv[i, m, part, :, v_in]
                probs, ds = backward_terms(segk[m, :, i:i + 1] == seg_q, k, v, q_scaled, g, lse, delta)
                if m < 2:
                    parts_kv[i][m][:, lanes] = (dot(ds, qs) * 0.125).astype(LOW)
                    parts_kv[i][m][:, v_lanes] = dot(probs, g).astype(LOW)
                for head in range(2):
                    dqt[head] = dqt[head] + dot(kt[head * HEAD_DIM:(head + 1) * HEAD_DIM, :], ds[:, cols_of(head)])
            dq = (jnp.concatenate(dqt, axis=0).T * 0.125).astype(LOW)
            dqkv[seq_rows(i), lanes] = dq
            qvacc[:, lanes] += fold(dq.astype(F32))

        loop(pairs, pair)
        near_got[i] = copies.start(parts_kv[i][1], dkv_r.at[i], seq_peer[1])
        at = (seq_rows(i), pl.ds(0, heads_w))
        dq_got[i] = copies.start(dqkv.at[at], dqkv_r.at[at], seq_peer[1])

    def back_far(i):
        q_next[i].wait_recv()
        for copy in g_next[i]:
            copy.wait_recv()
        near_got[i].wait_recv()
        seg_q = [twice(segs[2 + b, i:i + 1, :].astype(F32)) for b in range(2)]
        at_rows = seq_rows(i)

        def pair(p):
            lanes = span(p, LANES)
            v_lanes = pl.ds(pl.multiple_of(heads_w + p * LANES, LANES), LANES)
            part, k_in, v_in = key_lanes(p)
            k = kv[i, 0, part, :, k_in]
            v = kv[i, 0, part, :, v_in]
            dk = dv = 0.0
            for b in range(2):
                qs = jnp.concatenate(heads_of(q_far[i, b, :, lanes]), axis=0)
                q_scaled = qs * jnp.asarray(0.125, LOW)
                g = jnp.concatenate(heads_of(g_far[i, b, :, lanes]), axis=0)
                lse, delta = both(st_far[i, b, p], 4), both(st_far[i, b, p], 6)
                probs, ds = backward_terms(segk[0, :, i:i + 1] == seg_q[b], k, v, q_scaled, g, lse, delta)
                dk = dk + dot(ds, qs)
                dv = dv + dot(probs, g)
            near = lambda to: parts_kv[i][0][:, to].astype(F32) + dkv_r[i, :, to].astype(F32)
            k_at = pl.ds(pl.multiple_of(heads_w + p * LANES, LANES), LANES)
            v_at = pl.ds(pl.multiple_of(2 * heads_w + p * LANES, LANES), LANES)
            dqkv[at_rows, k_at] = (dk * 0.125 + near(lanes)).astype(LOW)
            low = (dv + near(v_lanes)).astype(LOW)
            dqkv[at_rows, v_at] = low
            qvacc[:, k_at] += fold(low.astype(F32))

        loop(pairs, pair)
        at = (at_rows, kv_cols)
        dkv_got[i] = copies.start(dqkv.at[at], dqkv_r.at[at], seq_peer[1])

    near_got, dq_got = [None] * 2, [None] * 2
    kv_cols = pl.ds(heads_w, 2 * heads_w)

    dkv_got, gf_got = [None] * 2, [None] * 2

    def first_back(i):
        gs_got[i].wait_send()

        def tile(j):
            at = span(j, WIDE)
            total = 0.0
            for c in range(3):
                total = total + dot(dqkv[seq_rows(i), c * heads_w:(c + 1) * heads_w], wqkv[c, at, :], NT)
            gs[seq_rows(i), at] = total.astype(LOW)

        loop(width // WIDE, tile)
        def sums(c):
            at = pl.ds(pl.multiple_of(i * rows + c * CHUNK, CHUNK), CHUNK)
            g = gs[at, :].astype(F32)
            normed = (tok[at, :].astype(F32) - stat[0, at, 0:1]) * stat[0, at, 1:2]
            vec[0] += fold(g * normed)
            vec[1] += fold(g)

        loop(rows // CHUNK, sums, 4)

    def send_first_back(i):
        gf_got[i] = copies.start(gs.at[seq_rows(i), :], gf_r.at[seq_rows(i), :], across)

    def norm1_back(i):
        gf_got[i].wait()

        def part(c):
            at = pl.ds(pl.multiple_of(i * rows + c * CHUNK, CHUNK), CHUNK)
            g = gs[at, :].astype(F32) + gf_r[at, :].astype(F32)
            inverse = stat[0, at, 1:2]
            normed = (tok[at, :].astype(F32) - stat[0, at, 0:1]) * inverse
            e = g * g1[...]
            e = e - jnp.mean(e, axis=-1, keepdims=True) - normed * jnp.mean(e * normed, axis=-1, keepdims=True)
            gs[at, :] = (gb[at, :].astype(F32) + inverse * e).astype(LOW)

        loop(rows // CHUNK, part, 4)
        load(gs.at[seq_rows(i), :], tg_h.at[seq_rows(i), :])

    def tiles(piece, chip, body):
        left, left_r, right, right_r, cols = piece
        at_rows = pl.ds(pl.multiple_of(chip * 2 * quarter + core * quarter, quarter), quarter)
        step = min(cols, 2 * WIDE)

        def tile(j):
            at = span(j, step)
            body(at, dot(left[at_rows, :], right[:, at]) + dot(left_r[chip], right_r[:, at]))

        loop(cols // step, tile)

    def block_rows(index):
        return pl.ds(pl.multiple_of(index * block, block), block)

    def send_beside(hold, arrive):
        further = lax.rem(next_z + 2, 4)
        return [
            copies.start(hold.at[block_rows(next_z), :], arrive[0], beside),
            copies.start(hold.at[block_rows(further), :], arrive[1], beside),
        ]

    def send_beyond(hold, arrive):
        at = block_rows(far_z)
        hold[at, :] = (hold[at, :].astype(F32) + arrive[1][...].astype(F32)).astype(LOW)
        return copies.start(hold.at[at, :], arrive[2], beyond)

    def own_block(hold, arrive, at=slice(None)):
        total = hold[block_rows(z), at].astype(F32)
        return total + arrive[0][:, at].astype(F32) + arrive[2][:, at].astype(F32)

    def hand_out(place, target, value):
        size = target.shape[1]
        top, left = place // 4 * block, place % 4 * (width // 4)
        mid[top:top + block, left:left + size] = value(slice(None))
        load(mid.at[top:top + block, left:left + size], target)
        return place + size * 4 // width

    class AcrossFirst:
        def __init__(self, piece, hold, offset, arrivals):
            self.piece, self.hold, self.arrivals = piece, hold, arrivals
            cols = pl.ds(offset, piece[4])
            self.xr = xr.at[:, cols]
            self.zr = [zr.at[d, :, cols] for d in range(3)]

        def prepare(self):
            for copy in self.arrivals():
                copy.wait_recv()

            def keep(at, value):
                self.hold[:, at] = value.astype(LOW)

            tiles(self.piece, 1 - x, keep)

        def across(self):
            self.far = copies.start(self.hold, self.xr, seq_peer[2])

        def beside(self):
            self.far.wait()

            def keep(at, value):
                self.hold[:, at] = (value + self.xr[:, at].astype(F32)).astype(LOW)

            tiles(self.piece, x, keep)
            self.near = send_beside(self.hold, self.zr)

        def beyond(self):
            for copy in self.near:
                copy.wait_recv()
            self.last = send_beyond(self.hold, self.zr)

        def done(self, place, target):
            self.last.wait_recv()
            return hand_out(place, target, lambda at: own_block(self.hold, self.zr, at))

    class AlongFirst:
        def __init__(self, piece, holds, offset, arrivals):
            self.piece, self.holds, self.arrivals = piece, holds, arrivals
            cols = pl.ds(offset, piece[4])
            self.zz = [[zz.at[r, d, :, cols] for d in range(3)] for r in range(2)]
            self.xz = xz.at[:, cols]

        def beside(self):
            for copy in self.arrivals():
                copy.wait_recv()
            self.near = []
            for r in (1, 0):

                def keep(at, value, r=r):
                    self.holds[r][:, at] = value.astype(LOW)

                tiles(self.piece, x ^ r, keep)
                self.near += send_beside(self.holds[r], self.zz[r])

        def beyond(self):
            for copy in self.near:
                copy.wait_recv()
            self.last = [send_beyond(self.holds[r], self.zz[r]) for r in (1, 0)]

        def across(self):
            for copy in self.last:
                copy.wait_recv()
            mine = block_rows(z)
            self.holds[1][mine, :] = own_block(self.holds[1], self.zz[1]).astype(LOW)
            self.far = copies.start(self.holds[1].at[mine, :], self.xz, seq_peer[2])

        def done(self, place, target):
            self.far.wait_recv()

            def value(at):
                return own_block(self.holds[0], self.zz[0], at) + self.xz[:, at].astype(F32)

            return hand_out(place, target, value)

    attn_own = attn.at[:, own_heads]
    q_cols, k_cols, v_cols = (slice(c * heads_w, (c + 1) * heads_w) for c in range(3))
    flips = {}
    down_piece = lambda at, n: (cot_t, cot_r, act.at[:, at:at + n], act_r.at[:, at:at + n], n)
    up_piece = lambda at, n: (second_t, second_r, gh.at[:, at:at + n], gh_r.at[:, at:at + n], n)
    proj_piece = lambda at, n: (first_t, first_r, dqkv.at[:, at], dqkv_r.at[:, at], n)
    quarter_h = hidden // 4
    halves_of = lambda got, at: [got[i][at // (2 * quarter_h)] for i in range(2)]
    from_cot = lambda at: lambda: flips["cot"] + halves_of(act_got, at)
    from_second = lambda at: lambda: flips["second"] + halves_of(gh_got, at)
    spans = [(0, 2 * quarter_h), (2 * quarter_h, quarter_h), (3 * quarter_h, quarter_h)]
    downs = [
        AcrossFirst(down_piece(at, n), lnb.at[0] if k == 0 else up.at[0:rows, at:at + n], at, from_cot(at))
        for k, (at, n) in enumerate(spans)
    ]
    ups = [
        AlongFirst(
            up_piece(at, n),
            [up.at[rows:2 * rows, at:at + n], up.at[0:rows, 0:n] if k == 0 else lnb.at[1, :, 0:n]],
            at,
            from_second(at),
        )
        for k, (at, n) in enumerate(spans[:2])
    ]
    up_last = AcrossFirst(
        up_piece(3 * quarter_h, quarter_h), up.at[rows:2 * rows, 3 * quarter_h:hidden], hidden, from_second(3 * quarter_h)
    )
    base = hidden + quarter_h
    proj_out = AcrossFirst(
        (gb_t, gb_r, attn_own, heads_r, heads_w),
        down.at[0:rows, 0:heads_w],
        base,
        lambda: flips["gb"] + heads_sent,
    )
    proj_q = AcrossFirst(
        proj_piece(q_cols, heads_w),
        down.at[0:rows, heads_w:2 * heads_w],
        base + heads_w,
        lambda: flips["first"] + dq_got,
    )
    from_proj = lambda: flips["first"] + dkv_got
    proj_k = AcrossFirst(
        proj_piece(k_cols, heads_w), down.at[rows:2 * rows, 0:heads_w], base + 2 * heads_w, from_proj
    )
    v_halves = [slice(heads_w + c * half_w, heads_w + (c + 1) * half_w) for c in range(2)]
    proj_v = [
        AcrossFirst(
            proj_piece(slice(heads_w + at.start, heads_w + at.stop), half_w),
            down.at[rows:2 * rows, at],
            base + 2 * heads_w + at.start,
            from_proj,
        )
        for at in v_halves
    ]

    def share_out():
        half = heads_w // 2
        get_out.wait()
        mine = pl.ds(pl.multiple_of(h * heads_w + core * half, half), half)
        return copies.start(outw.at[mine, :], outw.at[mine, :], across)

    def forward_out():
        out_got.wait_recv()
        half = heads_w // 2
        theirs = pl.ds(pl.multiple_of((1 - h) * heads_w + core * half, half), half)
        return copies.start(outw.at[theirs, :], outw.at[theirs, :], seq_peer[1])

    def scenes():
        for m in (1, 2, 3):
            seg_got[m].wait_recv()
        for m in range(4):
            seg_columns(m)

    def attend_near(i):
        for copy in kv_got[i][1]:
            copy.wait_recv()
        attend_blocks(i, (0, 1), True, False, 0, pairs)

    def prepare_cot():
        get_cot.wait()

        def part(c):
            vec[5] += fold(cot[span(c, CHUNK), :].astype(F32))

        loop(2 * rows // CHUNK, part, 4)
        for i in range(2):
            flip(cot.at[seq_rows(i), :], i, cot_t)
        flips["cot"] = swap_rows(cot_t, cot_r)

    def flip_branch():
        for i in range(2):
            flip(gb.at[seq_rows(i), :], i, gb_t)
        flips["gb"] = swap_rows(gb_t, gb_r)

    def vectors():
        ln1_got.wait_recv()
        lines = [jnp.sum(vec[k] + ln1_r[k], axis=0, keepdims=True) for k in range(2)]
        lines += [jnp.sum(vec[k], axis=0, keepdims=True) for k in range(2, 6)]
        lines += [jnp.sum(qvacc[...], axis=0, keepdims=True)]
        sums = jnp.sum(upacc[...], axis=0, keepdims=True)
        lines += [sums[:, c * width:(c + 1) * width] for c in range(hidden // width)]
        lines += [jnp.zeros((16 - len(lines), width), F32)]
        vs[0] = jnp.concatenate(lines, axis=0)
        return copies.start(vs.at[0], vr.at[0], seq_peer[1])

    def vectors_on(k, copy, device):
        copy.wait_recv()
        vs[k] = vs[k - 1] + vr[k - 1]
        return copies.start(vs.at[k], vr.at[k], device)

    def vectors_done():
        vec_4.wait_recv()
        vec_o[...] = vs[3] + vr[3]

    get_tok.wait()
    first_norm(0)
    get_qkv.wait()
    keys_values(0, 0)
    meet()
    send_keys(0, 0)
    keys_values(0, 1)
    send_keys(0, 1)
    get_out, get_cot = load(outw_h, outw.at[own_out, :]), load(cot_h, cot)
    get_down, get_up = load(down_h, down), load(up_h, up)
    first_norm(1)
    keys_values(1, 0)
    send_keys(1, 0)
    keys_values(1, 1)
    send_keys(1, 1)
    queries(0)
    queries(1)
    flips["first"] = swap_rows(first_t, first_r)
    out_got = share_out()
    scenes()
    attend_near(0)
    attend_near(1)
    forward_keys(0, 0)
    prepare_cot()
    forward_keys(0, 1)
    attend_far(0, 0)
    send_heads(0, 0)
    attend_far(0, 1)
    send_heads(0, 1)
    out_near = forward_out()
    get_down.wait()
    cot_down(0)
    forward_keys(1, 0)
    cot_down(1)
    attend_far(1, 0)
    send_heads(1, 0)
    forward_keys(1, 1)
    attend_far(1, 1)
    send_heads(1, 1)
    out_near.wait_recv()
    get_up.wait()
    middle(0)
    feed(0, 0)
    feed(0, 1)
    feed_back(0)
    middle(1)
    feed(1, 0)
    feed(1, 1)
    downs[0].prepare()
    downs[0].across()
    feed_back(1)
    flips["second"] = swap_rows(second_t, second_r)
    ups[0].beside()
    ups[1].beside()
    feed_out(0)
    send_feed_out(0)
    feed_out(1)
    forward_queries(0)
    forward_queries(1)
    norm2_back(0)
    downs[1].prepare()
    downs[1].across()
    back_own(0)
    ups[0].beyond()
    norm2_back(1)
    downs[0].beside()
    forward_grads(0)
    downs[2].prepare()
    downs[2].across()
    flip_branch()
    back_far(0)
    ups[1].beyond()
    first_back(0)
    send_first_back(0)
    proj_out.prepare()
    proj_out.across()
    up_last.prepare()
    up_last.across()
    back_own(1)
    forward_grads(1)
    downs[1].beside()
    downs[2].beside()
    downs[0].beyond()
    back_far(1)
    first_back(1)
    ln1_got = copies.start(vec.at[0:2], ln1_r, across)
    send_first_back(1)
    send_feed_out(1)
    proj_q.prepare()
    proj_q.across()
    proj_k.prepare()
    proj_k.across()
    proj_v[0].prepare()
    proj_v[0].across()
    proj_v[1].prepare()
    proj_v[1].across()
    proj_out.beside()
    norm1_back(0)
    downs[1].beyond()
    downs[2].beyond()
    finish_output(0)
    vec_1 = vectors()
    up_last.beside()
    proj_out.beyond()
    vec_2 = vectors_on(1, vec_1, seq_peer[2])
    ups[0].across()
    ups[1].across()
    proj_q.beside()
    norm1_back(1)
    proj_k.beside()
    up_last.beyond()
    proj_v[0].beside()
    proj_q.beyond()
    proj_k.beyond()
    proj_v[1].beside()
    proj_v[0].beyond()
    vec_3 = vectors_on(2, vec_2, beside)
    finish_output(1)
    proj_v[1].beyond()
    vec_4 = vectors_on(3, vec_3, beyond)
    place = 0
    for group, (at, n) in zip(downs, spans): place = group.done(place, downg_h.at[:, at:at + n])
    for group, (at, n) in zip(ups + [up_last], spans): place = group.done(place, upg_h.at[:, at:at + n])
    place = proj_out.done(place, outg_h)
    place = proj_q.done(place, qkvg_h.at[0])
    place = proj_k.done(place, qkvg_h.at[1])
    for group, c in zip(proj_v, range(2)): place = group.done(place, qkvg_h.at[2, :, c * half_w:(c + 1) * half_w])
    vectors_done()
    copies.finish()


def one_kernel(args):
    (
        tokens, segment_ids, ln1_gain, ln1_bias, qkv_weight, qv_bias, out_weight, out_bias,
        ln2_gain, ln2_bias, up_weight, up_bias, down_weight, down_bias, out_cotangent,
    ) = args
    count, rows, width = tokens.shape
    heads_w, hidden = qkv_weight.shape[2], up_weight.shape[1]
    n_dp = axis_size("dp")
    block = width // (4 * n_dp)
    total = count * rows
    grads = hidden + hidden // 4 + 4 * heads_w
    line = lambda v: v.reshape(1, -1)
    low = lambda *shape: pltpu.VMEM(shape, LOW)
    full = lambda *shape: pltpu.VMEM(shape, F32)
    shape = jax.ShapeDtypeStruct
    vmem, anywhere = pl.BlockSpec(memory_space=pltpu.VMEM), pl.BlockSpec(memory_space=pl.ANY)
    return pl.pallas_call(
        functools.partial(layer_kernel, n_dp),
        in_specs=[anywhere, vmem, vmem, vmem, anywhere, vmem, anywhere, vmem, vmem, vmem, anywhere, vmem, anywhere, vmem, anywhere],
        out_specs=[anywhere] * 6 + [vmem],
        out_shape=[
            shape((total, width), LOW),
            shape((total, width), LOW),
            shape((block, hidden), F32),
            shape((block, hidden), F32),
            shape((block, heads_w), F32),
            shape((3, block, heads_w), F32),
            shape((16, width), F32),
        ],
        scratch_shapes=[
            low(total, width), low(total, width), low(3, width, heads_w), low(2 * heads_w, width),
            low(width, hidden), low(hidden, width), low(total, heads_w), low(2, 4, 2, rows, heads_w),
            full(2, heads_w, rows), low(total, width), full(total, width), low(2, rows, width),
            low(total, hidden), low(total, hidden),
            low(width, total), low(width, total), low(width, total), low(width, total),
            low(2, rows, heads_w), low(total, width), low(total, width),
            full(2, total, 2), full(2, heads_w // LANES, 8, rows),
            low(total, width), low(total, width), low(total, width), low(2, rows, 2 * heads_w),
            low(2, 2, rows, heads_w), low(2, 2, rows, heads_w), full(2, 2, heads_w // LANES, 8, rows),
            low(total, hidden), low(total, hidden),
            low(2, width // 4, total), low(2, width // 4, total), low(2, width // 4, total), low(2, width // 4, total),
            low(total, heads_w), low(total, 3 * heads_w), low(width // 4, grads), low(3, block, grads),
            low(block, 3 * hidden // 4), low(2, 3, block, 3 * hidden // 4),
            pltpu.VMEM((4, 8, rows), jnp.int32), full(4, rows, 8), full(6, 8, width), full(8, 2 * heads_w), full(8, hidden),
            full(2, 8, width), full(4, 16, width), full(4, 16, width),
            pltpu.SemaphoreType.DMA((N_COPIES,)), pltpu.SemaphoreType.DMA((N_COPIES,)), pltpu.SemaphoreType.DMA((N_LOCAL,)),
        ],
        compiler_params=pltpu.CompilerParams(
            collective_id=0, has_side_effects=True, vmem_limit_bytes=FAST_VMEM
        ),
    )(
        tokens.reshape(total, width), segment_ids, line(ln1_gain), line(ln1_bias), jnp.transpose(qkv_weight, (1, 0, 2)),
        qv_bias, out_weight, line(out_bias), line(ln2_gain), line(ln2_bias), up_weight, line(up_bias),
        down_weight, line(down_bias), out_cotangent.reshape(total, width),
    )


FAST_VMEM = 62 * 2**20


def fits(args):
    tokens, qkv_weight, up_weight = args[0], args[4], args[10]
    count, rows, width = tokens.shape
    heads_w, hidden = qkv_weight.shape[2], up_weight.shape[1]
    return (
        (axis_size("seq"), axis_size("head"), axis_size("dp")) == (4, 2, 4)
        and (count, rows) == (2, 256)
        and (width, heads_w, hidden) == (1024, 512, 2048)
    )


def split_kernel(parts, index_ref, vec_ref, *refs):
    big = (len(refs) - 1 - 8) // 3
    sources, targets, small = refs[:big], refs[big:2 * big], refs[2 * big:2 * big + 8]
    held, sem = refs[2 * big + 8:-1], refs[-1]
    moves = [pltpu.make_async_copy(a, b, sem.at[0, k]) for k, (a, b) in enumerate(zip(sources, held))]
    for move in moves:
        move.start()
    back = [pltpu.make_async_copy(a, b, sem.at[1, k]) for k, (a, b) in enumerate(zip(held, targets))]
    for move, out in zip(moves, back):
        move.wait()
        out.start()
    at = index_ref[0]
    width = vec_ref.shape[1]

    def piece(row, size):
        shift = lax.rem(width - lax.rem(at * size, width), width)
        return pltpu.roll(vec_ref[row:row + 1, :], shift, 1)[:, :size]

    size = width // parts
    for ref, row in zip(small[:6], (0, 1, 2, 3, 4, 5)):
        ref[...] = piece(row, size)
    half = vec_ref[6:7, :]
    shift = lax.rem(width - at * (size // 2), width)
    turned = pltpu.roll(half, shift, 1)
    small[6][0:1, :] = turned[:, :size // 2]
    small[6][1:2, :] = pltpu.roll(turned, width // 2, 1)[:, :size // 2]
    size = small[7].shape[1]
    low, high = piece(7, size), piece(8, size)
    small[7][...] = jnp.where(at * size < width, low, high)
    for out in back:
        out.wait()


def split(parts, big, vec):
    at = lax.axis_index("seq") * axis_size("dp") + lax.axis_index("dp")
    size = vec.shape[1] // parts
    shape = jax.ShapeDtypeStruct
    smalls = [shape((1, size), F32)] * 6 + [shape((2, size // 2), F32), shape((1, 2 * size), F32)]
    vmem, anywhere = pl.BlockSpec(memory_space=pltpu.VMEM), pl.BlockSpec(memory_space=pl.ANY)
    out = pl.pallas_call(
        functools.partial(split_kernel, parts),
        in_specs=[pl.BlockSpec(memory_space=pltpu.SMEM), vmem] + [anywhere] * len(big),
        out_specs=[anywhere] * len(big) + [vmem] * 8,
        out_shape=[shape(v.shape, v.dtype) for v in big] + smalls,
        scratch_shapes=[pltpu.VMEM(v.shape, v.dtype) for v in big] + [pltpu.SemaphoreType.DMA((2, len(big)))],
        compiler_params=pltpu.CompilerParams(vmem_limit_bytes=FAST_VMEM),
    )(at.astype(jnp.int32).reshape(1), vec, *big)
    return out[:len(big)], out[len(big):]


def fast(*args):
    tokens = args[0]
    *big, vec = one_kernel(args)
    big, small = split(axis_size("seq") * axis_size("dp"), big, vec)
    out, tokens_grad, down_grad, up_grad, out_grad, qkv_grad = big
    flat = [v.reshape(-1) for v in small]
    return (
        out.reshape(tokens.shape),
        tokens_grad.reshape(tokens.shape),
        flat[0],
        flat[1],
        jnp.transpose(qkv_grad, (1, 0, 2)),
        small[6],
        out_grad.T,
        flat[2],
        flat[3],
        flat[4],
        up_grad,
        flat[7],
        down_grad.T,
        flat[5],
    )


def shards(*args):
    return fast(*args) if fits(args) else general(*args)


def general(
    tokens,
    segment_ids,
    ln1_gain,
    ln1_bias,
    qkv_weight,
    qv_bias,
    out_weight,
    out_bias,
    ln2_gain,
    ln2_bias,
    up_weight,
    up_bias,
    down_weight,
    down_bias,
    out_cotangent,
):
    count, rows, features = tokens.shape
    local = qkv_weight.shape[2]
    hidden_local = up_weight.shape[1]
    n_seq, n_dp = axis_size("seq"), axis_size("dp")
    every = range(count)
    wq, wk, wv = (qkv_weight[:, c, :] for c in range(3))

    seg = gather_seq(segment_ids)
    seg_rows = [jnp.broadcast_to(segment_ids[s][None, :], (8, rows)) for s in every]
    seg_cols = [jnp.stack([part[s] for part in seg])[:, :, None] for s in every]

    half = out_weight.shape[0] // 2
    core = lax.axis_index("seq") & 1
    fetched = other_head(lax.dynamic_slice_in_dim(out_weight, core * half, half, 0))
    swapped = swap(fetched, "seq", 1)
    out_other = jnp.where(
        core == 0,
        jnp.concatenate([fetched, swapped], 0),
        jnp.concatenate([swapped, fetched], 0),
    )
    out_full = by_head(out_weight, out_other, 0)

    inputs, first, normed1, inverse1, queries, kvs = [], [], [], [], [], []
    for s in every:
        x = tokens[s].astype(F32)
        pre, normed, inverse = layer_norm(x, ln1_gain, ln1_bias)
        low = pre.astype(LOW)
        k = dot(low, wk).astype(LOW)
        v = (dot(low, wv) + qv_bias[1]).astype(LOW)
        kvs.append(gather_seq(jnp.stack([k, v])))
        queries.append((dot(low, wq) + qv_bias[0]).astype(LOW))
        inputs.append(x)
        first.append(low)
        normed1.append(normed)
        inverse1.append(inverse)

    attended = [attend(queries[s], seg_rows[s], seg_cols[s], kvs[s]) for s in every]

    outputs, second, act, g_hidden, g_middle, heads = [], [], [], [], [], []
    g_queries, g_kv = [], []
    vec = {
        name: 0.0 for name in ("out_b", "ln2_g", "ln2_b", "down_b", "up_b", "q_b", "v_b", "ln1_g", "ln1_b")
    }
    add = lambda name, value: vec.__setitem__(name, vec[name] + jnp.sum(value, axis=0))
    state = []
    for s in every:
        weights, attn_full, attn_low, inv_total = attended[s]
        mixed = by_head(attn_low, other_head(attn_low), 1)
        middle = inputs[s] + dot(mixed, out_full) + out_bias
        pre, normed2, inverse2 = layer_norm(middle, ln2_gain, ln2_bias)
        low = pre.astype(LOW)
        hidden = dot(low, up_weight) + up_bias
        activated, slope = gelu_pair(hidden)
        act_low = activated.astype(LOW)
        cot = out_cotangent[s]
        gh = (dot(cot, down_weight, NT) * slope).astype(LOW)
        g_second = head_sum(dot(gh, up_weight, NT))
        mlp = head_sum(dot(act_low, down_weight))
        outputs.append((middle + mlp + down_bias).astype(LOW))
        second.append(low)
        act.append(act_low)
        g_hidden.append(gh)
        heads.append(attn_low)
        state.append((normed2, inverse2, g_second))
        add("down_b", cot.astype(F32))
        add("up_b", gh.astype(F32))

    g_branch, g_first_parts = [], []
    for s in every:
        normed2, inverse2, g_second = state[s]
        weights, attn_full, attn_low, inv_total = attended[s]
        add("ln2_g", g_second * normed2)
        add("ln2_b", g_second)
        gm = out_cotangent[s].astype(F32) + norm_backward(g_second, normed2, inverse2, ln2_gain)
        gb = gm.astype(LOW)
        add("out_b", gb.astype(F32))
        g_attn = dot(gb, out_weight, NT).astype(LOW)
        dq, dkv = attend_back(queries[s], g_attn, attn_full, inv_total, weights, kvs[s])
        g_queries.append(dq)
        g_kv.append(scatter_seq(dkv).astype(LOW))
        g_middle.append(gm)
        g_branch.append(gb)

    join = lambda items: jnp.concatenate(items, axis=0)
    cot_all = out_cotangent.reshape(count * rows, features)
    cot_rel = relative_columns(cot_all)
    down_grad = weight_grad(cot_rel, join(act))
    up_grad = weight_grad(relative_columns(join(second)), join(g_hidden))
    out_grad = weight_grad(relative_columns(join(g_branch)), join(heads))

    tokens_grads = []
    for s in every:
        gq, gk, gv = g_queries[s], g_kv[s][0], g_kv[s][1]
        part = (dot(gq, wq, NT) + dot(gk, wk, NT) + dot(gv, wv, NT)).astype(LOW)
        add("q_b", gq.astype(F32))
        add("v_b", gv.astype(F32))
        add("ln1_g", part.astype(F32) * normed1[s])
        add("ln1_b", part.astype(F32))
        g_first = part.astype(F32) + other_head(part).astype(F32)
        tokens_grads.append(
            (g_middle[s] + norm_backward(g_first, normed1[s], inverse1[s], ln1_gain)).astype(LOW)
        )
    first_rel = relative_columns(join(first))
    g_proj = [join(g_queries), join([g[0] for g in g_kv]), join([g[1] for g in g_kv])]
    qkv_grad = jnp.stack([weight_grad(first_rel, g) for g in g_proj], axis=1)

    ln1 = jnp.stack([vec["ln1_g"], vec["ln1_b"]])
    ln1 = ln1 + other_head(ln1)
    wide = [ln1[0], ln1[1], vec["out_b"], vec["ln2_g"], vec["ln2_b"], vec["down_b"]]
    blocks = [v.reshape(n_seq, n_dp, -1) for v in wide + [vec["q_b"], vec["v_b"], vec["up_b"]]]
    sizes = [b.shape[2] for b in blocks]
    small = scatter_small(jnp.concatenate(blocks, axis=2))
    pieces, at = [], 0
    for size in sizes:
        pieces.append(small[at:at + size])
        at += size

    return (
        jnp.stack(outputs),
        jnp.stack(tokens_grads),
        pieces[0],
        pieces[1],
        qkv_grad,
        jnp.stack([pieces[6], pieces[7]]),
        out_grad.T,
        pieces[2],
        pieces[3],
        pieces[4],
        up_grad,
        pieces[8],
        down_grad.T,
        pieces[5],
    )


def solution(mesh):
    in_specs = (
        P("dp", "seq", None),
        P("dp", "seq"),
        P(),
        P(),
        P(None, None, "head"),
        P(None, "head"),
        P("head", None),
        P(),
        P(),
        P(),
        P(None, "head"),
        P("head"),
        P("head", None),
        P(),
        P("dp", "seq", None),
    )
    out_specs = (
        P("dp", "seq", None),
        P("dp", "seq", None),
        P(("seq", "dp")),
        P(("seq", "dp")),
        P(("seq", "dp"), None, "head"),
        P(None, ("head", "seq", "dp")),
        P("head", ("seq", "dp")),
        P(("seq", "dp")),
        P(("seq", "dp")),
        P(("seq", "dp")),
        P(("seq", "dp"), "head"),
        P(("head", "seq", "dp")),
        P("head", ("seq", "dp")),
        P(("seq", "dp")),
    )
    return jax.shard_map(shards, mesh=mesh, in_specs=in_specs, out_specs=out_specs, check_vma=False)
```
